32 devices in a mesh: field: 2 (over y), epoch: 4 (over z), sky: 4 (over x, core).
Axes of the slice: x: 2, y: 2, z: 4, core: 2. Of those that a mesh axis runs over, the one named last changes fastest.
Arguments:
- sky_scene: bfloat16 [4096, 2048], P(('field', 'epoch'), 'sky'), parts along dimension 0, may hold values from -6 to 6
- images: bfloat16 [16, 2048, 2048], P(('field', 'epoch'), None, 'sky'), parts along dimension 0, may hold values from -6 to 6
- psf_rows: bfloat16 [16, 25], P('field'), parts along dimension 0, may hold values from 0.0099487305 to 0.06982422
- psf_cols: bfloat16 [16, 25], P('field'), parts along dimension 0, may hold values from 0.0099487305 to 0.06982422
- offsets: int32 [16, 2], P('field'), parts along dimension 0, may hold values from -4 to 4, as said below
- epoch_weight: float32 [16], P('field'), parts along dimension 0, may hold values from 0.25 to 2
- column_mask: int32 [16, 2048], P('field', 'sky'), parts along dimension 0, may hold values 0 or 1
- coverage: int32 [16, 4, 4], P('field'), parts along dimension 0, may hold values from 0 to 1, as said below
Outputs:
- gradient: float32 [4096, 2048], P(('field', 'epoch'), 'sky'), parts along dimension 0
The draws below stay inside these ranges and needn't reach their ends.
There are 2 independent parts, one for each index of `field`. The reference program is written for one: setup_inputs(seed, part) draws one part's arguments, and reference() takes and returns one part's arrays. A program takes and returns all parts, laid end to end along the dimension named above; each array names one. Nothing has to cross between parts.
Inputs may be any that keep to these rules, and one draw needn't show every extreme that they name: `offsets`: column 0 shifts rows and column 1 shifts columns. `coverage`: the tiles that one epoch covers form a rectangle of whole tiles that spans all tile rows or all but one of them, and all tile columns or all but one of them.
All inputs are finite; a program needn't handle non-finite values. No bound on the sum of `column_mask` on one device may be relied on, other than what follows from the above.
Results may differ from the reference program's by a relative error of at most 0.0045.
Values may be sent and summed in bfloat16 or wider, within the bound.
No kernel may reach another device: no remote copies, remote signals or barrier semaphores. Data moves between devices by JAX's collectives and lax.ppermute only.
A program may use at most 64 MiB of HBM per device.

```python
import math
import jax
import jax.numpy as jnp
from jax import lax

H = 2048
W = 2048
TILE = 512
KW = 25
MAXOFF = 4
PR = 12
HALO = 16
EPOCHS = 8
TROWS = 4
TCOLS = 4


def draw_offsets(key, part):
    values = jax.random.randint(key, (EPOCHS, 2), -MAXOFF, MAXOFF + 1)
    values = values.at[0, 0].set(MAXOFF).at[0, 1].set(-MAXOFF)
    values = values.at[1, 0].set(-MAXOFF).at[1, 1].set(MAXOFF)
    return values.astype(jnp.int32)


def footprint(key_length, key_start, count):
    shortest = max(count - 1, 1)
    span = jax.random.randint(key_length, (EPOCHS,), shortest, count + 1)
    first = jax.random.randint(key_start, (EPOCHS,), 0, count - span + 1)
    index = jnp.arange(count)[None, :]
    return (index >= first[:, None]) & (index < (first + span)[:, None])


def draw_coverage(key, part):
    key_rowa, key_rowb, key_cola, key_colb = jax.random.split(key, 4)
    inside_rows = footprint(key_rowa, key_rowb, TROWS)
    inside_cols = footprint(key_cola, key_colb, TCOLS)
    return (inside_rows[:, :, None] & inside_cols[:, None, :]).astype(jnp.int32)


def with_ends(values, key, smallest, high):
    longest = values.shape.index(max(values.shape))
    spots = []
    for shift in (0, 1):
        where = [jax.random.randint(jax.random.fold_in(key, axis), (), 0, length) for axis, length in enumerate(values.shape)]
        where[longest] = (where[longest] + shift) % values.shape[longest]
        spots.append(tuple(where))
    return values.at[spots[0]].set(smallest).at[spots[1]].set(high)


def steps_of(rng, extent, pieces, low, largest):
    factor_of = 1.0
    for position, shards_of in pieces:
        steps = jax.random.uniform(jax.random.fold_in(jax.random.fold_in(rng, 6), position), (shards_of,), jnp.float32, low / len(pieces), largest / len(pieces))
        factor_of = factor_of * jnp.repeat(jnp.exp(steps), extent[position] // shards_of).reshape((-1,) + (1,) * (len(extent) - 1 - position))
    return factor_of


def gaussian(stream_key, shape, width, bound, cuts=(), dtype=jnp.bfloat16):
    values = width * jax.random.normal(stream_key, shape, jnp.float32)
    if cuts:
        values = values * steps_of(stream_key, shape, cuts, -0.22, 0.18)
    return jnp.clip(values, -bound, bound).astype(dtype)


def setup_inputs(seed: int = 0, part: int = 0) -> dict:
    key_of = jax.random.split(jax.random.key(seed), 9)
    part_keys = jax.random.split(jax.random.fold_in(key_of[8], part), 9)
    sky_scene = gaussian(part_keys[0], (H, W), 1.0, 6.0, ((0, 4), (1, 4)))
    images = gaussian(part_keys[1], (EPOCHS, H, W), 1.0, 6.0, ((0, 4), (2, 4)))
    psf_rows = jnp.clip(jax.random.uniform(part_keys[2], (EPOCHS, KW), jnp.float32, 0.0099487305, 0.06982422), 0.0099487305, 0.06982422).astype(jnp.bfloat16)
    psf_cols = jnp.clip(jax.random.uniform(part_keys[3], (EPOCHS, KW), jnp.float32, 0.0099487305, 0.06982422), 0.0099487305, 0.06982422).astype(jnp.bfloat16)
    offsets = draw_offsets(jax.random.fold_in(jax.random.fold_in(key_of[8], part), 71), part)
    epoch_weight = jnp.clip(jnp.exp(jax.random.uniform(part_keys[5], (EPOCHS,), jnp.float32, math.log(0.25), math.log(2.0))), 0.25, 2.0)
    column_mask = with_ends((jax.random.randint(part_keys[6], (EPOCHS, W), 0, 16) < 15).astype(jnp.int32), jax.random.fold_in(part_keys[6], 1), 0, 1)
    coverage = draw_coverage(jax.random.fold_in(jax.random.fold_in(key_of[8], part), 71), part)
    return dict(sky_scene=sky_scene, images=images, psf_rows=psf_rows, psf_cols=psf_cols, offsets=offsets, epoch_weight=epoch_weight, column_mask=column_mask, coverage=coverage)


def correlate(plane_in, kernel, shift_by, along):
    length_out = plane_in.shape[along]
    if along == 0:
        padded = jnp.pad(plane_in, ((HALO, HALO), (0, 0)))
        weights = kernel.reshape(1, 1, KW, 1)
    else:
        padded = jnp.pad(plane_in, ((0, 0), (HALO, HALO)))
        weights = kernel.reshape(1, 1, 1, KW)
    begin = (HALO - PR + shift_by).astype(jnp.int32)
    window = lax.dynamic_slice_in_dim(padded, begin, length_out + KW - 1, along)
    result = lax.conv_general_dilated(window[None, None], weights, (1, 1), "VALID", precision=lax.Precision.HIGHEST)
    return result[0, 0]


def rounded(values):
    narrow = values.astype(jnp.bfloat16)
    narrow = lax.optimization_barrier(narrow)
    return narrow.astype(jnp.float32)


def reference(sky_scene, images, psf_rows, psf_cols, offsets, epoch_weight, column_mask, coverage):
    rows_tile = jnp.arange(H) // TILE
    cols_tile = jnp.arange(W) // TILE
    scene_wide = sky_scene.astype(jnp.float32)

    def one_epoch(running, item):
        observed, kernel_row, kernel_col, band_shift, weight, mask_row, tile_cover = item
        kernel_row = kernel_row.astype(jnp.float32)
        kernel_col = kernel_col.astype(jnp.float32)
        lifted = rounded(correlate(scene_wide, kernel_row, band_shift[0], 0))
        modeled = correlate(lifted, kernel_col, band_shift[1], 1)
        tile_map = tile_cover[rows_tile][:, cols_tile].astype(jnp.float32)
        factor = (2.0 * weight * tile_map) * mask_row.astype(jnp.float32)[None, :]
        residual = rounded(factor * (modeled - observed.astype(jnp.float32)))
        pulled = rounded(correlate(residual, kernel_col[::-1], -band_shift[1], 1))
        grad_term = correlate(pulled, kernel_row[::-1], -band_shift[0], 0)
        return running + grad_term, None

    start = jnp.zeros((H, W), jnp.float32)
    running, unused = lax.scan(one_epoch, start, (images, psf_rows, psf_cols, offsets, epoch_weight, column_mask, coverage))
    return running
```

```python
import functools

import jax
import jax.numpy as jnp
from jax import lax
from jax.experimental import pallas as pl
from jax.experimental.pallas import tpu as pltpu
from jax.sharding import PartitionSpec as P

TILE = 512
HALO = 16
RIM = 2 * HALO
LANES = 128
SPAN = 256
STEP = SPAN - RIM
F32 = jnp.float32
BF16 = jnp.bfloat16
VMEM = pl.BlockSpec(memory_space=pltpu.VMEM)
SMEM = pl.BlockSpec(memory_space=pltpu.SMEM)
HBM = pl.BlockSpec(memory_space=pl.ANY)
PARAMS = pltpu.CompilerParams(vmem_limit_bytes=40 * 1024 * 1024)


def up_to(value, unit):
    return -(-value // unit) * unit


def dot(a, b, dims=((1,), (0,))):
    return lax.dot_general(a, b, (dims, ((), ())), preferred_element_type=F32)


def iota(shape, dim):
    return lax.broadcasted_iota(jnp.int32, shape, dim)


def selection(rows, cols, shift):
    return (iota((rows, cols), 1) == iota((rows, cols), 0) + shift).astype(BF16)


def toeplitz(taps, start, rows, width):
    line = jnp.concatenate([taps, jnp.zeros((1, width - LANES), F32)], axis=1)
    line = jnp.broadcast_to(line, (8, width))
    line = pltpu.roll(line, lax.rem(2 * width - start, width), 1)[0:1]
    line = jnp.broadcast_to(line, (rows, width))
    return pltpu.roll(line, 0, 1, stride=1, stride_axis=0).astype(BF16)


def stacked(taps, start):
    pair = toeplitz(taps, start, LANES, SPAN)
    return jnp.concatenate([pair[:, :LANES], pair[:, LANES:]], axis=0)


def row_of(values, index):
    return jnp.sum(jnp.where(iota(values.shape, 0) == index, values, 0), axis=0, keepdims=True)


def spans(length):
    return [(s, min(STEP, length - s)) for s in range(0, length, STEP)]


class Sizes:
    def __init__(self, images, sky_scene, psf_rows):
        self.local, self.height, self.width = images.shape
        self.rows = sky_scene.shape[0]
        self.epochs = psf_rows.shape[0]
        self.taps = psf_rows.shape[1]
        self.tile_rows = self.height // TILE
        self.wide = self.width + LANES
        self.line = up_to(self.height + RIM, LANES)
        self.chunk = up_to(self.rows, LANES)
        self.mask_rows = up_to(self.epochs, HALO)
        self.buffer_rows = HALO * (self.local + 1)
        self.blocks = self.height // self.rows


def cover_at(coverage_ref, epoch, row_tile, col_tile):
    last_row = coverage_ref.shape[1] - 1
    last_col = coverage_ref.shape[2] - 1
    inside = (row_tile >= 0) & (row_tile <= last_row) & (col_tile >= 0) & (col_tile <= last_col)
    value = coverage_ref[epoch, jnp.clip(row_tile, 0, last_row), jnp.clip(col_tile, 0, last_col)]
    return jnp.where(inside, value, 0).astype(F32)


def tile_of(position):
    return (position + TILE) // TILE - 1


def edges_kernel(sz, coverage_ref, images_ref, scene_ref, mask_ref, left_ref, right_ref, edge, sem):
    first = lax.axis_index("epoch") * sz.local
    column = lax.axis_index("sky") * sz.width
    places = (0, sz.width - LANES)
    copies = []
    for e in range(sz.local):
        for side in range(2):
            slot = 2 * e + side
            copies.append(
                pltpu.make_async_copy(
                    images_ref.at[e, :, pl.ds(places[side], LANES)],
                    edge.at[slot, pl.ds(HALO, sz.height), :],
                    sem.at[slot],
                )
            )
            copies[-1].start()
            edge[slot, 0:HALO] = jnp.zeros((HALO, LANES), BF16)
            tail = sz.line - sz.height - HALO
            edge[slot, sz.line - tail :] = jnp.zeros((tail, LANES), BF16)
    tail_at = HALO * sz.local
    for side, out in enumerate((left_ref, right_ref)):
        out[tail_at:, :] = jnp.zeros((HALO, sz.line), BF16)
        shift = 0 if side == 0 else LANES - RIM
        cells = dot(
            selection(RIM, LANES, shift),
            scene_ref[:, places[side] : places[side] + LANES],
            ((1,), (1,)),
        ).astype(BF16)
        for q in range(2):
            out[tail_at:, q * sz.chunk : q * sz.chunk + sz.rows] = cells[q * HALO : (q + 1) * HALO]
        good = mask_ref[:, places[side] : places[side] + LANES].astype(F32)
        if side == 1:
            good = pltpu.roll(good, HALO, 1)
        if sz.mask_rows > sz.epochs:
            good = jnp.concatenate(
                [good, jnp.zeros((sz.mask_rows - sz.epochs, LANES), F32)], axis=0
            )
        good = good.astype(BF16)
        for q in range(sz.mask_rows // HALO):
            at = 2 * sz.chunk + q * LANES
            out[tail_at:, at : at + LANES] = good[q * HALO : (q + 1) * HALO]
    for e in range(sz.local):
        for side, out in enumerate((left_ref, right_ref)):
            slot = 2 * e + side
            copies[slot].wait()
            for t in range(sz.tile_rows):
                here = slice(HALO + t * TILE, HALO + (t + 1) * TILE)
                factor = cover_at(coverage_ref, first + e, t, column // TILE)
                edge[slot, here] = edge[slot, here] * jnp.full((1, LANES), factor, F32).astype(BF16)
            good = row_of(mask_ref[:, places[side] : places[side] + LANES].astype(F32), first + e)
            shift = 0 if side == 0 else LANES - HALO
            pick = (iota((HALO, LANES), 1) == iota((HALO, LANES), 0) + shift) & (good > 0)
            out[HALO * e : HALO * (e + 1), :] = dot(
                pick.astype(F32).astype(BF16), edge[slot], ((1,), (1,))
            ).astype(BF16)


def edges(sz, coverage, images, scene, mask):
    shape = jax.ShapeDtypeStruct((sz.buffer_rows, sz.line), BF16)
    return pl.pallas_call(
        functools.partial(edges_kernel, sz),
        out_shape=(shape, shape),
        in_specs=[SMEM, HBM, VMEM, VMEM],
        out_specs=(VMEM, VMEM),
        scratch_shapes=[
            pltpu.VMEM((2 * sz.local, sz.line, LANES), BF16),
            pltpu.SemaphoreType.DMA((2 * sz.local,)),
        ],
        compiler_params=PARAMS,
        name="edges",
    )(coverage, images, scene, mask)


def widen_kernel(sz, scene_ref, mask_ref, before_ref, after_ref, wide_ref, good_ref):
    tail_at = HALO * sz.local

    def cells(ref):
        return jnp.concatenate(
            [ref[tail_at:, q * sz.chunk : q * sz.chunk + sz.rows] for q in range(2)], axis=0
        )

    def flags(ref):
        parts = []
        for q in range(sz.mask_rows // HALO):
            at = 2 * sz.chunk + q * LANES
            parts.append(ref[tail_at:, at : at + LANES])
        return jnp.concatenate(parts, axis=0) if len(parts) > 1 else parts[0]

    wide = dot(scene_ref[...], selection(sz.width, sz.wide, RIM))
    wide += dot(cells(before_ref), selection(RIM, sz.wide, 0), ((0,), (0,)))
    wide += dot(cells(after_ref), selection(RIM, sz.wide, sz.width + RIM), ((0,), (0,)))
    wide_ref[...] = wide.astype(BF16)
    own = mask_ref[...].astype(F32)
    if sz.mask_rows > sz.epochs:
        own = jnp.concatenate(
            [own, jnp.zeros((sz.mask_rows - sz.epochs, sz.width), F32)], axis=0
        )
    good = dot(own.astype(BF16), selection(sz.width, sz.wide, HALO))
    inner = iota((LANES, sz.wide), 0) < HALO
    zero = jnp.zeros((LANES, sz.wide), BF16)
    good += dot(flags(before_ref), jnp.where(inner, selection(LANES, sz.wide, 0), zero))
    good += dot(
        flags(after_ref), jnp.where(inner, selection(LANES, sz.wide, sz.width + HALO), zero)
    )
    good_ref[...] = good


def widen(sz, scene, mask, before, after):
    return pl.pallas_call(
        functools.partial(widen_kernel, sz),
        out_shape=(
            jax.ShapeDtypeStruct((sz.rows, sz.wide), BF16),
            jax.ShapeDtypeStruct((sz.mask_rows, sz.wide), F32),
        ),
        in_specs=[VMEM] * 4,
        out_specs=(VMEM, VMEM),
        compiler_params=PARAMS,
        name="widen",
    )(scene, mask, before, after)


def destination(slot, place):
    return (
        3 * (1 - place % 2),
        2 - place // 2,
        (2 * place + 1) % 5,
        place,
    )[slot]


def image_kernel(
    sz, slots, coverage_ref, offsets_ref, weight_ref,
    images_ref, mask_ref, taps_ref, before_ref, after_ref,
    out_ref, window, row_table, main_table, cross_table, rim_table, sem,
):
    step = pl.program_id(0)
    steps = pl.num_programs(0)
    place = lax.axis_index("epoch")
    first = place * sz.local
    column = lax.axis_index("sky") * sz.width

    def target(index):
        if slots is None:
            return index
        value = destination(slots[0], place)
        for i in range(1, len(slots)):
            value = jnp.where(index == i, destination(slots[i], place), value)
        return value

    def copies(index, slot):
        start = target(index) * sz.rows
        head = jnp.maximum(start - HALO, 0)
        foot = jnp.minimum(start + sz.rows, sz.height - HALO)
        made = []
        for e in range(sz.local):
            for n, (source, at, count) in enumerate(
                ((start, HALO, sz.rows), (head, 0, HALO), (foot, HALO + sz.rows, HALO))
            ):
                made.append(
                    pltpu.make_async_copy(
                        images_ref.at[e, pl.ds(pl.multiple_of(source, HALO), count), :],
                        window.at[slot, e, pl.ds(at, count), :],
                        sem.at[slot, e, n],
                    )
                )
        return made

    @pl.when(step == 0)
    def _():
        for copy in copies(0, 0):
            copy.start()
        for e in range(sz.local):
            epoch = first + e
            row_shift, col_shift = offsets_ref[epoch, 0], offsets_ref[epoch, 1]
            line = taps_ref[1, pl.ds(epoch, 1), :]
            row_table[e] = toeplitz(line, row_shift - 4, STEP, SPAN)
            line = taps_ref[2, pl.ds(epoch, 1), :]
            main = toeplitz(line, 12 - col_shift, SPAN, SPAN + LANES)[:, :SPAN]
            main_table[e] = main
            apart = (iota((SPAN, SPAN), 0) < LANES) != (iota((SPAN, SPAN), 1) < LANES)
            cross_table[e] = jnp.where(apart, main, jnp.zeros_like(main))
            enter = toeplitz(line, 28 - col_shift, HALO, SPAN)[:, :LANES]
            leave = toeplitz(line, SPAN + LANES - 116 - col_shift, HALO, SPAN + LANES)[:, :LANES]
            none = jnp.zeros((HALO, LANES), BF16)
            rim_table[e] = jnp.concatenate(
                [
                    jnp.concatenate([enter, none], axis=1),
                    jnp.concatenate([none, leave], axis=1),
                ],
                axis=0,
            )

    slot = step % 2

    @pl.when(step + 1 < steps)
    def _():
        for copy in copies(step + 1, (step + 1) % 2):
            copy.start()

    for copy in copies(step, slot):
        copy.wait()
    start = target(step) * sz.rows
    zones = (
        (0, HALO, tile_of(start - HALO)),
        (HALO, HALO + sz.rows, tile_of(start)),
        (HALO + sz.rows, RIM + sz.rows, tile_of(start + sz.rows)),
    )
    total = [None] * (sz.width // LANES)

    def add(at, value):
        for n in range(value.shape[1] // LANES):
            piece = value[:, n * LANES : (n + 1) * LANES]
            k = at + n
            total[k] = piece if total[k] is None else total[k] + piece

    for e in range(sz.local):
        epoch = first + e
        twice = -2.0 * weight_ref[epoch]
        good = row_of(mask_ref[...].astype(F32), epoch)
        for begin, end, tile in zones:
            factor = good * cover_at(coverage_ref, epoch, tile, column // TILE)
            window[slot, e, begin:end] = window[slot, e, begin:end] * factor.astype(BF16)
        parts = []
        for s, n in spans(sz.rows):
            parts.append(
                (dot(row_table[e, :n, : n + RIM], window[slot, e, s : s + n + RIM]) * twice).astype(
                    BF16
                )
            )
        rows_done = jnp.concatenate(parts, axis=0) if len(parts) > 1 else parts[0]
        for b in range(0, sz.width, SPAN):
            add(b // LANES, dot(rows_done[:, b : b + SPAN], main_table[e]))
        for b in range(LANES, sz.width - LANES, SPAN):
            add(b // LANES, dot(rows_done[:, b : b + SPAN], cross_table[e]))
        rims = []
        size = min(sz.rows, LANES)
        for s in range(0, sz.rows, size):
            at = start + s
            base = pl.multiple_of((at // LANES) * LANES, LANES)
            both = jnp.concatenate(
                [
                    ref[HALO * e : HALO * (e + 1), pl.ds(base, SPAN)]
                    for ref in (before_ref, after_ref)
                ],
                axis=0,
            )
            if size < LANES:
                both = pltpu.roll(both.astype(F32), lax.rem(SPAN - (at - base), SPAN), 1)
                both = both.astype(BF16)
            rims.append((dot(both, row_table[e, :size], ((1,), (1,))) * twice).astype(BF16))
        rim = jnp.concatenate(rims, axis=1) if len(rims) > 1 else rims[0]
        rim_part = dot(rim, rim_table[e], ((0,), (0,)))
        add(0, rim_part[:, :LANES])
        add(sz.width // LANES - 1, rim_part[:, LANES:])
    for k, piece in enumerate(total):
        out_ref[:, k * LANES : (k + 1) * LANES] = piece.astype(BF16)


def image_blocks(sz, slots, coverage, offsets, weight, images, mask, taps, before, after):
    count = sz.blocks if slots is None else len(slots)
    return pl.pallas_call(
        functools.partial(image_kernel, sz, slots),
        grid=(count,),
        out_shape=jax.ShapeDtypeStruct((count * sz.rows, sz.width), BF16),
        in_specs=[SMEM, SMEM, SMEM, HBM, VMEM, VMEM, VMEM, VMEM],
        out_specs=pl.BlockSpec((sz.rows, sz.width), lambda i: (i, 0)),
        scratch_shapes=[
            pltpu.VMEM((2, sz.local, sz.rows + RIM, sz.width), BF16),
            pltpu.VMEM((sz.local, STEP, SPAN), BF16),
            pltpu.VMEM((sz.local, SPAN, SPAN), BF16),
            pltpu.VMEM((sz.local, SPAN, SPAN), BF16),
            pltpu.VMEM((sz.local, RIM, SPAN), BF16),
            pltpu.SemaphoreType.DMA((2, sz.local, 3)),
        ],
        compiler_params=PARAMS,
        cost_estimate=pl.CostEstimate(
            flops=count * 1400000000, bytes_accessed=count * 2000000, transcendentals=0
        ),
        name="image_blocks",
    )(coverage, offsets, weight, images, mask, taps, before, after)


def model_kernel(
    sz, coverage_ref, offsets_ref, weight_ref,
    wide_ref, head_ref, foot_ref, good_ref, taps_ref,
    out_ref, scene, lifted, residual, pulled,
):
    epoch = pl.program_id(0)
    place = lax.axis_index("epoch")
    start = place * sz.rows
    column = lax.axis_index("sky") * sz.width

    @pl.when(epoch == 0)
    def _():
        scene[0:RIM] = head_ref[...]
        scene[RIM : RIM + sz.rows] = wide_ref[...]
        scene[RIM + sz.rows :] = foot_ref[...]

    row_shift, col_shift = offsets_ref[epoch, 0], offsets_ref[epoch, 1]
    row_in = toeplitz(taps_ref[0, pl.ds(epoch, 1), :], -4 - row_shift, STEP, SPAN)
    row_out = toeplitz(taps_ref[1, pl.ds(epoch, 1), :], row_shift - 4, STEP, SPAN)
    col_in = stacked(taps_ref[3, pl.ds(epoch, 1), :], 28 + col_shift)
    col_out = stacked(taps_ref[2, pl.ds(epoch, 1), :], 28 - col_shift)

    for s, n in spans(sz.rows + RIM):
        lifted[s : s + n] = dot(row_in[:n, : n + RIM], scene[s : s + n + RIM]).astype(BF16)

    twice = 2.0 * weight_ref[epoch]
    good = row_of(good_ref[...], epoch) * twice
    lane = iota((1, sz.wide), 1)
    factors = []
    for row_tile in (tile_of(start - HALO), tile_of(start), tile_of(start + sz.rows)):
        left, here, right = (
            cover_at(coverage_ref, epoch, row_tile, tile_of(c))
            for c in (column - HALO, column, column + sz.width)
        )
        factors.append(
            good * jnp.where(lane < HALO, left, jnp.where(lane < HALO + sz.width, here, right))
        )
    for b in range(0, sz.wide, LANES):
        if b < sz.width:
            modeled = dot(lifted[:, b : b + SPAN], col_in)
        else:
            modeled = dot(lifted[:, b : b + LANES], col_in[:LANES])
        low, mid, high = (f[:, b : b + LANES] for f in factors)
        edge = sz.rows + HALO
        residual[0:HALO, b : b + LANES] = (modeled[0:HALO] * low).astype(BF16)
        residual[HALO:edge, b : b + LANES] = (modeled[HALO:edge] * mid).astype(BF16)
        residual[edge:, b : b + LANES] = (modeled[edge:] * high).astype(BF16)
    for b in range(0, sz.width, LANES):
        pulled[:, b : b + LANES] = dot(residual[:, b : b + SPAN], col_out).astype(BF16)
    for s, n in spans(sz.rows):
        term = dot(row_out[:n, : n + RIM], pulled[s : s + n + RIM])

        @pl.when(epoch == 0)
        def _():
            out_ref[s : s + n] = term

        @pl.when(epoch > 0)
        def _():
            out_ref[s : s + n] += term


def model_term(sz, coverage, offsets, weight, wide, head, foot, good, taps):
    high = sz.rows + RIM
    return pl.pallas_call(
        functools.partial(model_kernel, sz),
        grid=(sz.epochs,),
        out_shape=jax.ShapeDtypeStruct((sz.rows, sz.width), F32),
        in_specs=[SMEM, SMEM, SMEM, VMEM, VMEM, VMEM, VMEM, VMEM],
        out_specs=VMEM,
        scratch_shapes=[
            pltpu.VMEM((sz.rows + 2 * RIM, sz.wide), BF16),
            pltpu.VMEM((high, sz.wide), BF16),
            pltpu.VMEM((high, sz.wide), BF16),
            pltpu.VMEM((high, sz.width), BF16),
        ],
        compiler_params=PARAMS,
        cost_estimate=pl.CostEstimate(
            flops=sz.epochs * 1300000000, bytes_accessed=2000000, transcendentals=0
        ),
        name="model_term",
    )(coverage, offsets, weight, wide, head, foot, good, taps)


def on_device(sky_scene, images, psf_rows, psf_cols, offsets, epoch_weight, column_mask, coverage):
    sz = Sizes(images, sky_scene, psf_rows)
    peers = lax.axis_size("sky")
    depth = lax.axis_size("epoch")
    rightward = [(i, i + 1) for i in range(peers - 1)]
    leftward = [(i + 1, i) for i in range(peers - 1)]
    downward = [(i, i + 1) for i in range(depth - 1)]
    upward = [(i + 1, i) for i in range(depth - 1)]
    taps = jnp.stack([psf_rows, psf_rows[:, ::-1], psf_cols, psf_cols[:, ::-1]]).astype(F32)
    taps = jnp.pad(taps, ((0, 0), (0, 0), (0, LANES - sz.taps)))

    to_left, to_right = edges(sz, coverage, images, sky_scene, column_mask)
    before = lax.ppermute(to_right, "sky", rightward)
    after = lax.ppermute(to_left, "sky", leftward)
    wide, good = widen(sz, sky_scene, column_mask, before, after)
    head = lax.ppermute(wide[-RIM:], "epoch", downward)
    foot = lax.ppermute(wide[:RIM], "epoch", upward)

    def blocks(slots):
        return image_blocks(
            sz, slots, coverage, offsets, epoch_weight, images, column_mask, taps, before, after
        )

    if depth == 4:
        place = lax.axis_index("epoch")
        outer = (place == 0) | (place == 3)
        one = blocks((0,))
        got_one = lax.ppermute(one, "epoch", [(0, 1), (1, 0), (2, 3), (3, 2)])
        rest = blocks((1, 2, 3))
        two, three, own = (rest[i * sz.rows : (i + 1) * sz.rows] for i in range(3))
        got_two = lax.ppermute(two, "epoch", [(1, 2), (2, 1)])
        got_three = lax.ppermute(three, "epoch", [(0, 1), (3, 2)])
        merged = jnp.where(outer, two, three + got_one)
        got_four = lax.ppermute(merged, "epoch", [(0, 2), (3, 1), (1, 3), (2, 0)])
        model = model_term(sz, coverage, offsets, epoch_weight, wide, head, foot, good, taps)
        last = jnp.where(outer, got_one.astype(F32), got_two.astype(F32) + got_three.astype(F32))
        return model + own.astype(F32) + got_four.astype(F32) + last
    model = model_term(sz, coverage, offsets, epoch_weight, wide, head, foot, good, taps)
    summed = lax.psum_scatter(
        blocks(None).astype(F32), "epoch", scatter_dimension=0, tiled=True
    )
    return model + summed


def solution(mesh):
    return jax.shard_map(
        on_device,
        mesh=mesh,
        in_specs=(
            P(("field", "epoch"), "sky"),
            P(("field", "epoch"), None, "sky"),
            P("field", None),
            P("field", None),
            P("field", None),
            P("field"),
            P("field", "sky"),
            P("field", None, None),
        ),
        out_specs=P(("field", "epoch"), "sky"),
        check_vma=False,
    )
```

```python
import functools

import jax
import jax.numpy as jnp
from jax import lax
from jax.experimental import pallas as pl
from jax.experimental.pallas import tpu as pltpu
from jax.sharding import PartitionSpec as P

TILE = 512
HALO = 16
RIM = 2 * HALO
LANES = 128
SPAN = 256
STEP = SPAN - RIM
F32 = jnp.float32
BF16 = jnp.bfloat16
VMEM = pl.BlockSpec(memory_space=pltpu.VMEM)
SMEM = pl.BlockSpec(memory_space=pltpu.SMEM)
HBM = pl.BlockSpec(memory_space=pltpu.HBM)
PARAMS = pltpu.CompilerParams(vmem_limit_bytes=40 * 1024 * 1024)
SHORT = pl.CostEstimate(flops=1000, bytes_accessed=1000, transcendentals=0)
WHOLE = pltpu.CompilerParams(vmem_limit_bytes=59 * 1024 * 1024)


def up_to(value, unit):
    return -(-value // unit) * unit


def dot(a, b, dims=((1,), (0,))):
    return lax.dot_general(a, b, (dims, ((), ())), preferred_element_type=F32)


def iota(shape, dim):
    return lax.broadcasted_iota(jnp.int32, shape, dim)


def selection(rows, cols, shift):
    return (iota((rows, cols), 1) == iota((rows, cols), 0) + shift).astype(BF16)


def toeplitz(taps, start, rows, width):
    line = jnp.concatenate([taps, jnp.zeros((1, width - LANES), F32)], axis=1)
    line = jnp.broadcast_to(line, (8, width))
    line = pltpu.roll(line, lax.rem(2 * width - start, width), 1)[0:1]
    line = jnp.broadcast_to(line, (rows, width))
    return pltpu.roll(line, 0, 1, stride=1, stride_axis=0).astype(BF16)


def stacked(taps, start):
    pair = toeplitz(taps, start, LANES, SPAN)
    return jnp.concatenate([pair[:, :LANES], pair[:, LANES:]], axis=0)


def row_of(values, index):
    return jnp.sum(jnp.where(iota(values.shape, 0) == index, values, 0), axis=0, keepdims=True)


def load_taps(psf_ref, lines, epochs, taps):
    lines[0] = jnp.zeros(lines.shape[1:], F32)
    lines[0, :epochs, :taps] = psf_ref[...].astype(F32)
    mirror = iota((LANES, LANES), 0) + iota((LANES, LANES), 1) == taps - 1
    lines[1] = dot(lines[0].astype(BF16), mirror.astype(F32).astype(BF16))


def spans(length):
    return [(s, min(STEP, length - s)) for s in range(0, length, STEP)]


class Sizes:
    def __init__(self, images, sky_scene, psf_rows):
        self.local, self.height, self.width = images.shape
        self.rows = sky_scene.shape[0]
        self.epochs = psf_rows.shape[0]
        self.taps = psf_rows.shape[1]
        self.tile_rows = self.height // TILE
        self.wide = self.width + LANES
        self.line = up_to(self.height + RIM, LANES)
        self.chunk = up_to(self.rows, LANES)
        self.mask_rows = up_to(self.epochs, HALO)
        self.buffer_rows = HALO * (self.local + 1)
        self.blocks = self.height // self.rows
        self.tap_rows = self.mask_rows


def cover_at(coverage_ref, epoch, row_tile, col_tile):
    last_row = coverage_ref.shape[0] - 1
    last_col = coverage_ref.shape[1] - 1
    inside = (row_tile >= 0) & (row_tile <= last_row) & (col_tile >= 0) & (col_tile <= last_col)
    value = coverage_ref[jnp.clip(row_tile, 0, last_row), jnp.clip(col_tile, 0, last_col), epoch]
    return jnp.where(inside, value, 0).astype(F32)


def tile_of(position):
    return (position + TILE) // TILE - 1


def edges_kernel(sz, images_ref, scene_ref, mask_ref, first_ref, second_ref, *scratch):
    edge, sides, flags, sem, side_sem, flag_sem = scratch
    epoch = lax.axis_index("epoch") * sz.local
    even = lax.axis_index("sky") % 2 == 0
    places = (0, sz.width - LANES)
    flag_copy = pltpu.make_async_copy(mask_ref, flags, flag_sem)
    flag_copy.start()
    copies = []
    for e in range(sz.local):
        for side in range(2):
            slot = 2 * e + side
            copies.append(
                pltpu.make_async_copy(
                    images_ref.at[e, :, pl.ds(places[side], LANES)],
                    edge.at[slot, pl.ds(HALO, sz.height), :],
                    sem.at[slot],
                )
            )
            copies[-1].start()
    side_copies = [
        pltpu.make_async_copy(
            scene_ref.at[:, pl.ds(places[side], LANES)], sides.at[side], side_sem.at[side]
        )
        for side in range(2)
    ]
    for copy in side_copies:
        copy.start()
    tail = sz.line - sz.height - HALO
    for slot in range(2 * sz.local):
        edge[slot, 0:HALO] = jnp.zeros((HALO, LANES), BF16)
        edge[slot, sz.line - tail :] = jnp.zeros((tail, LANES), BF16)
    tail_at = HALO * sz.local

    def put(left, right, rows, cols):
        first_ref[rows, cols] = jnp.where(even, right, left).astype(BF16)
        second_ref[rows, cols] = jnp.where(even, left, right).astype(BF16)

    flag_copy.wait()
    goods = []
    for side in range(2):
        good = flags[:, places[side] : places[side] + LANES].astype(F32)
        if side == 1:
            good = pltpu.roll(good, HALO, 1)
        if sz.mask_rows > sz.epochs:
            good = jnp.concatenate(
                [good, jnp.zeros((sz.mask_rows - sz.epochs, LANES), F32)], axis=0
            )
        goods.append(good)
    below = slice(tail_at, tail_at + HALO)
    for q in range(sz.mask_rows // HALO):
        at = 2 * sz.chunk + q * LANES
        rows = slice(q * HALO, (q + 1) * HALO)
        put(goods[0][rows], goods[1][rows], below, slice(at, at + LANES))
    rest = 2 * sz.chunk + (sz.mask_rows // HALO) * LANES
    none = jnp.zeros((HALO, sz.line - rest), F32)
    put(none, none, below, slice(rest, sz.line))
    cells = []
    for side in range(2):
        side_copies[side].wait()
        shift = 0 if side == 0 else LANES - RIM
        cells.append(dot(selection(RIM, LANES, shift), sides[side], ((1,), (1,))))
    for q in range(2):
        rows = slice(q * HALO, (q + 1) * HALO)
        put(cells[0][rows], cells[1][rows], below, slice(q * sz.chunk, q * sz.chunk + sz.rows))
        if sz.chunk > sz.rows:
            none = jnp.zeros((HALO, sz.chunk - sz.rows), F32)
            put(none, none, below, slice(q * sz.chunk + sz.rows, (q + 1) * sz.chunk))
    for e in range(sz.local):
        lines = []
        for side in range(2):
            slot = 2 * e + side
            copies[slot].wait()
            good = row_of(flags[:, places[side] : places[side] + LANES].astype(F32), epoch + e)
            shift = 0 if side == 0 else LANES - HALO
            pick = (iota((HALO, LANES), 1) == iota((HALO, LANES), 0) + shift) & (good > 0)
            lines.append(dot(pick.astype(F32).astype(BF16), edge[slot], ((1,), (1,))))
        put(lines[0], lines[1], slice(HALO * e, HALO * (e + 1)), slice(0, sz.line))


def edges(sz, images, scene, mask):
    shape = jax.ShapeDtypeStruct((sz.buffer_rows, sz.line), BF16)
    return pl.pallas_call(
        functools.partial(edges_kernel, sz),
        out_shape=(shape, shape),
        in_specs=[HBM, HBM, HBM],
        out_specs=(VMEM, VMEM),
        scratch_shapes=[
            pltpu.VMEM((2 * sz.local, sz.line, LANES), BF16),
            pltpu.VMEM((2, sz.rows, LANES), BF16),
            pltpu.VMEM((sz.epochs, sz.width), jnp.int32),
            pltpu.SemaphoreType.DMA((2 * sz.local,)),
            pltpu.SemaphoreType.DMA((2,)),
            pltpu.SemaphoreType.DMA,
        ],
        compiler_params=WHOLE,
        cost_estimate=SHORT,
        name="edges",
    )(images, scene, mask)


def sides_of(first, second):
    even = lax.axis_index("sky") % 2 == 0
    return jnp.where(even, second, first), jnp.where(even, first, second)


def widen_kernel(sz, scene_ref, mask_ref, first_ref, second_ref, *outs):
    wide_ref, good_ref = outs
    below = slice(HALO * sz.local, HALO * (sz.local + 1))

    def cells(value):
        return jnp.concatenate(
            [value[:, q * sz.chunk : q * sz.chunk + sz.rows] for q in range(2)], axis=0
        )

    def flags(value):
        parts = []
        for q in range(sz.mask_rows // HALO):
            at = 2 * sz.chunk + q * LANES
            parts.append(value[:, at : at + LANES])
        return jnp.concatenate(parts, axis=0) if len(parts) > 1 else parts[0]

    before, after = sides_of(first_ref[below], second_ref[below])
    wide = dot(scene_ref[...], selection(sz.width, sz.wide, RIM))
    wide += dot(cells(before), selection(RIM, sz.wide, 0), ((0,), (0,)))
    wide += dot(cells(after), selection(RIM, sz.wide, sz.width + RIM), ((0,), (0,)))
    wide_ref[...] = wide.astype(BF16)
    own = mask_ref[...].astype(F32)
    if sz.mask_rows > sz.epochs:
        own = jnp.concatenate(
            [own, jnp.zeros((sz.mask_rows - sz.epochs, sz.width), F32)], axis=0
        )
    good = dot(own.astype(BF16), selection(sz.width, sz.wide, HALO))
    inner = iota((LANES, sz.wide), 0) < HALO
    zero = jnp.zeros((LANES, sz.wide), BF16)
    good += dot(flags(before), jnp.where(inner, selection(LANES, sz.wide, 0), zero))
    good += dot(flags(after), jnp.where(inner, selection(LANES, sz.wide, sz.width + HALO), zero))
    good_ref[...] = good


def destination(slot, place):
    return (
        3 * (1 - place % 2),
        2 - place // 2,
        (2 * place + 1) % 5,
        place,
    )[slot]


def rim_tables(sz, row_line, col_line, row_shift, col_shift):
    row_table = toeplitz(row_line, row_shift - 4, min(sz.rows, LANES), SPAN)
    enter = toeplitz(col_line, 28 - col_shift, HALO, SPAN)[:, :LANES]
    leave = toeplitz(col_line, SPAN + LANES - 116 - col_shift, HALO, SPAN + LANES)[:, :LANES]
    none = jnp.zeros((HALO, LANES), BF16)
    col_table = jnp.concatenate(
        [jnp.concatenate([enter, none], axis=1), jnp.concatenate([none, leave], axis=1)], axis=0
    )
    return row_table, col_table


def rim_line(sz, start, epoch, e, column, coverage_ref, twice, first_ref, second_ref, row_table):
    size = min(sz.rows, LANES)
    covers = []
    for tile in (tile_of(start - HALO), tile_of(start), tile_of(start + sz.rows)):
        covers.append(
            [
                cover_at(coverage_ref, epoch, tile, tile_of(c))
                for c in (column - HALO, column + sz.width)
            ]
        )
    side = iota((RIM, SPAN), 0) < HALO
    factors = [jnp.where(side, left, right) for left, right in covers]
    pieces = []
    for s in range(0, sz.rows, size):
        at = start + s
        base = pl.multiple_of((at // LANES) * LANES, LANES)
        rows = slice(HALO * e, HALO * (e + 1))
        both = jnp.concatenate(
            sides_of(first_ref[rows, pl.ds(base, SPAN)], second_ref[rows, pl.ds(base, SPAN)]),
            axis=0,
        ).astype(F32)
        if size < LANES:
            both = pltpu.roll(both, lax.rem(SPAN - (at - base), SPAN), 1)
        lane = iota((RIM, SPAN), 1) + (s - HALO)
        both = both * jnp.where(
            lane < 0, factors[0], jnp.where(lane < sz.rows, factors[1], factors[2])
        )
        pieces.append(dot(both.astype(BF16), row_table, ((1,), (1,))))
    rim = jnp.concatenate(pieces, axis=1) if len(pieces) > 1 else pieces[0]
    return (rim * twice).astype(BF16)


def finish_kernel(
    sz, slots, coverage_ref, offsets_ref, weight_ref, scene_ref, mask_ref, first_ref, second_ref,
    psf_rows_ref, psf_cols_ref, *more,
):
    count = len(slots)
    blocks, outs = more[:count], more[count : 2 * count]
    wide_ref, good_ref, row_lines, col_lines = more[2 * count :]
    place = lax.axis_index("epoch")
    column = lax.axis_index("sky") * sz.width
    load_taps(psf_rows_ref, row_lines, sz.epochs, sz.taps)
    load_taps(psf_cols_ref, col_lines, sz.epochs, sz.taps)
    totals = [None] * count
    for e in range(sz.local):
        epoch = place * sz.local + e
        row_table, col_table = rim_tables(
            sz, row_of(row_lines[1], epoch), row_of(col_lines[0], epoch),
            offsets_ref[0, epoch], offsets_ref[1, epoch],
        )
        for i, slot in enumerate(slots):
            line = rim_line(
                sz, destination(slot, place) * sz.rows, epoch, e, column, coverage_ref,
                -2.0 * weight_ref[epoch], first_ref, second_ref, row_table,
            )
            part = dot(line, col_table, ((0,), (0,)))
            totals[i] = part if e == 0 else totals[i] + part
    low, mid = slice(0, LANES), slice(LANES, sz.width - LANES)
    high = slice(sz.width - LANES, sz.width)
    own = slice(0, sz.rows)
    for block, out, total in zip(blocks, outs, totals):
        out[own, low] = (block[:, low].astype(F32) + total[:, :LANES]).astype(BF16)
        out[own, mid] = block[:, mid]
        out[own, high] = (block[:, high].astype(F32) + total[:, LANES:]).astype(BF16)
    widen_kernel(sz, scene_ref, mask_ref, first_ref, second_ref, wide_ref, good_ref)
    if count == 0:
        return
    top, bottom = wide_ref[:RIM], wide_ref[sz.rows - RIM :]
    for out, last in zip(outs, (place % 2 == 0, place < 2)):
        rim = jnp.where(last, bottom, top)
        out[sz.rows : sz.rows + RIM] = rim[:, : sz.width]
        left = slice(sz.rows + RIM, sz.rows + RIM + HALO)
        out[left, :LANES] = rim[:HALO, sz.width :]
        out[left, LANES:SPAN] = rim[HALO:, sz.width :]
        out[left, SPAN:] = jnp.zeros((HALO, sz.width - SPAN), BF16)


def unpack_rim(sz, ref):
    left = slice(sz.rows + RIM, sz.rows + RIM + HALO)
    rest = jnp.concatenate([ref[left, :LANES], ref[left, LANES:SPAN]], axis=0)
    return jnp.concatenate([ref[sz.rows : sz.rows + RIM], rest], axis=1)


def finish(
    sz, slots, coverage, offsets, weight, scene, mask, first, second, psf_rows, psf_cols, *blocks
):
    pack = jax.ShapeDtypeStruct((sz.rows + RIM + HALO, sz.width), BF16)
    shapes = [pack] * len(slots) + [
        jax.ShapeDtypeStruct((sz.rows, sz.wide), BF16),
        jax.ShapeDtypeStruct((sz.mask_rows, sz.wide), F32),
    ]
    return pl.pallas_call(
        functools.partial(finish_kernel, sz, slots),
        out_shape=tuple(shapes),
        in_specs=[SMEM] * 3 + [VMEM] * (6 + len(slots)),
        out_specs=tuple([VMEM] * len(shapes)),
        scratch_shapes=[pltpu.VMEM((2, sz.tap_rows, LANES), F32)] * 2,
        compiler_params=PARAMS,
        cost_estimate=SHORT,
        name="finish",
    )(coverage, offsets, weight, scene, mask, first, second, psf_rows, psf_cols, *blocks)


def image_kernel(
    sz, slots, rims, coverage_ref, offsets_ref, weight_ref,
    images_ref, mask_ref, psf_rows_ref, psf_cols_ref, *more,
):
    count = 1 if slots is None else len(slots)
    ends, more = more[:rims], more[rims:]
    outs = more[:count]
    window, row_lines, col_lines, row_table, main_table, cross_table, sem = more[count:]
    place = lax.axis_index("epoch")
    first = place * sz.local
    column = lax.axis_index("sky") * sz.width
    if slots is None:
        targets = [pl.program_id(0)]
    else:
        targets = [destination(slot, place) for slot in slots]

    copies = []
    for i, target in enumerate(targets):
        start = target * sz.rows
        head = jnp.maximum(start - HALO, 0)
        foot = jnp.minimum(start + sz.rows, sz.height - HALO)
        for e in range(sz.local):
            for n, (source, at, length) in enumerate(
                ((start, HALO, sz.rows), (head, 0, HALO), (foot, HALO + sz.rows, HALO))
            ):
                copies.append(
                    pltpu.make_async_copy(
                        images_ref.at[e, pl.ds(pl.multiple_of(source, HALO), length), :],
                        window.at[i, e, pl.ds(at, length), :],
                        sem.at[i, e, n],
                    )
                )
    for copy in copies:
        copy.start()
    load_taps(psf_rows_ref, row_lines, sz.epochs, sz.taps)
    load_taps(psf_cols_ref, col_lines, sz.epochs, sz.taps)
    for e in range(sz.local):
        epoch = first + e
        row_shift, col_shift = offsets_ref[0, epoch], offsets_ref[1, epoch]
        row_table[e] = toeplitz(row_of(row_lines[1], epoch), row_shift - 4, STEP, SPAN)
        line = row_of(col_lines[0], epoch)
        main = toeplitz(line, 12 - col_shift, SPAN, SPAN + LANES)[:, :SPAN]
        main_table[e] = main
        apart = (iota((SPAN, SPAN), 0) < LANES) != (iota((SPAN, SPAN), 1) < LANES)
        cross_table[e] = jnp.where(apart, main, jnp.zeros_like(main))
    rim_parts = []
    for e in range(sz.local if rims else 0):
        epoch = first + e
        tables = rim_tables(
            sz, row_of(row_lines[1], epoch), row_of(col_lines[0], epoch),
            offsets_ref[0, epoch], offsets_ref[1, epoch],
        )
        for i, target in enumerate(targets):
            line = rim_line(
                sz, target * sz.rows, epoch, e, column, coverage_ref,
                -2.0 * weight_ref[epoch], *ends, tables[0],
            )
            part = dot(line, tables[1], ((0,), (0,)))
            if e == 0:
                rim_parts.append(part)
            else:
                rim_parts[i] += part
    for i, target in enumerate(targets):
        for copy in copies[3 * sz.local * i : 3 * sz.local * (i + 1)]:
            copy.wait()
        start = target * sz.rows
        zones = (
            (0, HALO, tile_of(start - HALO)),
            (HALO, HALO + sz.rows, tile_of(start)),
            (HALO + sz.rows, RIM + sz.rows, tile_of(start + sz.rows)),
        )
        total = [None] * (sz.width // LANES)

        def add(at, value):
            for n in range(value.shape[1] // LANES):
                piece = value[:, n * LANES : (n + 1) * LANES]
                k = at + n
                total[k] = piece if total[k] is None else total[k] + piece

        for e in range(sz.local):
            epoch = first + e
            twice = -2.0 * weight_ref[epoch]
            good = row_of(mask_ref[...].astype(F32), epoch)
            for begin, end, tile in zones:
                factor = good * cover_at(coverage_ref, epoch, tile, column // TILE)
                window[i, e, begin:end] = window[i, e, begin:end] * factor.astype(BF16)
            parts = []
            for s, n in spans(sz.rows):
                part = dot(row_table[e, :n, : n + RIM], window[i, e, s : s + n + RIM])
                parts.append((part * twice).astype(BF16))
            rows_done = jnp.concatenate(parts, axis=0) if len(parts) > 1 else parts[0]
            for b in range(0, sz.width, SPAN):
                add(b // LANES, dot(rows_done[:, b : b + SPAN], main_table[e]))
            for b in range(LANES, sz.width - LANES, SPAN):
                add(b // LANES, dot(rows_done[:, b : b + SPAN], cross_table[e]))
        if rims:
            add(0, rim_parts[i][:, :LANES])
            add(sz.width // LANES - 1, rim_parts[i][:, LANES:])
        for k, piece in enumerate(total):
            outs[i][:, k * LANES : (k + 1) * LANES] = piece.astype(BF16)


def image_blocks(sz, slots, coverage, offsets, weight, images, mask, psf_rows, psf_cols, *ends):
    if slots is None:
        count = 1
        grid = dict(
            grid=(sz.blocks,),
            out_shape=jax.ShapeDtypeStruct((sz.blocks * sz.rows, sz.width), BF16),
            out_specs=pl.BlockSpec((sz.rows, sz.width), lambda i: (i, 0)),
        )
    else:
        count = len(slots)
        grid = dict(
            out_shape=tuple([jax.ShapeDtypeStruct((sz.rows, sz.width), BF16)] * count),
            out_specs=tuple([VMEM] * count),
        )
    return pl.pallas_call(
        functools.partial(image_kernel, sz, slots, len(ends)),
        in_specs=[SMEM, SMEM, SMEM, HBM] + [VMEM] * (3 + len(ends)),
        scratch_shapes=[
            pltpu.VMEM((count, sz.local, sz.rows + RIM, sz.width), BF16),
            pltpu.VMEM((2, sz.tap_rows, LANES), F32),
            pltpu.VMEM((2, sz.tap_rows, LANES), F32),
            pltpu.VMEM((sz.local, STEP, SPAN), BF16),
            pltpu.VMEM((sz.local, SPAN, SPAN), BF16),
            pltpu.VMEM((sz.local, SPAN, SPAN), BF16),
            pltpu.SemaphoreType.DMA((count, sz.local, 3)),
        ],
        compiler_params=PARAMS,
        cost_estimate=SHORT,
        name="image_blocks",
        **grid,
    )(coverage, offsets, weight, images, mask, psf_rows, psf_cols, *ends)


def model_kernel(
    sz, coverage_ref, offsets_ref, weight_ref,
    wide_ref, good_ref, psf_rows_ref, psf_cols_ref, *more,
):
    *extra, out_ref, scene, lifted, residual, pulled, row_lines, col_lines = more
    epoch = pl.program_id(0)
    place = lax.axis_index("epoch")
    start = place * sz.rows
    column = lax.axis_index("sky") * sz.width

    @pl.when(epoch == 0)
    def _():
        load_taps(psf_rows_ref, row_lines, sz.epochs, sz.taps)
        load_taps(psf_cols_ref, col_lines, sz.epochs, sz.taps)
        scene[RIM : RIM + sz.rows] = wide_ref[...]
        if sz.blocks != 4:
            head_ref, foot_ref, base_ref = extra
            scene[0:RIM] = head_ref[...]
            scene[RIM + sz.rows :] = foot_ref[...]
            out_ref[...] = base_ref[...]
        else:
            own_ref, one_ref, two_ref = extra
            near, far = unpack_rim(sz, one_ref), unpack_rim(sz, two_ref)
            none = jnp.zeros_like(near)
            outer = (place == 0) | (place == 3)
            odd = place % 2 == 1
            scene[0:RIM] = jnp.where(odd, near, jnp.where(outer, none, far))
            scene[RIM + sz.rows :] = jnp.where(odd, jnp.where(outer, none, far), near)
            for b in range(0, sz.width, LANES):
                cols = slice(b, b + LANES)
                one = one_ref[: sz.rows, cols].astype(F32)
                two = two_ref[: sz.rows, cols].astype(F32)
                out_ref[:, cols] = own_ref[:, cols].astype(F32) + jnp.where(outer, one, two)

    row_shift, col_shift = offsets_ref[0, epoch], offsets_ref[1, epoch]
    row_in = toeplitz(row_of(row_lines[0], epoch), -4 - row_shift, STEP, SPAN)
    row_out = toeplitz(row_of(row_lines[1], epoch), row_shift - 4, STEP, SPAN)
    col_in = stacked(row_of(col_lines[1], epoch), 28 + col_shift)
    col_out = stacked(row_of(col_lines[0], epoch), 28 - col_shift)

    for s, n in spans(sz.rows + RIM):
        lifted[s : s + n] = dot(row_in[:n, : n + RIM], scene[s : s + n + RIM]).astype(BF16)

    twice = 2.0 * weight_ref[epoch]
    good = row_of(good_ref[...], epoch) * twice
    lane = iota((1, sz.wide), 1)
    factors = []
    for row_tile in (tile_of(start - HALO), tile_of(start), tile_of(start + sz.rows)):
        left, here, right = (
            cover_at(coverage_ref, epoch, row_tile, tile_of(c))
            for c in (column - HALO, column, column + sz.width)
        )
        factors.append(
            good * jnp.where(lane < HALO, left, jnp.where(lane < HALO + sz.width, here, right))
        )
    for b in range(0, sz.wide, LANES):
        if b < sz.width:
            modeled = dot(lifted[:, b : b + SPAN], col_in)
        else:
            modeled = dot(lifted[:, b : b + LANES], col_in[:LANES])
        low, mid, high = (f[:, b : b + LANES] for f in factors)
        edge = sz.rows + HALO
        residual[0:HALO, b : b + LANES] = (modeled[0:HALO] * low).astype(BF16)
        residual[HALO:edge, b : b + LANES] = (modeled[HALO:edge] * mid).astype(BF16)
        residual[edge:, b : b + LANES] = (modeled[edge:] * high).astype(BF16)
    for b in range(0, sz.width, LANES):
        pulled[:, b : b + LANES] = dot(residual[:, b : b + SPAN], col_out).astype(BF16)
    for s, n in spans(sz.rows):
        out_ref[s : s + n] += dot(row_out[:n, : n + RIM], pulled[s : s + n + RIM])


def model_term(sz, coverage, offsets, weight, wide, good, psf_rows, psf_cols, *extra):
    high = sz.rows + RIM
    return pl.pallas_call(
        functools.partial(model_kernel, sz),
        grid=(sz.epochs,),
        out_shape=jax.ShapeDtypeStruct((sz.rows, sz.width), F32),
        in_specs=[SMEM] * 3 + [VMEM] * (4 + len(extra)),
        out_specs=VMEM,
        scratch_shapes=[
            pltpu.VMEM((sz.rows + 2 * RIM, sz.wide), BF16),
            pltpu.VMEM((high, sz.wide), BF16),
            pltpu.VMEM((high, sz.wide), BF16),
            pltpu.VMEM((high, sz.width), BF16),
            pltpu.VMEM((2, sz.tap_rows, LANES), F32),
            pltpu.VMEM((2, sz.tap_rows, LANES), F32),
        ],
        compiler_params=PARAMS,
        cost_estimate=pl.CostEstimate(
            flops=sz.epochs * 1300000000, bytes_accessed=2000000, transcendentals=0
        ),
        name="model_term",
    )(coverage, offsets, weight, wide, good, psf_rows, psf_cols, *extra)


def on_device(sky_scene, images, psf_rows, psf_cols, offsets, epoch_weight, column_mask, coverage):
    sz = Sizes(images, sky_scene, psf_rows)
    peers = lax.axis_size("sky")
    depth = lax.axis_size("epoch")
    scalars = (jnp.transpose(coverage, (1, 2, 0)), offsets.T, epoch_weight)
    profiles = (psf_rows, psf_cols)

    def pairs(start, count):
        return [p for i in range(start, count - 1, 2) for p in ((i, i + 1), (i + 1, i))]

    def blocks(slots, shifts, *ends):
        return image_blocks(
            sz, slots, scalars[0], shifts, epoch_weight, images, column_mask, *profiles, *ends
        )

    first, second = edges(sz, images, sky_scene, column_mask)
    shifts, first = lax.optimization_barrier((scalars[1], first))
    first = lax.ppermute(first, "sky", pairs(0, peers))
    second = lax.ppermute(second, "sky", pairs(1, peers))
    if depth == 4:
        place = lax.axis_index("epoch")
        outer = (place == 0) | (place == 3)
        one, two = blocks((0, 1), shifts)
        one, two, wide, good = finish(
            sz, (0, 1), *scalars, sky_scene, column_mask, first, second, *profiles, one, two
        )
        got_one = lax.ppermute(one, "epoch", pairs(0, depth))
        got_two = lax.ppermute(two, "epoch", pairs(1, depth))
        shifts, two = lax.optimization_barrier((scalars[1], two))
        three, own = blocks((2, 3), shifts, first, second)
        got_three = lax.ppermute(three, "epoch", [(0, 1), (3, 2)])
        passed = jnp.where(outer, two[: sz.rows], three + got_one[: sz.rows])
        passed, good = lax.optimization_barrier((passed, good))
        got_four = lax.ppermute(passed, "epoch", [(0, 2), (3, 1), (1, 3), (2, 0)])
        model = model_term(sz, *scalars, wide, good, *profiles, own, got_one, got_two)
        return model + got_four.astype(F32) + got_three.astype(F32)

    downward = [(i, i + 1) for i in range(depth - 1)]
    upward = [(i + 1, i) for i in range(depth - 1)]
    wide, good = finish(
        sz, (), *scalars, sky_scene, column_mask, first, second, *profiles
    )
    head = lax.ppermute(wide[-RIM:], "epoch", downward)
    foot = lax.ppermute(wide[:RIM], "epoch", upward)
    terms = blocks(None, scalars[1], first, second).astype(F32)
    base = lax.psum_scatter(terms, "epoch", scatter_dimension=0, tiled=True)
    return model_term(sz, *scalars, wide, good, *profiles, head, foot, base)


def solution(mesh):
    return jax.shard_map(
        on_device,
        mesh=mesh,
        in_specs=(
            P(("field", "epoch"), "sky"),
            P(("field", "epoch"), None, "sky"),
            P("field", None),
            P("field", None),
            P("field", None),
            P("field"),
            P("field", "sky"),
            P("field", None, None),
        ),
        out_specs=P(("field", "epoch"), "sky"),
        check_vma=False,
    )
```

```python
import functools

import jax
import jax.numpy as jnp
from jax import lax
from jax.experimental import pallas as pl
from jax.experimental.pallas import tpu as pltpu
from jax.sharding import PartitionSpec as P

TILE = 512
HALO = 16
RIM = 2 * HALO
LANES = 128
SPAN = 256
STEP = SPAN - RIM
F32 = jnp.float32
BF16 = jnp.bfloat16
VMEM = pl.BlockSpec(memory_space=pltpu.VMEM)
SMEM = pl.BlockSpec(memory_space=pltpu.SMEM)
HBM = pl.BlockSpec(memory_space=pltpu.HBM)
PARAMS = pltpu.CompilerParams(vmem_limit_bytes=40 * 1024 * 1024)
SHORT = pl.CostEstimate(flops=1000, bytes_accessed=1000, transcendentals=0)
WHOLE = pltpu.CompilerParams(vmem_limit_bytes=59 * 1024 * 1024)


def up_to(value, unit):
    return -(-value // unit) * unit


def dot(a, b, dims=((1,), (0,))):
    return lax.dot_general(a, b, (dims, ((), ())), preferred_element_type=F32)


def iota(shape, dim):
    return lax.broadcasted_iota(jnp.int32, shape, dim)


def selection(rows, cols, shift):
    return (iota((rows, cols), 1) == iota((rows, cols), 0) + shift).astype(BF16)


def toeplitz(taps, start, rows, width):
    line = jnp.concatenate([taps, jnp.zeros((1, width - LANES), F32)], axis=1)
    line = jnp.broadcast_to(line, (8, width))
    line = pltpu.roll(line, lax.rem(2 * width - start, width), 1)[0:1]
    line = jnp.broadcast_to(line, (rows, width))
    return pltpu.roll(line, 0, 1, stride=1, stride_axis=0).astype(BF16)


def row_of(values, index):
    return jnp.sum(jnp.where(iota(values.shape, 0) == index, values, 0), axis=0, keepdims=True)


def load_taps(psf_ref, lines, epochs, taps):
    lines[0] = jnp.zeros(lines.shape[1:], F32)
    lines[0, :epochs, :taps] = psf_ref[...].astype(F32)
    mirror = iota((LANES, LANES), 0) + iota((LANES, LANES), 1) == taps - 1
    lines[1] = dot(lines[0].astype(BF16), mirror.astype(F32).astype(BF16))


def spans(length):
    return [(s, min(STEP, length - s)) for s in range(0, length, STEP)]


class Sizes:
    def __init__(self, images, sky_scene, psf_rows):
        self.local, self.height, self.width = images.shape
        self.rows = sky_scene.shape[0]
        self.epochs = psf_rows.shape[0]
        self.taps = psf_rows.shape[1]
        self.tile_rows = self.height // TILE
        self.wide = self.width + LANES
        self.groups = self.height // SPAN
        self.part = min(self.rows, SPAN)
        self.mask_rows = up_to(self.epochs, HALO)
        self.scene_at = SPAN * self.local
        self.mask_at = self.scene_at + self.part
        self.buffer_rows = self.mask_at + self.mask_rows
        self.blocks = self.height // self.rows
        self.tap_rows = self.mask_rows


def cover_at(coverage_ref, epoch, row_tile, col_tile):
    last_row = coverage_ref.shape[0] - 1
    last_col = coverage_ref.shape[1] - 1
    inside = (row_tile >= 0) & (row_tile <= last_row) & (col_tile >= 0) & (col_tile <= last_col)
    value = coverage_ref[jnp.clip(row_tile, 0, last_row), jnp.clip(col_tile, 0, last_col), epoch]
    return jnp.where(inside, value, 0).astype(F32)


def tile_of(position):
    return (position + TILE) // TILE - 1


def low(index, size):
    return index & (size - 1)


def high(index, size):
    return lax.shift_right_logical(index, size.bit_length() - 1)


def packing(count, width, shift):
    row, lane = iota((LANES * count, LANES), 0), iota((LANES * count, LANES), 1)
    here = high(lane, width) == high(row, LANES)
    here &= low(row, LANES) == low(lane, width) + shift
    return here.astype(F32).astype(BF16)


def side_by_side(ref, count, rows):
    return jnp.concatenate([ref[g * rows : (g + 1) * rows] for g in range(count)], axis=1)


def edge_copies(sz, images_ref, scene_ref, edge, sides, sem, side_sem):
    places = (0, sz.width - LANES)
    copies = []
    for e in range(sz.local):
        for side in range(2):
            slot = 2 * e + side
            copies.append(
                pltpu.make_async_copy(
                    images_ref.at[e, :, pl.ds(places[side], LANES)], edge.at[slot], sem.at[slot]
                )
            )
    side_copies = [
        pltpu.make_async_copy(
            scene_ref.at[:, pl.ds(places[side], LANES)], sides.at[side], side_sem.at[side]
        )
        for side in range(2)
    ]
    return copies, side_copies


def pack_edges(sz, flags, edge, sides, copies, side_copies, first_ref, second_ref):
    epoch = lax.axis_index("epoch") * sz.local
    even = lax.axis_index("sky") % 2 == 0
    places = (0, sz.width - LANES)

    def put(left, right, rows):
        first_ref[rows] = jnp.where(even, right, left).astype(BF16)
        second_ref[rows] = jnp.where(even, left, right).astype(BF16)

    packs = [packing(sz.groups, HALO, shift) for shift in (0, LANES - HALO)]
    row, lane = iota((LANES, LANES), 0), iota((LANES, LANES), 1)
    repeats = [
        (row == low(lane, HALO) + shift).astype(F32).astype(BF16) for shift in (0, LANES - HALO)
    ]
    for copy in copies + side_copies:
        copy.wait()
    goods, rows_good = [], []
    for side in range(2):
        good = flags[:, places[side] : places[side] + LANES].astype(F32)
        rows_good.append(good)
        if side == 1:
            good = pltpu.roll(good, HALO, 1)
        if sz.mask_rows > sz.epochs:
            good = jnp.concatenate(
                [good, jnp.zeros((sz.mask_rows - sz.epochs, LANES), F32)], axis=0
            )
        goods.append(good)
    put(goods[0], goods[1], slice(sz.mask_at, sz.buffer_rows))
    for e in range(sz.local):
        lines = []
        for side in range(2):
            slot = 2 * e + side
            good = jnp.broadcast_to(row_of(rows_good[side], epoch + e), (HALO, LANES))
            good = dot(good.astype(BF16), repeats[side])[0:1]
            lines.append(dot(side_by_side(edge.at[slot], sz.groups, SPAN), packs[side]) * good)
        put(lines[0], lines[1], slice(SPAN * e, SPAN * (e + 1)))
    cells = []
    count = sz.rows // sz.part
    for side, shift in enumerate((0, LANES - RIM)):
        cells.append(
            dot(side_by_side(sides.at[side], count, sz.part), packing(count, RIM, shift))
        )
    put(cells[0], cells[1], slice(sz.scene_at, sz.mask_at))


def edges_kernel(sz, images_ref, scene_ref, mask_ref, first_ref, second_ref, *scratch):
    edge, sides, flags, sem, side_sem, flag_sem = scratch
    copies, side_copies = edge_copies(sz, images_ref, scene_ref, edge, sides, sem, side_sem)
    flag_copy = pltpu.make_async_copy(mask_ref, flags, flag_sem)
    for copy in [flag_copy] + copies + side_copies:
        copy.start()
    flag_copy.wait()
    pack_edges(sz, flags, edge, sides, copies, side_copies, first_ref, second_ref)


def edges(sz, images, scene, mask):
    shape = jax.ShapeDtypeStruct((sz.buffer_rows, LANES), BF16)
    return pl.pallas_call(
        functools.partial(edges_kernel, sz),
        out_shape=(shape, shape),
        in_specs=[HBM, HBM, HBM],
        out_specs=(VMEM, VMEM),
        scratch_shapes=[
            pltpu.VMEM((2 * sz.local, sz.height, LANES), BF16),
            pltpu.VMEM((2, sz.rows, LANES), BF16),
            pltpu.VMEM((sz.epochs, sz.width), jnp.int32),
            pltpu.SemaphoreType.DMA((2 * sz.local,)),
            pltpu.SemaphoreType.DMA((2,)),
            pltpu.SemaphoreType.DMA,
        ],
        compiler_params=WHOLE,
        cost_estimate=SHORT,
        name="edges",
    )(images, scene, mask)


def sides_of(first, second):
    even = lax.axis_index("sky") % 2 == 0
    return jnp.where(even, second, first), jnp.where(even, first, second)


def widen_rows(sz, scene_ref, first_ref, second_ref, start, count):
    group, inside = start // sz.part, start % sz.part
    cells = slice(sz.scene_at + inside, sz.scene_at + inside + count)
    row, lane = iota((LANES, sz.wide), 0), iota((LANES, sz.wide), 1)
    wide = dot(scene_ref[start : start + count], selection(sz.width, sz.wide, RIM))
    ends = sides_of(first_ref[cells], second_ref[cells])
    for end, at in zip(ends, (0, sz.width + RIM)):
        place = (high(row, RIM) == group) & (lane == low(row, RIM) + at)
        wide += dot(end, place.astype(F32).astype(BF16))
    return wide.astype(BF16)


def widen_kernel(sz, scene_ref, mask_ref, first_ref, second_ref, wide_ref, good_ref):
    for start in range(0, sz.rows, sz.part):
        wide_ref[start : start + sz.part] = widen_rows(
            sz, scene_ref, first_ref, second_ref, start, sz.part
        )
    flags = slice(sz.mask_at, sz.buffer_rows)
    before, after = sides_of(first_ref[flags], second_ref[flags])
    own = mask_ref[...].astype(F32)
    if sz.mask_rows > sz.epochs:
        own = jnp.concatenate(
            [own, jnp.zeros((sz.mask_rows - sz.epochs, sz.width), F32)], axis=0
        )
    good = dot(own.astype(BF16), selection(sz.width, sz.wide, HALO))
    inner = iota((LANES, sz.wide), 0) < HALO
    zero = jnp.zeros((LANES, sz.wide), BF16)
    good += dot(before, jnp.where(inner, selection(LANES, sz.wide, 0), zero))
    good += dot(after, jnp.where(inner, selection(LANES, sz.wide, sz.width + HALO), zero))
    good_ref[...] = good


def destination(slot, place):
    return (
        3 * (1 - place % 2),
        2 - place // 2,
        (2 * place + 1) % 5,
        place,
    )[slot]


def rim_rows(sz, epoch, e, coverage_ref, row_line, row_shift, twice, first_ref, second_ref):
    rows = slice(SPAN * e, SPAN * (e + 1))
    column = lax.axis_index("sky") * sz.width
    both = jnp.concatenate(sides_of(first_ref[rows], second_ref[rows]), axis=1)
    lane = iota((1, 2 * LANES), 1)
    factor = jnp.zeros((1, 2 * LANES), F32)
    for side, at in enumerate((column - HALO, column + sz.width)):
        for tile in range(sz.tile_rows):
            cover = cover_at(coverage_ref, epoch, tile, tile_of(at))
            here = high(lane, LANES) == side
            here &= high(low(lane, LANES), HALO * TILE // SPAN) == tile
            factor = jnp.where(here, cover, factor)
    both = both.astype(F32) * factor
    above = pltpu.roll(both[SPAN - HALO :], HALO, 1)
    below = pltpu.roll(both[:HALO], 2 * LANES - HALO, 1)
    above = jnp.where(low(lane, LANES) < HALO, 0.0, above)
    below = jnp.where(low(lane, LANES) >= HALO * (sz.groups - 1), 0.0, below)
    window = jnp.concatenate([above, both, below], axis=0).astype(BF16)
    table = toeplitz(row_line, row_shift - 4, SPAN, SPAN + LANES)[:, : SPAN + RIM]
    return (dot(table, window) * twice).astype(BF16)


def rim_columns(col_line, col_shift):
    enter = toeplitz(col_line, 28 - col_shift, HALO, SPAN)[:, :LANES]
    leave = toeplitz(col_line, SPAN + LANES - 116 - col_shift, HALO, SPAN + LANES)[:, :LANES]
    none = jnp.zeros((HALO, LANES), BF16)
    upper = [jnp.concatenate([enter, none], axis=1)] * (LANES // HALO)
    lower = [jnp.concatenate([none, leave], axis=1)] * (LANES // HALO)
    return jnp.concatenate(upper + lower, axis=0)


def rim_part(sz, start, rim_ref, table):
    group = start // SPAN
    row = iota((2 * LANES, SPAN), 0)
    parts = []
    for k in range(max(sz.rows // SPAN, 1)):
        picked = jnp.where(high(low(row, LANES), HALO) == group + k, table, jnp.zeros_like(table))
        if sz.rows >= SPAN:
            rows = rim_ref[...]
        else:
            rows = rim_ref[pl.ds(pl.multiple_of(start - group * SPAN, sz.rows), sz.rows)]
        parts.append(dot(rows, picked))
    return jnp.concatenate(parts, axis=0) if len(parts) > 1 else parts[0]


def rim_places(sz, h):
    row, lane = iota((SPAN, LANES), 0), iota((SPAN, LANES), 1)
    here = (lane == row + RIM * h) & (row < HALO)
    here |= (lane == row - SPAN + RIM * (h + 1)) & (row >= SPAN - HALO)
    return here.astype(F32).astype(BF16)


def rim_spread(sz, h):
    row, lane = iota((LANES, SPAN), 0), iota((LANES, SPAN), 1)
    here = (row == lane + RIM * h) & (lane < HALO)
    here |= (row == lane - SPAN + RIM * (h + 1)) & (lane >= SPAN - HALO)
    return here.astype(F32).astype(BF16)


def pack_rows(sz, ref, at, rim):
    ref[at : at + RIM] = rim[:, : sz.width]
    left = slice(at + RIM, at + RIM + HALO)
    ref[left, :LANES] = rim[:HALO, sz.width :]
    ref[left, LANES:SPAN] = rim[HALO:, sz.width :]
    ref[left, SPAN:] = jnp.zeros((HALO, sz.width - SPAN), BF16)


def pack_part(sz, ref, at, part):
    total = None
    for h in range(sz.rows // LANES):
        rows = part[h * LANES : (h + 1) * LANES].astype(BF16)
        moved = dot(rows, rim_places(sz, h))
        total = moved if total is None else total + moved
    total = total.astype(BF16)
    for k in range(LANES // RIM):
        ref[at : at + RIM, k * LANES : (k + 1) * LANES] = total[k * RIM : (k + 1) * RIM]


def unpack_rim(sz, ref, at):
    left = slice(at + RIM, at + RIM + HALO)
    rest = jnp.concatenate([ref[left, :LANES], ref[left, LANES:SPAN]], axis=0)
    return jnp.concatenate([ref[at : at + RIM], rest], axis=1)


def unpack_part(sz, ref, at):
    pieces = [ref[at : at + RIM, k * LANES : (k + 1) * LANES] for k in range(LANES // RIM)]
    packed = jnp.concatenate(pieces, axis=0)
    parts = [dot(packed, rim_spread(sz, h)) for h in range(sz.rows // LANES)]
    return jnp.concatenate(parts, axis=0)


def complete(sz, block, part):
    left, right = slice(0, LANES), slice(sz.width - LANES, sz.width)
    mid = slice(LANES, sz.width - LANES)
    return (
        (left, (block[:, left].astype(F32) + part[:, :LANES]).astype(BF16)),
        (mid, block[:, mid]),
        (right, (block[:, right].astype(F32) + part[:, LANES:]).astype(BF16)),
    )


def rim_parts_of(sz, slots, place, offsets_ref, col_lines, rim_ref):
    tables = []
    for e in range(sz.local):
        epoch = place * sz.local + e
        tables.append(rim_columns(row_of(col_lines[0], epoch), offsets_ref[1, epoch]))
    parts = []
    for slot in slots:
        part = None
        for e in range(sz.local):
            term = rim_part(sz, destination(slot, place) * sz.rows, rim_ref.at[e], tables[e])
            part = term if part is None else part + term
        parts.append(part)
    return parts


def early_kernel(
    sz, coverage_ref, offsets_ref, weight_ref, scene_ref, first_ref, second_ref,
    psf_rows_ref, psf_cols_ref, one_ref, three_ref, near_out, far_out, pass_out, rim_ref,
    row_lines, col_lines,
):
    place = lax.axis_index("epoch")
    outer = (place == 0) | (place == 3)
    load_taps(psf_rows_ref, row_lines, sz.epochs, sz.taps)
    load_taps(psf_cols_ref, col_lines, sz.epochs, sz.taps)
    for e in range(sz.local):
        epoch = place * sz.local + e
        rim_ref[e] = rim_rows(
            sz, epoch, e, coverage_ref, row_of(row_lines[1], epoch), offsets_ref[0, epoch],
            -2.0 * weight_ref[epoch], first_ref, second_ref,
        )
    parts = rim_parts_of(sz, (0, 2, 1), place, offsets_ref, col_lines, rim_ref)
    top = widen_rows(sz, scene_ref, first_ref, second_ref, 0, RIM)
    bottom = widen_rows(sz, scene_ref, first_ref, second_ref, sz.rows - RIM, RIM)
    pack_rows(sz, near_out, sz.rows, jnp.where(place % 2 == 0, bottom, top))
    pack_rows(sz, far_out, 0, jnp.where(place < 2, bottom, top))
    pack_part(sz, far_out, RIM + HALO, parts[2])
    first_block, third_block = complete(sz, one_ref, parts[0]), complete(sz, three_ref, parts[1])
    for (cols, other), (_, mine) in zip(first_block, third_block):
        near_out[: sz.rows, cols] = jnp.where(outer, mine, other)
        pass_out[: sz.rows, cols] = mine
    pass_out[sz.rows :] = jnp.zeros((HALO, sz.width), BF16)


def early(sz, coverage, offsets, weight, scene, first, second, psf_rows, psf_cols, one, three):
    return pl.pallas_call(
        functools.partial(early_kernel, sz),
        out_shape=(
            jax.ShapeDtypeStruct((sz.rows + RIM + HALO, sz.width), BF16),
            jax.ShapeDtypeStruct((2 * RIM + HALO, sz.width), BF16),
            jax.ShapeDtypeStruct((sz.rows + HALO, sz.width), BF16),
            jax.ShapeDtypeStruct((sz.local, SPAN, 2 * LANES), BF16),
        ),
        in_specs=[SMEM] * 3 + [VMEM] * 7,
        out_specs=(VMEM, VMEM, VMEM, VMEM),
        scratch_shapes=[pltpu.VMEM((2, sz.tap_rows, LANES), F32)] * 2,
        compiler_params=PARAMS,
        cost_estimate=SHORT,
        name="early",
    )(coverage, offsets, weight, scene, first, second, psf_rows, psf_cols, one, three)


def finish_kernel(sz, offsets_ref, scene_ref, mask_ref, first_ref, second_ref, *more):
    if sz.blocks != 4:
        widen_kernel(sz, scene_ref, mask_ref, first_ref, second_ref, *more)
        return
    psf_cols_ref, rim_ref, two_ref, own_ref, wide_ref, good_ref, fix_out = more[:7]
    two_out, own_out, col_lines = more[7:]
    place = lax.axis_index("epoch")
    load_taps(psf_cols_ref, col_lines, sz.epochs, sz.taps)
    parts = rim_parts_of(sz, (0, 1, 3), place, offsets_ref, col_lines, rim_ref)
    widen_kernel(sz, scene_ref, mask_ref, first_ref, second_ref, wide_ref, good_ref)
    pack_part(sz, fix_out, 0, parts[0])
    for block, out, part in ((two_ref, two_out, parts[1]), (own_ref, own_out, parts[2])):
        for cols, value in complete(sz, block, part):
            out[:, cols] = value


def finish(sz, offsets, scene, mask, first, second, *more):
    full = jax.ShapeDtypeStruct((sz.rows, sz.width), BF16)
    shapes = [
        jax.ShapeDtypeStruct((sz.rows, sz.wide), BF16),
        jax.ShapeDtypeStruct((sz.mask_rows, sz.wide), F32),
    ]
    scratch = []
    if more:
        shapes += [jax.ShapeDtypeStruct((RIM, sz.width), BF16), full, full]
        scratch = [pltpu.VMEM((2, sz.tap_rows, LANES), F32)]
    return pl.pallas_call(
        functools.partial(finish_kernel, sz),
        out_shape=tuple(shapes),
        in_specs=[SMEM] + [VMEM] * (4 + len(more)),
        out_specs=tuple([VMEM] * len(shapes)),
        scratch_shapes=scratch,
        compiler_params=PARAMS,
        cost_estimate=SHORT,
        name="finish",
    )(offsets, scene, mask, first, second, *more)


def image_kernel(sz, slots, rims, packs, images_ref, *more):
    count = 1 if slots is None else len(slots)
    small, ends, more = more[:6], more[6 : 6 + rims], more[6 + rims :]
    if packs:
        scene_ref, *more = more
    outs, more = more[:count], more[count:]
    if packs:
        first_out, second_out, edge, sides, edge_sem, side_sem, *more = more
    held, small_sem, more = more[:6], more[6], more[7:]
    coverage_ref, offsets_ref, weight_ref, mask_ref, psf_rows_ref, psf_cols_ref = held
    window, row_done, row_lines, col_lines, row_table, main_table, cross_table, rim_ref, sem = more
    place = lax.axis_index("epoch")
    first = place * sz.local
    column = lax.axis_index("sky") * sz.width
    if slots is None:
        targets = [pl.program_id(0)]
    else:
        targets = [destination(slot, place) for slot in slots]

    copies = []
    for i, target in enumerate(targets):
        start = target * sz.rows
        head = jnp.maximum(start - HALO, 0)
        foot = jnp.minimum(start + sz.rows, sz.height - HALO)
        for e in range(sz.local):
            for n, (source, at, length) in enumerate(
                ((start, HALO, sz.rows), (head, 0, HALO), (foot, HALO + sz.rows, HALO))
            ):
                copies.append(
                    pltpu.make_async_copy(
                        images_ref.at[e, pl.ds(pl.multiple_of(source, HALO), length), :],
                        window.at[i, e, pl.ds(at, length), :],
                        sem.at[i, e, n],
                    )
                )
    held_copies = [
        pltpu.make_async_copy(source, target, small_sem.at[n])
        for n, (source, target) in enumerate(zip(small, held))
    ]
    for copy in held_copies + copies:
        copy.start()
    if packs:
        edge_waits = edge_copies(sz, images_ref, scene_ref, edge, sides, edge_sem, side_sem)
        for copy in edge_waits[0] + edge_waits[1]:
            copy.start()
    for copy in held_copies:
        copy.wait()
    load_taps(psf_rows_ref, row_lines, sz.epochs, sz.taps)
    load_taps(psf_cols_ref, col_lines, sz.epochs, sz.taps)
    for e in range(sz.local):
        epoch = first + e
        row_shift, col_shift = offsets_ref[0, epoch], offsets_ref[1, epoch]
        row_table[e] = toeplitz(row_of(row_lines[1], epoch), row_shift - 4, STEP, SPAN)
        line = row_of(col_lines[0], epoch)
        main = toeplitz(line, 12 - col_shift, SPAN, SPAN + LANES)[:, :SPAN]
        main_table[e] = main
        apart = (iota((SPAN, SPAN), 0) < LANES) != (iota((SPAN, SPAN), 1) < LANES)
        cross_table[e] = jnp.where(apart, main, jnp.zeros_like(main))
    rim_parts = []
    for e in range(sz.local if rims else 0):
        epoch = first + e
        rim_ref[e] = rim_rows(
            sz, epoch, e, coverage_ref, row_of(row_lines[1], epoch), offsets_ref[0, epoch],
            -2.0 * weight_ref[epoch], *ends,
        )
        table = rim_columns(row_of(col_lines[0], epoch), offsets_ref[1, epoch])
        for i, target in enumerate(targets):
            part = rim_part(sz, target * sz.rows, rim_ref.at[e], table)
            if e == 0:
                rim_parts.append(part)
            else:
                rim_parts[i] += part
    column_tile = column // TILE
    for i, target in enumerate(targets):
        for copy in copies[3 * sz.local * i : 3 * sz.local * (i + 1)]:
            copy.wait()
        start = target * sz.rows
        zones = (
            (0, HALO, tile_of(start - HALO)),
            (HALO, HALO + sz.rows, tile_of(start)),
            (HALO + sz.rows, RIM + sz.rows, tile_of(start + sz.rows)),
        )
        for e in range(sz.local):
            epoch = first + e
            good = row_of(mask_ref[...].astype(F32), epoch)
            for begin, end, tile in zones:
                factor = good * cover_at(coverage_ref, epoch, tile, column_tile)
                window[i, e, begin:end] = window[i, e, begin:end] * factor.astype(BF16)
            twice = -2.0 * weight_ref[epoch]
            for s, n in spans(sz.rows):
                part = dot(row_table[e, :n, : n + RIM], window[i, e, s : s + n + RIM])
                row_done[i, e, s : s + n] = (part * twice).astype(BF16)
    for i in range(count):
        total = []
        for b in range(0, sz.width, SPAN):
            out = None
            for e in range(sz.local):
                part = dot(row_done[i, e, :, b : b + SPAN], main_table[e])
                out = part if out is None else out + part
            total += [out[:, :LANES], out[:, LANES:]]
        for b in range(LANES, sz.width - LANES, SPAN):
            out = None
            for e in range(sz.local):
                part = dot(row_done[i, e, :, b : b + SPAN], cross_table[e])
                out = part if out is None else out + part
            total[b // LANES] += out[:, :LANES]
            total[b // LANES + 1] += out[:, LANES:]
        if rims:
            total[0] += rim_parts[i][:, :LANES]
            total[-1] += rim_parts[i][:, LANES:]
        for k, piece in enumerate(total):
            outs[i][:, k * LANES : (k + 1) * LANES] = piece.astype(BF16)
    if packs:
        pack_edges(sz, mask_ref, edge, sides, *edge_waits, first_out, second_out)


def image_blocks(
    sz, slots, coverage, offsets, weight, images, mask, psf_rows, psf_cols, *ends, scene=None
):
    packs = scene is not None
    if slots is None:
        count = 1
        grid = dict(
            grid=(sz.blocks,),
            out_shape=jax.ShapeDtypeStruct((sz.blocks * sz.rows, sz.width), BF16),
            out_specs=pl.BlockSpec((sz.rows, sz.width), lambda i: (i, 0)),
        )
    else:
        count = len(slots)
        shapes = [jax.ShapeDtypeStruct((sz.rows, sz.width), BF16)] * count
        if packs:
            shapes += [jax.ShapeDtypeStruct((sz.buffer_rows, LANES), BF16)] * 2
        grid = dict(out_shape=tuple(shapes), out_specs=tuple([VMEM] * len(shapes)))
    pack_scratch = [
        pltpu.VMEM((2 * sz.local, sz.height, LANES), BF16),
        pltpu.VMEM((2, sz.rows, LANES), BF16),
        pltpu.SemaphoreType.DMA((2 * sz.local,)),
        pltpu.SemaphoreType.DMA((2,)),
    ]
    return pl.pallas_call(
        functools.partial(image_kernel, sz, slots, len(ends), packs),
        in_specs=[HBM] * 7 + [VMEM] * len(ends) + [HBM] * packs,
        scratch_shapes=pack_scratch * packs
        + [
            pltpu.SMEM(coverage.shape, jnp.int32),
            pltpu.SMEM(offsets.shape, jnp.int32),
            pltpu.SMEM(weight.shape, F32),
            pltpu.VMEM(mask.shape, jnp.int32),
            pltpu.VMEM(psf_rows.shape, BF16),
            pltpu.VMEM(psf_cols.shape, BF16),
            pltpu.SemaphoreType.DMA((6,)),
            pltpu.VMEM((count, sz.local, sz.rows + RIM, sz.width), BF16),
            pltpu.VMEM((count, sz.local, sz.rows, sz.width), BF16),
            pltpu.VMEM((2, sz.tap_rows, LANES), F32),
            pltpu.VMEM((2, sz.tap_rows, LANES), F32),
            pltpu.VMEM((sz.local, STEP, SPAN), BF16),
            pltpu.VMEM((sz.local, SPAN, SPAN), BF16),
            pltpu.VMEM((sz.local, SPAN, SPAN), BF16),
            pltpu.VMEM((sz.local, SPAN, 2 * LANES), BF16),
            pltpu.SemaphoreType.DMA((count, sz.local, 3)),
        ],
        compiler_params=WHOLE if slots is not None and 0 in slots else PARAMS,
        cost_estimate=SHORT,
        name="image_blocks",
        **grid,
    )(images, coverage, offsets, weight, mask, psf_rows, psf_cols, *ends, *([scene] * packs))


def column_tables(taps, start):
    pair = toeplitz(taps, start, LANES, SPAN)
    here, past = pair[:, :LANES], pair[:, LANES:]
    none = jnp.zeros_like(here)
    main = jnp.concatenate(
        [jnp.concatenate([here, none], axis=1), jnp.concatenate([past, here], axis=1)], axis=0
    )
    rest = jnp.concatenate(
        [jnp.concatenate([past, none], axis=1), jnp.concatenate([none, past], axis=1)], axis=0
    )
    return main, rest, here, past


def column_pass(sz, source, tables, tail):
    main, rest, here, past = tables
    tiles = []
    for b in range(0, sz.width, SPAN):
        out = dot(source[:, b : b + SPAN], main)
        tiles += [out[:, :LANES], out[:, LANES:]]
    ends = list(range(SPAN, sz.wide, SPAN))
    if len(ends) == 2:
        joined = jnp.concatenate([source[:, at : at + LANES] for at in ends], axis=1)
        out = dot(joined, rest)
        parts = [out[:, :LANES], out[:, LANES:]]
    else:
        parts = [dot(source[:, at : at + LANES], past) for at in ends]
    for at, part in zip(ends, parts):
        tiles[at // LANES - 1] += part
    if tail:
        tiles.append(dot(source[:, sz.width : sz.wide], here))
    return tiles


def model_kernel(
    sz, batch, coverage_ref, offsets_ref, weight_ref,
    wide_ref, good_ref, psf_rows_ref, psf_cols_ref, *more,
):
    *extra, out_ref, scene, lifted, residual, pulled, row_lines, col_lines = more
    step = pl.program_id(0)
    place = lax.axis_index("epoch")
    start = place * sz.rows
    column = lax.axis_index("sky") * sz.width

    @pl.when(step == 0)
    def _():
        load_taps(psf_rows_ref, row_lines, sz.epochs, sz.taps)
        load_taps(psf_cols_ref, col_lines, sz.epochs, sz.taps)
        scene[RIM : RIM + sz.rows] = wide_ref[...]
        if sz.blocks != 4:
            head_ref, foot_ref, base_ref = extra
            scene[0:RIM] = head_ref[...]
            scene[RIM + sz.rows :] = foot_ref[...]
            out_ref[...] = base_ref[...]
        else:
            own_ref, two_ref, near_ref, far_ref = extra
            near, far = unpack_rim(sz, near_ref, sz.rows), unpack_rim(sz, far_ref, 0)
            none = jnp.zeros_like(near)
            outer = (place == 0) | (place == 3)
            odd = place % 2 == 1
            scene[0:RIM] = jnp.where(odd, near, jnp.where(outer, none, far))
            scene[RIM + sz.rows :] = jnp.where(odd, jnp.where(outer, none, far), near)
            fix = unpack_part(sz, far_ref, RIM + HALO)
            for b in range(0, sz.width, LANES):
                cols = slice(b, b + LANES)
                base = own_ref[:, cols].astype(F32) + two_ref[:, cols].astype(F32)
                base += near_ref[: sz.rows, cols].astype(F32)
                for at, side in ((0, 0), (LANES, sz.width - LANES)):
                    if b == side:
                        base += fix[:, at : at + LANES]
                out_ref[:, cols] = base

    epochs = [step * batch + n for n in range(batch)]
    edge = sz.rows + HALO
    for n, epoch in enumerate(epochs):
        row_in = toeplitz(row_of(row_lines[0], epoch), -4 - offsets_ref[0, epoch], STEP, SPAN)
        for s, count in spans(sz.rows + RIM):
            lifted[n, s : s + count] = dot(
                row_in[:count, : count + RIM], scene[s : s + count + RIM]
            ).astype(BF16)
    for n, epoch in enumerate(epochs):
        good = row_of(good_ref[...], epoch) * (2.0 * weight_ref[epoch])
        lane = iota((1, sz.wide), 1)
        factors = []
        for row_tile in (tile_of(start - HALO), tile_of(start), tile_of(start + sz.rows)):
            left, here, right = (
                cover_at(coverage_ref, epoch, row_tile, tile_of(c))
                for c in (column - HALO, column, column + sz.width)
            )
            factors.append(
                good * jnp.where(lane < HALO, left, jnp.where(lane < HALO + sz.width, here, right))
            )
        tables = column_tables(row_of(col_lines[1], epoch), 28 + offsets_ref[1, epoch])
        for k, modeled in enumerate(column_pass(sz, lifted[n], tables, True)):
            b = k * LANES
            head, mid, foot = (f[:, b : b + LANES] for f in factors)
            residual[n, 0:HALO, b : b + LANES] = (modeled[0:HALO] * head).astype(BF16)
            residual[n, HALO:edge, b : b + LANES] = (modeled[HALO:edge] * mid).astype(BF16)
            residual[n, edge:, b : b + LANES] = (modeled[edge:] * foot).astype(BF16)
    for n, epoch in enumerate(epochs):
        tables = column_tables(row_of(col_lines[0], epoch), 28 - offsets_ref[1, epoch])
        for k, tile in enumerate(column_pass(sz, residual[n], tables, False)):
            pulled[n, :, k * LANES : (k + 1) * LANES] = tile.astype(BF16)
    row_outs = [
        toeplitz(row_of(row_lines[1], epoch), offsets_ref[0, epoch] - 4, STEP, SPAN)
        for epoch in epochs
    ]
    for s, count in spans(sz.rows):
        total = out_ref[s : s + count]
        for n in range(batch):
            total += dot(row_outs[n][:count, : count + RIM], pulled[n, s : s + count + RIM])
        out_ref[s : s + count] = total


def model_term(sz, coverage, offsets, weight, wide, good, psf_rows, psf_cols, *extra):
    high = sz.rows + RIM
    batch = 4 if sz.epochs % 4 == 0 else 1
    return pl.pallas_call(
        functools.partial(model_kernel, sz, batch),
        grid=(sz.epochs // batch,),
        out_shape=jax.ShapeDtypeStruct((sz.rows, sz.width), F32),
        in_specs=[SMEM] * 3 + [VMEM] * (4 + len(extra)),
        out_specs=VMEM,
        scratch_shapes=[
            pltpu.VMEM((sz.rows + 2 * RIM, sz.wide), BF16),
            pltpu.VMEM((batch, high, sz.wide), BF16),
            pltpu.VMEM((batch, high, sz.wide), BF16),
            pltpu.VMEM((batch, high, sz.width), BF16),
            pltpu.VMEM((2, sz.tap_rows, LANES), F32),
            pltpu.VMEM((2, sz.tap_rows, LANES), F32),
        ],
        compiler_params=PARAMS,
        cost_estimate=SHORT,
        name="model_term",
    )(coverage, offsets, weight, wide, good, psf_rows, psf_cols, *extra)


def spread_kernel(sz, part_ref, model_ref, out_ref):
    part = unpack_part(sz, part_ref, 0)
    for at, cols in ((0, slice(0, LANES)), (LANES, slice(sz.width - LANES, sz.width))):
        out_ref[:, cols] = model_ref[:, cols] + part[:, at : at + LANES]


def spread(sz, part, model):
    return pl.pallas_call(
        functools.partial(spread_kernel, sz),
        out_shape=jax.ShapeDtypeStruct(model.shape, F32),
        in_specs=[VMEM, VMEM],
        out_specs=VMEM,
        input_output_aliases={1: 0},
        compiler_params=PARAMS,
        cost_estimate=SHORT,
        name="spread",
    )(part, model)


def on_device(sky_scene, images, psf_rows, psf_cols, offsets, epoch_weight, column_mask, coverage):
    sz = Sizes(images, sky_scene, psf_rows)
    peers = lax.axis_size("sky")
    depth = lax.axis_size("epoch")
    scalars = (jnp.transpose(coverage, (1, 2, 0)), offsets.T, epoch_weight)
    profiles = (psf_rows, psf_cols)

    def pairs(start, count):
        return [p for i in range(start, count - 1, 2) for p in ((i, i + 1), (i + 1, i))]

    def blocks(slots, shifts, *ends, scene=None):
        return image_blocks(
            sz, slots, scalars[0], shifts, epoch_weight, images, column_mask, *profiles, *ends,
            scene=scene,
        )

    if depth == 4:
        one, two, first, second = blocks((0, 1), scalars[1], scene=sky_scene)
        got_one = lax.ppermute(one, "epoch", [(0, 1), (3, 2)])
        got_two = lax.ppermute(two, "epoch", pairs(1, depth))
        shifts, one = lax.optimization_barrier((scalars[1], one))
        three, own = blocks((2, 3), shifts)
        first = lax.ppermute(first, "sky", pairs(0, peers))
        second = lax.ppermute(second, "sky", pairs(1, peers))
        near, far, passed, rim = early(
            sz, *scalars, sky_scene, first, second, *profiles, one, three
        )
        got_near = lax.ppermute(near, "epoch", pairs(0, depth))
        got_far = lax.ppermute(far, "epoch", pairs(1, depth))
        passed += jnp.pad(got_one, ((0, HALO), (0, 0)))
        passed, got_far, got_two, rim = lax.optimization_barrier((passed, got_far, got_two, rim))
        got_passed = lax.ppermute(passed, "epoch", [(1, 3), (2, 0)])
        wide, good, fix, two, own = finish(
            sz, scalars[1], sky_scene, column_mask, first, second, psf_cols, rim, two, own
        )
        got_fix = lax.ppermute(fix, "epoch", [(0, 3), (3, 0)])
        got_last = lax.ppermute(two, "epoch", [(0, 2), (3, 1)])
        model = model_term(sz, *scalars, wide, good, *profiles, own, got_two, got_near, got_far)
        model = spread(sz, got_fix, model)
        return model + (got_passed[: sz.rows].astype(F32) + got_last.astype(F32))

    first, second = edges(sz, images, sky_scene, column_mask)
    first = lax.ppermute(first, "sky", pairs(0, peers))
    second = lax.ppermute(second, "sky", pairs(1, peers))
    downward = [(i, i + 1) for i in range(depth - 1)]
    upward = [(i + 1, i) for i in range(depth - 1)]
    wide, good = finish(sz, scalars[1], sky_scene, column_mask, first, second)
    head = lax.ppermute(wide[-RIM:], "epoch", downward)
    foot = lax.ppermute(wide[:RIM], "epoch", upward)
    terms = blocks(None, scalars[1], first, second).astype(F32)
    base = lax.psum_scatter(terms, "epoch", scatter_dimension=0, tiled=True)
    return model_term(sz, *scalars, wide, good, *profiles, head, foot, base)


def solution(mesh):
    return jax.shard_map(
        on_device,
        mesh=mesh,
        in_specs=(
            P(("field", "epoch"), "sky"),
            P(("field", "epoch"), None, "sky"),
            P("field", None),
            P("field", None),
            P("field", None),
            P("field"),
            P("field", "sky"),
            P("field", None, None),
        ),
        out_specs=P(("field", "epoch"), "sky"),
        check_vma=False,
    )
```

```python
import functools

import jax
import jax.numpy as jnp
from jax import lax
from jax.experimental import pallas as pl
from jax.experimental.pallas import tpu as pltpu
from jax.sharding import PartitionSpec as P

TILE = 512
HALO = 16
RIM = 2 * HALO
LANES = 128
SPAN = 256
STEP = SPAN - RIM
F32 = jnp.float32
BF16 = jnp.bfloat16
VMEM = pl.BlockSpec(memory_space=pltpu.VMEM)
SMEM = pl.BlockSpec(memory_space=pltpu.SMEM)
HBM = pl.BlockSpec(memory_space=pltpu.HBM)
PARAMS = pltpu.CompilerParams(vmem_limit_bytes=40 * 1024 * 1024)
SHORT = pl.CostEstimate(flops=1000, bytes_accessed=1000, transcendentals=0)
WHOLE = pltpu.CompilerParams(vmem_limit_bytes=59 * 1024 * 1024)


def up_to(value, unit):
    return -(-value // unit) * unit


def dot(a, b, dims=((1,), (0,))):
    return lax.dot_general(a, b, (dims, ((), ())), preferred_element_type=F32)


def iota(shape, dim):
    return lax.broadcasted_iota(jnp.int32, shape, dim)


def selection(rows, cols, shift):
    return (iota((rows, cols), 1) == iota((rows, cols), 0) + shift).astype(BF16)


def toeplitz(taps, start, rows, width):
    line = jnp.concatenate([taps, jnp.zeros((1, width - LANES), F32)], axis=1)
    line = jnp.broadcast_to(line, (8, width))
    line = pltpu.roll(line, lax.rem(2 * width - start, width), 1)[0:1]
    line = jnp.broadcast_to(line, (rows, width))
    return pltpu.roll(line, 0, 1, stride=1, stride_axis=0).astype(BF16)


def row_of(values, index):
    return jnp.sum(jnp.where(iota(values.shape, 0) == index, values, 0), axis=0, keepdims=True)


def load_taps(psf_ref, lines, epochs, taps):
    lines[0] = jnp.zeros(lines.shape[1:], F32)
    lines[0, :epochs, :taps] = psf_ref[...].astype(F32)
    mirror = iota((LANES, LANES), 0) + iota((LANES, LANES), 1) == taps - 1
    lines[1] = dot(lines[0].astype(BF16), mirror.astype(F32).astype(BF16))


def spans(length):
    return [(s, min(STEP, length - s)) for s in range(0, length, STEP)]


class Sizes:
    def __init__(self, images, sky_scene, psf_rows):
        self.local, self.height, self.width = images.shape
        self.rows = sky_scene.shape[0]
        self.epochs = psf_rows.shape[0]
        self.taps = psf_rows.shape[1]
        self.tile_rows = self.height // TILE
        self.wide = self.width + LANES
        self.groups = self.height // SPAN
        self.part = min(self.rows, SPAN)
        self.mask_rows = up_to(self.epochs, HALO)
        self.scene_at = SPAN * self.local
        self.mask_at = self.scene_at + self.part
        self.buffer_rows = self.mask_at + self.mask_rows
        self.blocks = self.height // self.rows
        self.tap_rows = self.mask_rows


def cover_at(coverage_ref, epoch, row_tile, col_tile):
    last_row = coverage_ref.shape[0] - 1
    last_col = coverage_ref.shape[1] - 1
    inside = (row_tile >= 0) & (row_tile <= last_row) & (col_tile >= 0) & (col_tile <= last_col)
    value = coverage_ref[jnp.clip(row_tile, 0, last_row), jnp.clip(col_tile, 0, last_col), epoch]
    return jnp.where(inside, value, 0).astype(F32)


def tile_of(position):
    return (position + TILE) // TILE - 1


def low(index, size):
    return index & (size - 1)


def high(index, size):
    return lax.shift_right_logical(index, size.bit_length() - 1)


def packing(count, width, shift):
    row, lane = iota((LANES * count, LANES), 0), iota((LANES * count, LANES), 1)
    here = high(lane, width) == high(row, LANES)
    here &= low(row, LANES) == low(lane, width) + shift
    return here.astype(F32).astype(BF16)


def side_by_side(ref, count, rows):
    return jnp.concatenate([ref[g * rows : (g + 1) * rows] for g in range(count)], axis=1)


def edge_copies(sz, images_ref, scene_ref, edge, sides, sem, side_sem):
    places = (0, sz.width - LANES)
    copies = []
    for e in range(sz.local):
        for side in range(2):
            slot = 2 * e + side
            copies.append(
                pltpu.make_async_copy(
                    images_ref.at[e, :, pl.ds(places[side], LANES)], edge.at[slot], sem.at[slot]
                )
            )
    side_copies = [
        pltpu.make_async_copy(
            scene_ref.at[:, pl.ds(places[side], LANES)], sides.at[side], side_sem.at[side]
        )
        for side in range(2)
    ]
    return copies, side_copies


def pack_edges(sz, flags, edge, sides, copies, side_copies, first_ref, second_ref):
    epoch = lax.axis_index("epoch") * sz.local
    even = lax.axis_index("sky") % 2 == 0
    places = (0, sz.width - LANES)

    def put(left, right, rows):
        first_ref[rows] = jnp.where(even, right, left).astype(BF16)
        second_ref[rows] = jnp.where(even, left, right).astype(BF16)

    packs = [packing(sz.groups, HALO, shift) for shift in (0, LANES - HALO)]
    row, lane = iota((LANES, LANES), 0), iota((LANES, LANES), 1)
    repeats = [
        (row == low(lane, HALO) + shift).astype(F32).astype(BF16) for shift in (0, LANES - HALO)
    ]
    for copy in copies + side_copies:
        copy.wait()
    goods, rows_good = [], []
    for side in range(2):
        good = flags[:, places[side] : places[side] + LANES].astype(F32)
        rows_good.append(good)
        if side == 1:
            good = pltpu.roll(good, HALO, 1)
        if sz.mask_rows > sz.epochs:
            good = jnp.concatenate(
                [good, jnp.zeros((sz.mask_rows - sz.epochs, LANES), F32)], axis=0
            )
        goods.append(good)
    put(goods[0], goods[1], slice(sz.mask_at, sz.buffer_rows))
    for e in range(sz.local):
        lines = []
        for side in range(2):
            slot = 2 * e + side
            good = jnp.broadcast_to(row_of(rows_good[side], epoch + e), (HALO, LANES))
            good = dot(good.astype(BF16), repeats[side])[0:1]
            lines.append(dot(side_by_side(edge.at[slot], sz.groups, SPAN), packs[side]) * good)
        put(lines[0], lines[1], slice(SPAN * e, SPAN * (e + 1)))
    cells = []
    count = sz.rows // sz.part
    for side, shift in enumerate((0, LANES - RIM)):
        cells.append(
            dot(side_by_side(sides.at[side], count, sz.part), packing(count, RIM, shift))
        )
    put(cells[0], cells[1], slice(sz.scene_at, sz.mask_at))


def edges_kernel(sz, images_ref, scene_ref, mask_ref, first_ref, second_ref, *scratch):
    edge, sides, flags, sem, side_sem, flag_sem = scratch
    copies, side_copies = edge_copies(sz, images_ref, scene_ref, edge, sides, sem, side_sem)
    flag_copy = pltpu.make_async_copy(mask_ref, flags, flag_sem)
    for copy in [flag_copy] + copies + side_copies:
        copy.start()
    flag_copy.wait()
    pack_edges(sz, flags, edge, sides, copies, side_copies, first_ref, second_ref)


def edges(sz, images, scene, mask):
    shape = jax.ShapeDtypeStruct((sz.buffer_rows, LANES), BF16)
    return pl.pallas_call(
        functools.partial(edges_kernel, sz),
        out_shape=(shape, shape),
        in_specs=[HBM, HBM, HBM],
        out_specs=(VMEM, VMEM),
        scratch_shapes=[
            pltpu.VMEM((2 * sz.local, sz.height, LANES), BF16),
            pltpu.VMEM((2, sz.rows, LANES), BF16),
            pltpu.VMEM((sz.epochs, sz.width), jnp.int32),
            pltpu.SemaphoreType.DMA((2 * sz.local,)),
            pltpu.SemaphoreType.DMA((2,)),
            pltpu.SemaphoreType.DMA,
        ],
        compiler_params=WHOLE,
        cost_estimate=SHORT,
        name="edges",
    )(images, scene, mask)


def sides_of(first, second):
    even = lax.axis_index("sky") % 2 == 0
    return jnp.where(even, second, first), jnp.where(even, first, second)


def widen_rows(sz, scene_ref, first_ref, second_ref, start, count):
    group, inside = start // sz.part, start % sz.part
    cells = slice(sz.scene_at + inside, sz.scene_at + inside + count)
    row, lane = iota((LANES, sz.wide), 0), iota((LANES, sz.wide), 1)
    wide = dot(scene_ref[start : start + count], selection(sz.width, sz.wide, RIM))
    ends = sides_of(first_ref[cells], second_ref[cells])
    for end, at in zip(ends, (0, sz.width + RIM)):
        place = (high(row, RIM) == group) & (lane == low(row, RIM) + at)
        wide += dot(end, place.astype(F32).astype(BF16))
    return wide.astype(BF16)


def widen_kernel(sz, scene_ref, mask_ref, first_ref, second_ref, wide_ref, good_ref):
    for start in range(0, sz.rows, sz.part):
        wide_ref[start : start + sz.part] = widen_rows(
            sz, scene_ref, first_ref, second_ref, start, sz.part
        )
    flags = slice(sz.mask_at, sz.buffer_rows)
    before, after = sides_of(first_ref[flags], second_ref[flags])
    own = mask_ref[...].astype(F32)
    if sz.mask_rows > sz.epochs:
        own = jnp.concatenate(
            [own, jnp.zeros((sz.mask_rows - sz.epochs, sz.width), F32)], axis=0
        )
    good = dot(own.astype(BF16), selection(sz.width, sz.wide, HALO))
    inner = iota((LANES, sz.wide), 0) < HALO
    zero = jnp.zeros((LANES, sz.wide), BF16)
    good += dot(before, jnp.where(inner, selection(LANES, sz.wide, 0), zero))
    good += dot(after, jnp.where(inner, selection(LANES, sz.wide, sz.width + HALO), zero))
    good_ref[...] = good


def destination(slot, place):
    return (
        3 * (1 - place % 2),
        2 - place // 2,
        (2 * place + 1) % 5,
        place,
    )[slot]


def rim_rows(sz, epoch, e, coverage_ref, row_line, row_shift, twice, first_ref, second_ref):
    rows = slice(SPAN * e, SPAN * (e + 1))
    column = lax.axis_index("sky") * sz.width
    both = jnp.concatenate(sides_of(first_ref[rows], second_ref[rows]), axis=1)
    lane = iota((1, 2 * LANES), 1)
    factor = jnp.zeros((1, 2 * LANES), F32)
    for side, at in enumerate((column - HALO, column + sz.width)):
        for tile in range(sz.tile_rows):
            cover = cover_at(coverage_ref, epoch, tile, tile_of(at))
            here = high(lane, LANES) == side
            here &= high(low(lane, LANES), HALO * TILE // SPAN) == tile
            factor = jnp.where(here, cover, factor)
    both = both.astype(F32) * factor
    above = pltpu.roll(both[SPAN - HALO :], HALO, 1)
    below = pltpu.roll(both[:HALO], 2 * LANES - HALO, 1)
    above = jnp.where(low(lane, LANES) < HALO, 0.0, above)
    below = jnp.where(low(lane, LANES) >= HALO * (sz.groups - 1), 0.0, below)
    window = jnp.concatenate([above, both, below], axis=0).astype(BF16)
    table = toeplitz(row_line, row_shift - 4, SPAN, SPAN + LANES)[:, : SPAN + RIM]
    return (dot(table, window) * twice).astype(BF16)


def rim_columns(col_line, col_shift):
    enter = toeplitz(col_line, 28 - col_shift, HALO, SPAN)[:, :LANES]
    leave = toeplitz(col_line, SPAN + LANES - 116 - col_shift, HALO, SPAN + LANES)[:, :LANES]
    none = jnp.zeros((HALO, LANES), BF16)
    upper = [jnp.concatenate([enter, none], axis=1)] * (LANES // HALO)
    lower = [jnp.concatenate([none, leave], axis=1)] * (LANES // HALO)
    return jnp.concatenate(upper + lower, axis=0)


def rim_part(sz, start, rim_ref, table):
    group = start // SPAN
    row = iota((2 * LANES, SPAN), 0)
    parts = []
    for k in range(max(sz.rows // SPAN, 1)):
        picked = jnp.where(high(low(row, LANES), HALO) == group + k, table, jnp.zeros_like(table))
        if sz.rows >= SPAN:
            rows = rim_ref[...]
        else:
            rows = rim_ref[pl.ds(pl.multiple_of(start - group * SPAN, sz.rows), sz.rows)]
        parts.append(dot(rows, picked))
    return jnp.concatenate(parts, axis=0) if len(parts) > 1 else parts[0]


def rim_places(sz, h):
    row, lane = iota((SPAN, LANES), 0), iota((SPAN, LANES), 1)
    here = (lane == row + RIM * h) & (row < HALO)
    here |= (lane == row - SPAN + RIM * (h + 1)) & (row >= SPAN - HALO)
    return here.astype(F32).astype(BF16)


def rim_spread(sz, h):
    row, lane = iota((LANES, SPAN), 0), iota((LANES, SPAN), 1)
    here = (row == lane + RIM * h) & (lane < HALO)
    here |= (row == lane - SPAN + RIM * (h + 1)) & (lane >= SPAN - HALO)
    return here.astype(F32).astype(BF16)


def pack_rows(sz, ref, at, rim):
    ref[at : at + RIM] = rim[:, : sz.width]
    left = slice(at + RIM, at + RIM + HALO)
    ref[left, :LANES] = rim[:HALO, sz.width :]
    ref[left, LANES:SPAN] = rim[HALO:, sz.width :]
    ref[left, SPAN:] = jnp.zeros((HALO, sz.width - SPAN), BF16)


def pack_part(sz, ref, at, part):
    total = None
    for h in range(sz.rows // LANES):
        rows = part[h * LANES : (h + 1) * LANES].astype(BF16)
        moved = dot(rows, rim_places(sz, h))
        total = moved if total is None else total + moved
    total = total.astype(BF16)
    for k in range(LANES // RIM):
        ref[at : at + RIM, k * LANES : (k + 1) * LANES] = total[k * RIM : (k + 1) * RIM]


def unpack_rim(sz, ref, at):
    left = slice(at + RIM, at + RIM + HALO)
    rest = jnp.concatenate([ref[left, :LANES], ref[left, LANES:SPAN]], axis=0)
    return jnp.concatenate([ref[at : at + RIM], rest], axis=1)


def unpack_part(sz, ref, at):
    pieces = [ref[at : at + RIM, k * LANES : (k + 1) * LANES] for k in range(LANES // RIM)]
    packed = jnp.concatenate(pieces, axis=0)
    parts = [dot(packed, rim_spread(sz, h)) for h in range(sz.rows // LANES)]
    return jnp.concatenate(parts, axis=0)


def complete(sz, out, part):
    rows = slice(0, sz.rows)
    for at, cols in ((0, slice(0, LANES)), (LANES, slice(sz.width - LANES, sz.width))):
        value = out[rows, cols].astype(F32) + part[:, at : at + LANES]
        out[rows, cols] = value.astype(BF16)


def rim_parts_of(sz, slots, place, offsets_ref, col_lines, rim_ref):
    tables = []
    for e in range(sz.local):
        epoch = place * sz.local + e
        tables.append(rim_columns(row_of(col_lines[0], epoch), offsets_ref[1, epoch]))
    parts = []
    for slot in slots:
        part = None
        for e in range(sz.local):
            term = rim_part(sz, destination(slot, place) * sz.rows, rim_ref.at[e], tables[e])
            part = term if part is None else part + term
        parts.append(part)
    return parts


def notes_kernel(
    sz, coverage_ref, offsets_ref, weight_ref, scene_ref, first_ref, second_ref,
    psf_rows_ref, psf_cols_ref, far_out, rim_ref, part_out, row_lines, col_lines,
):
    place = lax.axis_index("epoch")
    outer = (place == 0) | (place == 3)
    load_taps(psf_rows_ref, row_lines, sz.epochs, sz.taps)
    load_taps(psf_cols_ref, col_lines, sz.epochs, sz.taps)
    for e in range(sz.local):
        epoch = place * sz.local + e
        rim_ref[e] = rim_rows(
            sz, epoch, e, coverage_ref, row_of(row_lines[1], epoch), offsets_ref[0, epoch],
            -2.0 * weight_ref[epoch], first_ref, second_ref,
        )
    parts = rim_parts_of(sz, (0, 1), place, offsets_ref, col_lines, rim_ref)
    top = widen_rows(sz, scene_ref, first_ref, second_ref, 0, RIM)
    bottom = widen_rows(sz, scene_ref, first_ref, second_ref, sz.rows - RIM, RIM)
    pack_rows(sz, far_out, 0, jnp.where(place < 2, bottom, top))
    pack_part(sz, far_out, RIM + HALO, jnp.where(outer, parts[0], parts[1]))
    part_out[...] = parts[1].astype(BF16)


def notes(sz, coverage, offsets, weight, scene, first, second, psf_rows, psf_cols):
    return pl.pallas_call(
        functools.partial(notes_kernel, sz),
        out_shape=(
            jax.ShapeDtypeStruct((2 * RIM + HALO, sz.width), BF16),
            jax.ShapeDtypeStruct((sz.local, SPAN, 2 * LANES), BF16),
            jax.ShapeDtypeStruct((sz.rows, SPAN), BF16),
        ),
        in_specs=[SMEM] * 3 + [VMEM] * 5,
        out_specs=(VMEM, VMEM, VMEM),
        scratch_shapes=[pltpu.VMEM((2, sz.tap_rows, LANES), F32)] * 2,
        compiler_params=PARAMS,
        cost_estimate=SHORT,
        name="notes",
    )(coverage, offsets, weight, scene, first, second, psf_rows, psf_cols)


def early_kernel(
    sz, offsets_ref, scene_ref, first_ref, second_ref, psf_cols_ref, rim_ref, three_ref,
    near_out, col_lines,
):
    place = lax.axis_index("epoch")
    load_taps(psf_cols_ref, col_lines, sz.epochs, sz.taps)
    (part,) = rim_parts_of(sz, (2,), place, offsets_ref, col_lines, rim_ref)
    top = widen_rows(sz, scene_ref, first_ref, second_ref, 0, RIM)
    bottom = widen_rows(sz, scene_ref, first_ref, second_ref, sz.rows - RIM, RIM)
    pack_rows(sz, near_out, sz.rows, jnp.where(place % 2 == 0, bottom, top))
    near_out[: sz.rows] = three_ref[...]
    complete(sz, near_out, part)


def early(sz, offsets, scene, first, second, psf_cols, rim, three):
    return pl.pallas_call(
        functools.partial(early_kernel, sz),
        out_shape=jax.ShapeDtypeStruct((sz.rows + RIM + HALO, sz.width), BF16),
        in_specs=[SMEM] + [VMEM] * 6,
        out_specs=VMEM,
        scratch_shapes=[pltpu.VMEM((2, sz.tap_rows, LANES), F32)],
        compiler_params=PARAMS,
        cost_estimate=SHORT,
        name="early",
    )(offsets, scene, first, second, psf_cols, rim, three)


def merge_kernel(sz, two_ref, near_ref, one_ref, part_ref, out_ref):
    place = lax.axis_index("epoch")
    outer = (place == 0) | (place == 3)

    @pl.when(outer)
    def _():
        out_ref[...] = two_ref[...]
        complete(sz, out_ref, part_ref[...].astype(F32))

    @pl.when(jnp.logical_not(outer))
    def _():
        total = near_ref[: sz.rows].astype(F32) + one_ref[...].astype(F32)
        out_ref[...] = total.astype(BF16)


def merge(sz, two, near, one, part):
    return pl.pallas_call(
        functools.partial(merge_kernel, sz),
        out_shape=jax.ShapeDtypeStruct((sz.rows, sz.width), BF16),
        in_specs=[VMEM] * 4,
        out_specs=VMEM,
        compiler_params=PARAMS,
        cost_estimate=SHORT,
        name="merge",
    )(two, near, one, part)


def finish_kernel(sz, offsets_ref, scene_ref, mask_ref, first_ref, second_ref, *more):
    if sz.blocks != 4:
        widen_kernel(sz, scene_ref, mask_ref, first_ref, second_ref, *more)
        return
    psf_cols_ref, rim_ref, own_ref, wide_ref, good_ref, back_out, own_out, col_lines, sem = more
    place = lax.axis_index("epoch")
    copy = pltpu.make_async_copy(own_ref, own_out, sem)
    copy.start()
    load_taps(psf_cols_ref, col_lines, sz.epochs, sz.taps)
    parts = rim_parts_of(sz, (0, 3), place, offsets_ref, col_lines, rim_ref)
    widen_kernel(sz, scene_ref, mask_ref, first_ref, second_ref, wide_ref, good_ref)
    top, bottom = wide_ref[:RIM], wide_ref[sz.rows - RIM :]
    pack_rows(sz, back_out, 0, jnp.where(place % 2 == 0, bottom, top))
    pack_part(sz, back_out, RIM + HALO, parts[0])
    copy.wait()
    complete(sz, own_out, parts[1])


def finish(sz, offsets, scene, mask, first, second, *more):
    full = jax.ShapeDtypeStruct((sz.rows, sz.width), BF16)
    shapes = [
        jax.ShapeDtypeStruct((sz.rows, sz.wide), BF16),
        jax.ShapeDtypeStruct((sz.mask_rows, sz.wide), F32),
    ]
    scratch = []
    if more:
        shapes += [jax.ShapeDtypeStruct((2 * RIM + HALO, sz.width), BF16), full]
        scratch = [pltpu.VMEM((2, sz.tap_rows, LANES), F32), pltpu.SemaphoreType.DMA]
    return pl.pallas_call(
        functools.partial(finish_kernel, sz),
        out_shape=tuple(shapes),
        in_specs=[SMEM] + [VMEM] * 4 + [VMEM, VMEM, HBM][: len(more)],
        out_specs=tuple([VMEM] * len(shapes)),
        scratch_shapes=scratch,
        compiler_params=PARAMS,
        cost_estimate=SHORT,
        name="finish",
    )(offsets, scene, mask, first, second, *more)


def image_kernel(sz, slots, rims, packs, images_ref, *more):
    count = 1 if slots is None else len(slots)
    small, ends, more = more[:6], more[6 : 6 + rims], more[6 + rims :]
    if packs:
        scene_ref, *more = more
    outs, more = more[:count], more[count:]
    if packs:
        first_out, second_out, edge, sides, edge_sem, side_sem, *more = more
    held, small_sem, more = more[:6], more[6], more[7:]
    coverage_ref, offsets_ref, weight_ref, mask_ref, psf_rows_ref, psf_cols_ref = held
    window, row_done, row_lines, col_lines, row_table, main_table, cross_table, rim_ref, sem = more
    place = lax.axis_index("epoch")
    first = place * sz.local
    column = lax.axis_index("sky") * sz.width
    if slots is None:
        targets = [pl.program_id(0)]
    else:
        targets = [destination(slot, place) for slot in slots]

    copies = []
    for i, target in enumerate(targets):
        start = target * sz.rows
        head = jnp.maximum(start - HALO, 0)
        foot = jnp.minimum(start + sz.rows, sz.height - HALO)
        for e in range(sz.local):
            for n, (source, at, length) in enumerate(
                ((start, HALO, sz.rows), (head, 0, HALO), (foot, HALO + sz.rows, HALO))
            ):
                copies.append(
                    pltpu.make_async_copy(
                        images_ref.at[e, pl.ds(pl.multiple_of(source, HALO), length), :],
                        window.at[i, e, pl.ds(at, length), :],
                        sem.at[i, e, n],
                    )
                )
    held_copies = [
        pltpu.make_async_copy(source, target, small_sem.at[n])
        for n, (source, target) in enumerate(zip(small, held))
    ]
    for copy in held_copies + copies:
        copy.start()
    if packs:
        edge_waits = edge_copies(sz, images_ref, scene_ref, edge, sides, edge_sem, side_sem)
        for copy in edge_waits[0] + edge_waits[1]:
            copy.start()
    for copy in held_copies:
        copy.wait()
    load_taps(psf_rows_ref, row_lines, sz.epochs, sz.taps)
    load_taps(psf_cols_ref, col_lines, sz.epochs, sz.taps)
    for e in range(sz.local):
        epoch = first + e
        row_shift, col_shift = offsets_ref[0, epoch], offsets_ref[1, epoch]
        row_table[e] = toeplitz(row_of(row_lines[1], epoch), row_shift - 4, STEP, SPAN)
        line = row_of(col_lines[0], epoch)
        main = toeplitz(line, 12 - col_shift, SPAN, SPAN + LANES)[:, :SPAN]
        main_table[e] = main
        apart = (iota((SPAN, SPAN), 0) < LANES) != (iota((SPAN, SPAN), 1) < LANES)
        cross_table[e] = jnp.where(apart, main, jnp.zeros_like(main))
    rim_parts = []
    for e in range(sz.local if rims else 0):
        epoch = first + e
        rim_ref[e] = rim_rows(
            sz, epoch, e, coverage_ref, row_of(row_lines[1], epoch), offsets_ref[0, epoch],
            -2.0 * weight_ref[epoch], *ends,
        )
        table = rim_columns(row_of(col_lines[0], epoch), offsets_ref[1, epoch])
        for i, target in enumerate(targets):
            part = rim_part(sz, target * sz.rows, rim_ref.at[e], table)
            if e == 0:
                rim_parts.append(part)
            else:
                rim_parts[i] += part
    column_tile = column // TILE
    for i, target in enumerate(targets):
        for copy in copies[3 * sz.local * i : 3 * sz.local * (i + 1)]:
            copy.wait()
        start = target * sz.rows
        zones = (
            (0, HALO, tile_of(start - HALO)),
            (HALO, HALO + sz.rows, tile_of(start)),
            (HALO + sz.rows, RIM + sz.rows, tile_of(start + sz.rows)),
        )
        for e in range(sz.local):
            epoch = first + e
            good = row_of(mask_ref[...].astype(F32), epoch)
            for begin, end, tile in zones:
                factor = good * cover_at(coverage_ref, epoch, tile, column_tile)
                window[i, e, begin:end] = window[i, e, begin:end] * factor.astype(BF16)
            twice = -2.0 * weight_ref[epoch]
            for s, n in spans(sz.rows):
                part = dot(row_table[e, :n, : n + RIM], window[i, e, s : s + n + RIM])
                row_done[i, e, s : s + n] = (part * twice).astype(BF16)
    for i in range(count):
        total = []
        for b in range(0, sz.width, SPAN):
            out = None
            for e in range(sz.local):
                part = dot(row_done[i, e, :, b : b + SPAN], main_table[e])
                out = part if out is None else out + part
            total += [out[:, :LANES], out[:, LANES:]]
        for b in range(LANES, sz.width - LANES, SPAN):
            out = None
            for e in range(sz.local):
                part = dot(row_done[i, e, :, b : b + SPAN], cross_table[e])
                out = part if out is None else out + part
            total[b // LANES] += out[:, :LANES]
            total[b // LANES + 1] += out[:, LANES:]
        if rims:
            total[0] += rim_parts[i][:, :LANES]
            total[-1] += rim_parts[i][:, LANES:]
        for k, piece in enumerate(total):
            outs[i][:, k * LANES : (k + 1) * LANES] = piece.astype(BF16)
    if packs:
        pack_edges(sz, mask_ref, edge, sides, *edge_waits, first_out, second_out)


def image_blocks(
    sz, slots, coverage, offsets, weight, images, mask, psf_rows, psf_cols, *ends, scene=None
):
    packs = scene is not None
    if slots is None:
        count = 1
        grid = dict(
            grid=(sz.blocks,),
            out_shape=jax.ShapeDtypeStruct((sz.blocks * sz.rows, sz.width), BF16),
            out_specs=pl.BlockSpec((sz.rows, sz.width), lambda i: (i, 0)),
        )
    else:
        count = len(slots)
        shapes = [jax.ShapeDtypeStruct((sz.rows, sz.width), BF16)] * count
        if packs:
            shapes += [jax.ShapeDtypeStruct((sz.buffer_rows, LANES), BF16)] * 2
        grid = dict(out_shape=tuple(shapes), out_specs=tuple([VMEM] * len(shapes)))
    pack_scratch = [
        pltpu.VMEM((2 * sz.local, sz.height, LANES), BF16),
        pltpu.VMEM((2, sz.rows, LANES), BF16),
        pltpu.SemaphoreType.DMA((2 * sz.local,)),
        pltpu.SemaphoreType.DMA((2,)),
    ]
    return pl.pallas_call(
        functools.partial(image_kernel, sz, slots, len(ends), packs),
        in_specs=[HBM] * 7 + [VMEM] * len(ends) + [HBM] * packs,
        scratch_shapes=pack_scratch * packs
        + [
            pltpu.SMEM(coverage.shape, jnp.int32),
            pltpu.SMEM(offsets.shape, jnp.int32),
            pltpu.SMEM(weight.shape, F32),
            pltpu.VMEM(mask.shape, jnp.int32),
            pltpu.VMEM(psf_rows.shape, BF16),
            pltpu.VMEM(psf_cols.shape, BF16),
            pltpu.SemaphoreType.DMA((6,)),
            pltpu.VMEM((count, sz.local, sz.rows + RIM, sz.width), BF16),
            pltpu.VMEM((count, sz.local, sz.rows, sz.width), BF16),
            pltpu.VMEM((2, sz.tap_rows, LANES), F32),
            pltpu.VMEM((2, sz.tap_rows, LANES), F32),
            pltpu.VMEM((sz.local, STEP, SPAN), BF16),
            pltpu.VMEM((sz.local, SPAN, SPAN), BF16),
            pltpu.VMEM((sz.local, SPAN, SPAN), BF16),
            pltpu.VMEM((sz.local, SPAN, 2 * LANES), BF16),
            pltpu.SemaphoreType.DMA((count, sz.local, 3)),
        ],
        compiler_params=WHOLE if slots is not None and 0 in slots else PARAMS,
        cost_estimate=SHORT,
        name="image_blocks",
        **grid,
    )(images, coverage, offsets, weight, mask, psf_rows, psf_cols, *ends, *([scene] * packs))


def column_tables(taps, start):
    pair = toeplitz(taps, start, LANES, SPAN)
    here, past = pair[:, :LANES], pair[:, LANES:]
    none = jnp.zeros_like(here)
    main = jnp.concatenate(
        [jnp.concatenate([here, none], axis=1), jnp.concatenate([past, here], axis=1)], axis=0
    )
    rest = jnp.concatenate(
        [jnp.concatenate([past, none], axis=1), jnp.concatenate([none, past], axis=1)], axis=0
    )
    return main, rest, here, past


def column_pass(sz, source, tables, tail):
    main, rest, here, past = tables
    tiles = []
    for b in range(0, sz.width, SPAN):
        out = dot(source[:, b : b + SPAN], main)
        tiles += [out[:, :LANES], out[:, LANES:]]
    ends = list(range(SPAN, sz.wide, SPAN))
    if len(ends) == 2:
        joined = jnp.concatenate([source[:, at : at + LANES] for at in ends], axis=1)
        out = dot(joined, rest)
        parts = [out[:, :LANES], out[:, LANES:]]
    else:
        parts = [dot(source[:, at : at + LANES], past) for at in ends]
    for at, part in zip(ends, parts):
        tiles[at // LANES - 1] += part
    if tail:
        tiles.append(dot(source[:, sz.width : sz.wide], here))
    return tiles


def model_kernel(
    sz, batch, coverage_ref, offsets_ref, weight_ref,
    wide_ref, good_ref, psf_rows_ref, psf_cols_ref, *more,
):
    *extra, out_ref, scene, lifted, residual, pulled, row_lines, col_lines = more
    step = pl.program_id(0)
    place = lax.axis_index("epoch")
    start = place * sz.rows
    column = lax.axis_index("sky") * sz.width

    @pl.when(step == 0)
    def _():
        load_taps(psf_rows_ref, row_lines, sz.epochs, sz.taps)
        load_taps(psf_cols_ref, col_lines, sz.epochs, sz.taps)
        scene[RIM : RIM + sz.rows] = wide_ref[...]
        if sz.blocks != 4:
            head_ref, foot_ref, base_ref = extra
            scene[0:RIM] = head_ref[...]
            scene[RIM + sz.rows :] = foot_ref[...]
            out_ref[...] = base_ref[...]
        else:
            own_ref, one_ref, two_ref, three_ref, back_ref, far_ref = extra
            outer = (place == 0) | (place == 3)
            near = jnp.where(
                outer, unpack_rim(sz, back_ref, 0), unpack_rim(sz, three_ref, sz.rows)
            )
            far = unpack_rim(sz, far_ref, 0)
            none = jnp.zeros_like(near)
            odd = place % 2 == 1
            scene[0:RIM] = jnp.where(odd, near, jnp.where(outer, none, far))
            scene[RIM + sz.rows :] = jnp.where(odd, jnp.where(outer, none, far), near)
            rows = slice(RIM + HALO, 2 * RIM + HALO)
            fix = unpack_part(sz, back_ref[rows], 0) + unpack_part(sz, far_ref[rows], 0)
            for b in range(0, sz.width, LANES):
                cols = slice(b, b + LANES)
                inner = two_ref[:, cols].astype(F32) + three_ref[: sz.rows, cols].astype(F32)
                base = jnp.where(outer, one_ref[:, cols].astype(F32), inner)
                base += own_ref[:, cols].astype(F32)
                for at, side in ((0, 0), (LANES, sz.width - LANES)):
                    if b == side:
                        base += fix[:, at : at + LANES]
                out_ref[:, cols] = base

    epochs = [step * batch + n for n in range(batch)]
    edge = sz.rows + HALO
    for n, epoch in enumerate(epochs):
        row_in = toeplitz(row_of(row_lines[0], epoch), -4 - offsets_ref[0, epoch], STEP, SPAN)
        for s, count in spans(sz.rows + RIM):
            lifted[n, s : s + count] = dot(
                row_in[:count, : count + RIM], scene[s : s + count + RIM]
            ).astype(BF16)
    for n, epoch in enumerate(epochs):
        good = row_of(good_ref[...], epoch) * (2.0 * weight_ref[epoch])
        lane = iota((1, sz.wide), 1)
        factors = []
        for row_tile in (tile_of(start - HALO), tile_of(start), tile_of(start + sz.rows)):
            left, here, right = (
                cover_at(coverage_ref, epoch, row_tile, tile_of(c))
                for c in (column - HALO, column, column + sz.width)
            )
            factors.append(
                good * jnp.where(lane < HALO, left, jnp.where(lane < HALO + sz.width, here, right))
            )
        tables = column_tables(row_of(col_lines[1], epoch), 28 + offsets_ref[1, epoch])
        for k, modeled in enumerate(column_pass(sz, lifted[n], tables, True)):
            b = k * LANES
            head, mid, foot = (f[:, b : b + LANES] for f in factors)
            residual[n, 0:HALO, b : b + LANES] = (modeled[0:HALO] * head).astype(BF16)
            residual[n, HALO:edge, b : b + LANES] = (modeled[HALO:edge] * mid).astype(BF16)
            residual[n, edge:, b : b + LANES] = (modeled[edge:] * foot).astype(BF16)
    for n, epoch in enumerate(epochs):
        tables = column_tables(row_of(col_lines[0], epoch), 28 - offsets_ref[1, epoch])
        for k, tile in enumerate(column_pass(sz, residual[n], tables, False)):
            pulled[n, :, k * LANES : (k + 1) * LANES] = tile.astype(BF16)
    row_outs = [
        toeplitz(row_of(row_lines[1], epoch), offsets_ref[0, epoch] - 4, STEP, SPAN)
        for epoch in epochs
    ]
    for s, count in spans(sz.rows):
        total = out_ref[s : s + count]
        for n in range(batch):
            total += dot(row_outs[n][:count, : count + RIM], pulled[n, s : s + count + RIM])
        out_ref[s : s + count] = total


def model_term(sz, coverage, offsets, weight, wide, good, psf_rows, psf_cols, *extra):
    high = sz.rows + RIM
    batch = 4 if sz.epochs % 4 == 0 else 1
    return pl.pallas_call(
        functools.partial(model_kernel, sz, batch),
        grid=(sz.epochs // batch,),
        out_shape=jax.ShapeDtypeStruct((sz.rows, sz.width), F32),
        in_specs=[SMEM] * 3 + [VMEM] * (4 + len(extra)),
        out_specs=VMEM,
        scratch_shapes=[
            pltpu.VMEM((sz.rows + 2 * RIM, sz.wide), BF16),
            pltpu.VMEM((batch, high, sz.wide), BF16),
            pltpu.VMEM((batch, high, sz.wide), BF16),
            pltpu.VMEM((batch, high, sz.width), BF16),
            pltpu.VMEM((2, sz.tap_rows, LANES), F32),
            pltpu.VMEM((2, sz.tap_rows, LANES), F32),
        ],
        compiler_params=PARAMS,
        cost_estimate=SHORT,
        name="model_term",
    )(coverage, offsets, weight, wide, good, psf_rows, psf_cols, *extra)


def on_device(sky_scene, images, psf_rows, psf_cols, offsets, epoch_weight, column_mask, coverage):
    sz = Sizes(images, sky_scene, psf_rows)
    peers = lax.axis_size("sky")
    depth = lax.axis_size("epoch")
    scalars = (jnp.transpose(coverage, (1, 2, 0)), offsets.T, epoch_weight)
    profiles = (psf_rows, psf_cols)

    def pairs(start, count):
        return [p for i in range(start, count - 1, 2) for p in ((i, i + 1), (i + 1, i))]

    def blocks(slots, shifts, *ends, scene=None):
        return image_blocks(
            sz, slots, scalars[0], shifts, epoch_weight, images, column_mask, *profiles, *ends,
            scene=scene,
        )

    if depth == 4:
        one, two, first, second = blocks((0, 1), scalars[1], scene=sky_scene)
        got_one = lax.ppermute(one, "epoch", pairs(0, depth))
        got_two = lax.ppermute(two, "epoch", pairs(1, depth))
        shifts, one = lax.optimization_barrier((scalars[1], one))
        three, own = blocks((2, 3), shifts)
        first = lax.ppermute(first, "sky", pairs(0, peers))
        second = lax.ppermute(second, "sky", pairs(1, peers))
        second, three = lax.optimization_barrier((second, three))
        far, rim, part = notes(sz, *scalars, sky_scene, first, second, *profiles)
        near = early(sz, scalars[1], sky_scene, first, second, psf_cols, rim, three)
        got_three = lax.ppermute(near, "epoch", [(0, 1), (3, 2)])
        got_far = lax.ppermute(far, "epoch", [(0, 3), (3, 0), (1, 2), (2, 1)])
        passed = merge(sz, two, near, got_one, part)
        passed, got_far, got_two, rim = lax.optimization_barrier((passed, got_far, got_two, rim))
        got_passed = lax.ppermute(passed, "epoch", [(0, 2), (3, 1), (1, 3), (2, 0)])
        wide, good, back, own = finish(
            sz, scalars[1], sky_scene, column_mask, first, second, psf_cols, rim, own
        )
        got_back = lax.ppermute(back, "epoch", [(1, 0), (2, 3)])
        model = model_term(
            sz, *scalars, wide, good, *profiles,
            own, got_one, got_two, got_three, got_back, got_far,
        )
        return model + got_passed.astype(F32)

    first, second = edges(sz, images, sky_scene, column_mask)
    first = lax.ppermute(first, "sky", pairs(0, peers))
    second = lax.ppermute(second, "sky", pairs(1, peers))
    downward = [(i, i + 1) for i in range(depth - 1)]
    upward = [(i + 1, i) for i in range(depth - 1)]
    wide, good = finish(sz, scalars[1], sky_scene, column_mask, first, second)
    head = lax.ppermute(wide[-RIM:], "epoch", downward)
    foot = lax.ppermute(wide[:RIM], "epoch", upward)
    terms = blocks(None, scalars[1], first, second).astype(F32)
    base = lax.psum_scatter(terms, "epoch", scatter_dimension=0, tiled=True)
    return model_term(sz, *scalars, wide, good, *profiles, head, foot, base)


def solution(mesh):
    return jax.shard_map(
        on_device,
        mesh=mesh,
        in_specs=(
            P(("field", "epoch"), "sky"),
            P(("field", "epoch"), None, "sky"),
            P("field", None),
            P("field", None),
            P("field", None),
            P("field"),
            P("field", "sky"),
            P("field", None, None),
        ),
        out_specs=P(("field", "epoch"), "sky"),
        check_vma=False,
    )
```

```python
import functools

import jax
import jax.numpy as jnp
from jax import lax
from jax.experimental import pallas as pl
from jax.experimental.pallas import tpu as pltpu
from jax.sharding import PartitionSpec as P

TILE = 512
HALO = 16
RIM = 2 * HALO
LANES = 128
SPAN = 256
STEP = SPAN - RIM
F32 = jnp.float32
BF16 = jnp.bfloat16
VMEM = pl.BlockSpec(memory_space=pltpu.VMEM)
SMEM = pl.BlockSpec(memory_space=pltpu.SMEM)
HBM = pl.BlockSpec(memory_space=pltpu.HBM)
PARAMS = pltpu.CompilerParams(vmem_limit_bytes=40 * 1024 * 1024)
SHORT = pl.CostEstimate(flops=1000, bytes_accessed=1000, transcendentals=0)
WHOLE = pltpu.CompilerParams(vmem_limit_bytes=59 * 1024 * 1024)


def up_to(value, unit):
    return -(-value // unit) * unit


def dot(a, b, dims=((1,), (0,))):
    return lax.dot_general(a, b, (dims, ((), ())), preferred_element_type=F32)


def iota(shape, dim):
    return lax.broadcasted_iota(jnp.int32, shape, dim)


def selection(rows, cols, shift):
    return (iota((rows, cols), 1) == iota((rows, cols), 0) + shift).astype(BF16)


def toeplitz(taps, start, rows, width):
    line = jnp.concatenate([taps, jnp.zeros((1, width - LANES), F32)], axis=1)
    line = jnp.broadcast_to(line, (8, width))
    line = pltpu.roll(line, lax.rem(2 * width - start, width), 1)[0:1]
    line = jnp.broadcast_to(line, (rows, width))
    return pltpu.roll(line, 0, 1, stride=1, stride_axis=0).astype(BF16)


def row_of(values, index):
    return jnp.sum(jnp.where(iota(values.shape, 0) == index, values, 0), axis=0, keepdims=True)


def load_taps(psf_ref, lines, epochs, taps):
    lines[0] = jnp.zeros(lines.shape[1:], F32)
    lines[0, :epochs, :taps] = psf_ref[...].astype(F32)
    mirror = iota((LANES, LANES), 0) + iota((LANES, LANES), 1) == taps - 1
    lines[1] = dot(lines[0].astype(BF16), mirror.astype(F32).astype(BF16))


def spans(length):
    return [(s, min(STEP, length - s)) for s in range(0, length, STEP)]


class Sizes:
    def __init__(self, images, sky_scene, psf_rows):
        self.local, self.height, self.width = images.shape
        self.rows = sky_scene.shape[0]
        self.epochs = psf_rows.shape[0]
        self.taps = psf_rows.shape[1]
        self.tile_rows = self.height // TILE
        self.wide = self.width + LANES
        self.groups = self.height // SPAN
        self.part = min(self.rows, SPAN)
        self.mask_rows = up_to(self.epochs, HALO)
        self.scene_at = SPAN * self.local
        self.mask_at = self.scene_at + self.part
        self.buffer_rows = self.mask_at + self.mask_rows
        self.blocks = self.height // self.rows
        self.tap_rows = self.mask_rows


def cover_at(coverage_ref, epoch, row_tile, col_tile):
    last_row = coverage_ref.shape[0] - 1
    last_col = coverage_ref.shape[1] - 1
    inside = (row_tile >= 0) & (row_tile <= last_row) & (col_tile >= 0) & (col_tile <= last_col)
    value = coverage_ref[jnp.clip(row_tile, 0, last_row), jnp.clip(col_tile, 0, last_col), epoch]
    return jnp.where(inside, value, 0).astype(F32)


def tile_of(position):
    return (position + TILE) // TILE - 1


def low(index, size):
    return index & (size - 1)


def high(index, size):
    return lax.shift_right_logical(index, size.bit_length() - 1)


def packing(count, width, shift):
    row, lane = iota((LANES * count, LANES), 0), iota((LANES * count, LANES), 1)
    here = high(lane, width) == high(row, LANES)
    here &= low(row, LANES) == low(lane, width) + shift
    return here.astype(F32).astype(BF16)


def side_by_side(ref, count, rows):
    return jnp.concatenate([ref[g * rows : (g + 1) * rows] for g in range(count)], axis=1)


def edge_copies(sz, images_ref, scene_ref, edge, sides, sem, side_sem):
    places = (0, sz.width - LANES)
    copies = []
    for e in range(sz.local):
        for side in range(2):
            slot = 2 * e + side
            copies.append(
                pltpu.make_async_copy(
                    images_ref.at[e, :, pl.ds(places[side], LANES)], edge.at[slot], sem.at[slot]
                )
            )
    side_copies = [
        pltpu.make_async_copy(
            scene_ref.at[:, pl.ds(places[side], LANES)], sides.at[side], side_sem.at[side]
        )
        for side in range(2)
    ]
    return copies, side_copies


def pack_edges(sz, flags, edge, sides, copies, side_copies, first_ref, second_ref):
    epoch = lax.axis_index("epoch") * sz.local
    even = lax.axis_index("sky") % 2 == 0
    places = (0, sz.width - LANES)

    def put(left, right, rows):
        first_ref[rows] = jnp.where(even, right, left).astype(BF16)
        second_ref[rows] = jnp.where(even, left, right).astype(BF16)

    packs = [packing(sz.groups, HALO, shift) for shift in (0, LANES - HALO)]
    row, lane = iota((LANES, LANES), 0), iota((LANES, LANES), 1)
    repeats = [
        (row == low(lane, HALO) + shift).astype(F32).astype(BF16) for shift in (0, LANES - HALO)
    ]
    for copy in copies + side_copies:
        copy.wait()
    goods, rows_good = [], []
    for side in range(2):
        good = flags[:, places[side] : places[side] + LANES].astype(F32)
        rows_good.append(good)
        if side == 1:
            good = pltpu.roll(good, HALO, 1)
        if sz.mask_rows > sz.epochs:
            good = jnp.concatenate(
                [good, jnp.zeros((sz.mask_rows - sz.epochs, LANES), F32)], axis=0
            )
        goods.append(good)
    put(goods[0], goods[1], slice(sz.mask_at, sz.buffer_rows))
    for e in range(sz.local):
        lines = []
        for side in range(2):
            slot = 2 * e + side
            good = jnp.broadcast_to(row_of(rows_good[side], epoch + e), (HALO, LANES))
            good = dot(good.astype(BF16), repeats[side])[0:1]
            lines.append(dot(side_by_side(edge.at[slot], sz.groups, SPAN), packs[side]) * good)
        put(lines[0], lines[1], slice(SPAN * e, SPAN * (e + 1)))
    cells = []
    count = sz.rows // sz.part
    for side, shift in enumerate((0, LANES - RIM)):
        cells.append(
            dot(side_by_side(sides.at[side], count, sz.part), packing(count, RIM, shift))
        )
    put(cells[0], cells[1], slice(sz.scene_at, sz.mask_at))


def edges_kernel(sz, images_ref, scene_ref, mask_ref, first_ref, second_ref, *scratch):
    edge, sides, flags, sem, side_sem, flag_sem = scratch
    copies, side_copies = edge_copies(sz, images_ref, scene_ref, edge, sides, sem, side_sem)
    flag_copy = pltpu.make_async_copy(mask_ref, flags, flag_sem)
    for copy in [flag_copy] + copies + side_copies:
        copy.start()
    flag_copy.wait()
    pack_edges(sz, flags, edge, sides, copies, side_copies, first_ref, second_ref)


def edges(sz, images, scene, mask):
    shape = jax.ShapeDtypeStruct((sz.buffer_rows, LANES), BF16)
    return pl.pallas_call(
        functools.partial(edges_kernel, sz),
        out_shape=(shape, shape),
        in_specs=[HBM, HBM, HBM],
        out_specs=(VMEM, VMEM),
        scratch_shapes=[
            pltpu.VMEM((2 * sz.local, sz.height, LANES), BF16),
            pltpu.VMEM((2, sz.rows, LANES), BF16),
            pltpu.VMEM((sz.epochs, sz.width), jnp.int32),
            pltpu.SemaphoreType.DMA((2 * sz.local,)),
            pltpu.SemaphoreType.DMA((2,)),
            pltpu.SemaphoreType.DMA,
        ],
        compiler_params=WHOLE,
        cost_estimate=SHORT,
        name="edges",
    )(images, scene, mask)


def sides_of(first, second):
    even = lax.axis_index("sky") % 2 == 0
    return jnp.where(even, second, first), jnp.where(even, first, second)


def widen_rows(sz, scene_ref, first_ref, second_ref, start, count):
    group, inside = start // sz.part, start % sz.part
    cells = slice(sz.scene_at + inside, sz.scene_at + inside + count)
    row, lane = iota((LANES, sz.wide), 0), iota((LANES, sz.wide), 1)
    wide = dot(scene_ref[start : start + count], selection(sz.width, sz.wide, RIM))
    ends = sides_of(first_ref[cells], second_ref[cells])
    for end, at in zip(ends, (0, sz.width + RIM)):
        place = (high(row, RIM) == group) & (lane == low(row, RIM) + at)
        wide += dot(end, place.astype(F32).astype(BF16))
    return wide.astype(BF16)


def widen_kernel(sz, scene_ref, mask_ref, first_ref, second_ref, wide_ref, good_ref):
    for start in range(0, sz.rows, sz.part):
        wide_ref[start : start + sz.part] = widen_rows(
            sz, scene_ref, first_ref, second_ref, start, sz.part
        )
    flags = slice(sz.mask_at, sz.buffer_rows)
    before, after = sides_of(first_ref[flags], second_ref[flags])
    own = mask_ref[...].astype(F32)
    if sz.mask_rows > sz.epochs:
        own = jnp.concatenate(
            [own, jnp.zeros((sz.mask_rows - sz.epochs, sz.width), F32)], axis=0
        )
    good = dot(own.astype(BF16), selection(sz.width, sz.wide, HALO))
    inner = iota((LANES, sz.wide), 0) < HALO
    zero = jnp.zeros((LANES, sz.wide), BF16)
    good += dot(before, jnp.where(inner, selection(LANES, sz.wide, 0), zero))
    good += dot(after, jnp.where(inner, selection(LANES, sz.wide, sz.width + HALO), zero))
    good_ref[...] = good


def destination(slot, place):
    return (
        3 * (1 - place % 2),
        2 - place // 2,
        (2 * place + 1) % 5,
        place,
    )[slot]


def rim_rows(sz, epoch, e, coverage_ref, row_line, row_shift, twice, first_ref, second_ref):
    rows = slice(SPAN * e, SPAN * (e + 1))
    column = lax.axis_index("sky") * sz.width
    both = jnp.concatenate(sides_of(first_ref[rows], second_ref[rows]), axis=1)
    lane = iota((1, 2 * LANES), 1)
    factor = jnp.zeros((1, 2 * LANES), F32)
    for side, at in enumerate((column - HALO, column + sz.width)):
        for tile in range(sz.tile_rows):
            cover = cover_at(coverage_ref, epoch, tile, tile_of(at))
            here = high(lane, LANES) == side
            here &= high(low(lane, LANES), HALO * TILE // SPAN) == tile
            factor = jnp.where(here, cover, factor)
    both = both.astype(F32) * factor
    above = pltpu.roll(both[SPAN - HALO :], HALO, 1)
    below = pltpu.roll(both[:HALO], 2 * LANES - HALO, 1)
    above = jnp.where(low(lane, LANES) < HALO, 0.0, above)
    below = jnp.where(low(lane, LANES) >= HALO * (sz.groups - 1), 0.0, below)
    window = jnp.concatenate([above, both, below], axis=0).astype(BF16)
    table = toeplitz(row_line, row_shift - 4, SPAN, SPAN + LANES)[:, : SPAN + RIM]
    return (dot(table, window) * twice).astype(BF16)


def rim_columns(col_line, col_shift):
    enter = toeplitz(col_line, 28 - col_shift, HALO, SPAN)[:, :LANES]
    leave = toeplitz(col_line, SPAN + LANES - 116 - col_shift, HALO, SPAN + LANES)[:, :LANES]
    none = jnp.zeros((HALO, LANES), BF16)
    upper = [jnp.concatenate([enter, none], axis=1)] * (LANES // HALO)
    lower = [jnp.concatenate([none, leave], axis=1)] * (LANES // HALO)
    return jnp.concatenate(upper + lower, axis=0)


def rim_part(sz, start, rim_ref, table):
    group = start // SPAN
    row = iota((2 * LANES, SPAN), 0)
    parts = []
    for k in range(max(sz.rows // SPAN, 1)):
        picked = jnp.where(high(low(row, LANES), HALO) == group + k, table, jnp.zeros_like(table))
        if sz.rows >= SPAN:
            rows = rim_ref[...]
        else:
            rows = rim_ref[pl.ds(pl.multiple_of(start - group * SPAN, sz.rows), sz.rows)]
        parts.append(dot(rows, picked))
    return jnp.concatenate(parts, axis=0) if len(parts) > 1 else parts[0]


def rim_places(sz, h):
    row, lane = iota((SPAN, LANES), 0), iota((SPAN, LANES), 1)
    here = (lane == row + RIM * h) & (row < HALO)
    here |= (lane == row - SPAN + RIM * (h + 1)) & (row >= SPAN - HALO)
    return here.astype(F32).astype(BF16)


def rim_spread(sz, h):
    row, lane = iota((LANES, SPAN), 0), iota((LANES, SPAN), 1)
    here = (row == lane + RIM * h) & (lane < HALO)
    here |= (row == lane - SPAN + RIM * (h + 1)) & (lane >= SPAN - HALO)
    return here.astype(F32).astype(BF16)


def pack_rows(sz, ref, at, rim):
    ref[at : at + RIM] = rim[:, : sz.width]
    left = slice(at + RIM, at + RIM + HALO)
    ref[left, :LANES] = rim[:HALO, sz.width :]
    ref[left, LANES:SPAN] = rim[HALO:, sz.width :]
    ref[left, SPAN:] = jnp.zeros((HALO, sz.width - SPAN), BF16)


def pack_part(sz, ref, at, part):
    total = None
    for h in range(sz.rows // LANES):
        rows = part[h * LANES : (h + 1) * LANES].astype(BF16)
        moved = dot(rows, rim_places(sz, h))
        total = moved if total is None else total + moved
    total = total.astype(BF16)
    for k in range(LANES // RIM):
        ref[at : at + RIM, k * LANES : (k + 1) * LANES] = total[k * RIM : (k + 1) * RIM]


def unpack_rim(sz, ref, at):
    left = slice(at + RIM, at + RIM + HALO)
    rest = jnp.concatenate([ref[left, :LANES], ref[left, LANES:SPAN]], axis=0)
    return jnp.concatenate([ref[at : at + RIM], rest], axis=1)


def unpack_part(sz, ref, at):
    pieces = [ref[at : at + RIM, k * LANES : (k + 1) * LANES] for k in range(LANES // RIM)]
    packed = jnp.concatenate(pieces, axis=0)
    parts = [dot(packed, rim_spread(sz, h)) for h in range(sz.rows // LANES)]
    return jnp.concatenate(parts, axis=0)


def complete(sz, out, part):
    rows = slice(0, sz.rows)
    for at, cols in ((0, slice(0, LANES)), (LANES, slice(sz.width - LANES, sz.width))):
        value = out[rows, cols].astype(F32) + part[:, at : at + LANES]
        out[rows, cols] = value.astype(BF16)


def rim_parts_of(sz, slots, place, offsets_ref, col_lines, rim_ref):
    tables = []
    for e in range(sz.local):
        epoch = place * sz.local + e
        tables.append(rim_columns(row_of(col_lines[0], epoch), offsets_ref[1, epoch]))
    parts = []
    for slot in slots:
        part = None
        for e in range(sz.local):
            term = rim_part(sz, destination(slot, place) * sz.rows, rim_ref.at[e], tables[e])
            part = term if part is None else part + term
        parts.append(part)
    return parts


def notes_kernel(
    sz, coverage_ref, offsets_ref, weight_ref, scene_ref, first_ref, second_ref,
    psf_rows_ref, psf_cols_ref, far_out, rim_ref, part_out, row_lines, col_lines,
):
    place = lax.axis_index("epoch")
    outer = (place == 0) | (place == 3)
    load_taps(psf_rows_ref, row_lines, sz.epochs, sz.taps)
    load_taps(psf_cols_ref, col_lines, sz.epochs, sz.taps)
    for e in range(sz.local):
        epoch = place * sz.local + e
        rim_ref[e] = rim_rows(
            sz, epoch, e, coverage_ref, row_of(row_lines[1], epoch), offsets_ref[0, epoch],
            -2.0 * weight_ref[epoch], first_ref, second_ref,
        )
    parts = rim_parts_of(sz, (0, 1), place, offsets_ref, col_lines, rim_ref)
    top = widen_rows(sz, scene_ref, first_ref, second_ref, 0, RIM)
    bottom = widen_rows(sz, scene_ref, first_ref, second_ref, sz.rows - RIM, RIM)
    pack_rows(sz, far_out, 0, jnp.where(place < 2, bottom, top))
    pack_part(sz, far_out, RIM + HALO, jnp.where(outer, parts[0], parts[1]))
    part_out[...] = parts[1].astype(BF16)


def notes(sz, coverage, offsets, weight, scene, first, second, psf_rows, psf_cols):
    return pl.pallas_call(
        functools.partial(notes_kernel, sz),
        out_shape=(
            jax.ShapeDtypeStruct((2 * RIM + HALO, sz.width), BF16),
            jax.ShapeDtypeStruct((sz.local, SPAN, 2 * LANES), BF16),
            jax.ShapeDtypeStruct((sz.rows, SPAN), BF16),
        ),
        in_specs=[SMEM] * 3 + [VMEM] * 5,
        out_specs=(VMEM, VMEM, VMEM),
        scratch_shapes=[pltpu.VMEM((2, sz.tap_rows, LANES), F32)] * 2,
        compiler_params=PARAMS,
        cost_estimate=SHORT,
        name="notes",
    )(coverage, offsets, weight, scene, first, second, psf_rows, psf_cols)


def early_kernel(
    sz, offsets_ref, scene_ref, first_ref, second_ref, psf_cols_ref, rim_ref, three_ref,
    near_out, col_lines,
):
    place = lax.axis_index("epoch")
    load_taps(psf_cols_ref, col_lines, sz.epochs, sz.taps)
    (part,) = rim_parts_of(sz, (2,), place, offsets_ref, col_lines, rim_ref)
    top = widen_rows(sz, scene_ref, first_ref, second_ref, 0, RIM)
    bottom = widen_rows(sz, scene_ref, first_ref, second_ref, sz.rows - RIM, RIM)
    pack_rows(sz, near_out, sz.rows, jnp.where(place % 2 == 0, bottom, top))
    near_out[: sz.rows] = three_ref[...]
    complete(sz, near_out, part)


def early(sz, offsets, scene, first, second, psf_cols, rim, three):
    return pl.pallas_call(
        functools.partial(early_kernel, sz),
        out_shape=jax.ShapeDtypeStruct((sz.rows + RIM + HALO, sz.width), BF16),
        in_specs=[SMEM] + [VMEM] * 6,
        out_specs=VMEM,
        scratch_shapes=[pltpu.VMEM((2, sz.tap_rows, LANES), F32)],
        compiler_params=PARAMS,
        cost_estimate=SHORT,
        name="early",
    )(offsets, scene, first, second, psf_cols, rim, three)


def merge_kernel(sz, two_ref, near_ref, one_ref, part_ref, out_ref):
    place = lax.axis_index("epoch")
    outer = (place == 0) | (place == 3)

    @pl.when(outer)
    def _():
        out_ref[...] = two_ref[...]
        complete(sz, out_ref, part_ref[...].astype(F32))

    @pl.when(jnp.logical_not(outer))
    def _():
        total = near_ref[: sz.rows].astype(F32) + one_ref[...].astype(F32)
        out_ref[...] = total.astype(BF16)


def merge(sz, two, near, one, part):
    return pl.pallas_call(
        functools.partial(merge_kernel, sz),
        out_shape=jax.ShapeDtypeStruct((sz.rows, sz.width), BF16),
        in_specs=[VMEM] * 4,
        out_specs=VMEM,
        compiler_params=PARAMS,
        cost_estimate=SHORT,
        name="merge",
    )(two, near, one, part)


def finish_kernel(sz, offsets_ref, scene_ref, mask_ref, first_ref, second_ref, *more):
    if sz.blocks != 4:
        widen_kernel(sz, scene_ref, mask_ref, first_ref, second_ref, *more)
        return
    psf_cols_ref, rim_ref, own_ref, wide_ref, good_ref, back_out, own_out, col_lines, sem = more
    place = lax.axis_index("epoch")
    copy = pltpu.make_async_copy(own_ref, own_out, sem)
    copy.start()
    load_taps(psf_cols_ref, col_lines, sz.epochs, sz.taps)
    parts = rim_parts_of(sz, (0, 3), place, offsets_ref, col_lines, rim_ref)
    widen_kernel(sz, scene_ref, mask_ref, first_ref, second_ref, wide_ref, good_ref)
    top, bottom = wide_ref[:RIM], wide_ref[sz.rows - RIM :]
    pack_rows(sz, back_out, 0, jnp.where(place % 2 == 0, bottom, top))
    pack_part(sz, back_out, RIM + HALO, parts[0])
    copy.wait()
    complete(sz, own_out, parts[1])


def finish(sz, offsets, scene, mask, first, second, *more):
    full = jax.ShapeDtypeStruct((sz.rows, sz.width), BF16)
    shapes = [
        jax.ShapeDtypeStruct((sz.rows, sz.wide), BF16),
        jax.ShapeDtypeStruct((sz.mask_rows, sz.wide), F32),
    ]
    scratch = []
    if more:
        shapes += [jax.ShapeDtypeStruct((2 * RIM + HALO, sz.width), BF16), full]
        scratch = [pltpu.VMEM((2, sz.tap_rows, LANES), F32), pltpu.SemaphoreType.DMA]
    return pl.pallas_call(
        functools.partial(finish_kernel, sz),
        out_shape=tuple(shapes),
        in_specs=[SMEM] + [VMEM] * 4 + [VMEM, VMEM, HBM][: len(more)],
        out_specs=tuple([VMEM] * len(shapes)),
        scratch_shapes=scratch,
        compiler_params=PARAMS,
        cost_estimate=SHORT,
        name="finish",
    )(offsets, scene, mask, first, second, *more)


def image_kernel(sz, slots, rims, packs, images_ref, *more):
    count = 1 if slots is None else len(slots)
    small, ends, more = more[:6], more[6 : 6 + rims], more[6 + rims :]
    if packs:
        scene_ref, *more = more
    outs, more = more[:count], more[count:]
    if packs:
        first_out, second_out, edge, sides, edge_sem, side_sem, *more = more
    held, small_sem, more = more[:6], more[6], more[7:]
    coverage_ref, offsets_ref, weight_ref, mask_ref, psf_rows_ref, psf_cols_ref = held
    window, row_done, row_lines, col_lines, row_table, main_table, cross_table, rim_ref, sem = more
    place = lax.axis_index("epoch")
    first = place * sz.local
    column = lax.axis_index("sky") * sz.width
    if slots is None:
        targets = [pl.program_id(0)]
    else:
        targets = [destination(slot, place) for slot in slots]

    copies = []
    for i, target in enumerate(targets):
        start = target * sz.rows
        head = jnp.maximum(start - HALO, 0)
        foot = jnp.minimum(start + sz.rows, sz.height - HALO)
        for e in range(sz.local):
            for n, (source, at, length) in enumerate(
                ((start, HALO, sz.rows), (head, 0, HALO), (foot, HALO + sz.rows, HALO))
            ):
                copies.append(
                    pltpu.make_async_copy(
                        images_ref.at[e, pl.ds(pl.multiple_of(source, HALO), length), :],
                        window.at[i, e, pl.ds(at, length), :],
                        sem.at[i, e, n],
                    )
                )
    held_copies = [
        pltpu.make_async_copy(source, target, small_sem.at[n])
        for n, (source, target) in enumerate(zip(small, held))
    ]
    for copy in held_copies + copies:
        copy.start()
    if packs:
        edge_waits = edge_copies(sz, images_ref, scene_ref, edge, sides, edge_sem, side_sem)
        for copy in edge_waits[0] + edge_waits[1]:
            copy.start()
    for copy in held_copies:
        copy.wait()
    load_taps(psf_rows_ref, row_lines, sz.epochs, sz.taps)
    load_taps(psf_cols_ref, col_lines, sz.epochs, sz.taps)
    for e in range(sz.local):
        epoch = first + e
        row_shift, col_shift = offsets_ref[0, epoch], offsets_ref[1, epoch]
        row_table[e] = toeplitz(row_of(row_lines[1], epoch), row_shift - 4, STEP, SPAN)
        line = row_of(col_lines[0], epoch)
        main = toeplitz(line, 12 - col_shift, SPAN, SPAN + LANES)[:, :SPAN]
        main_table[e] = main
        apart = (iota((SPAN, SPAN), 0) < LANES) != (iota((SPAN, SPAN), 1) < LANES)
        cross_table[e] = jnp.where(apart, main, jnp.zeros_like(main))
    rim_parts = []
    for e in range(sz.local if rims else 0):
        epoch = first + e
        rim_ref[e] = rim_rows(
            sz, epoch, e, coverage_ref, row_of(row_lines[1], epoch), offsets_ref[0, epoch],
            -2.0 * weight_ref[epoch], *ends,
        )
        table = rim_columns(row_of(col_lines[0], epoch), offsets_ref[1, epoch])
        for i, target in enumerate(targets):
            part = rim_part(sz, target * sz.rows, rim_ref.at[e], table)
            if e == 0:
                rim_parts.append(part)
            else:
                rim_parts[i] += part
    column_tile = column // TILE
    for i, target in enumerate(targets):
        for copy in copies[3 * sz.local * i : 3 * sz.local * (i + 1)]:
            copy.wait()
        start = target * sz.rows
        zones = (
            (0, HALO, tile_of(start - HALO)),
            (HALO, HALO + sz.rows, tile_of(start)),
            (HALO + sz.rows, RIM + sz.rows, tile_of(start + sz.rows)),
        )
        for e in range(sz.local):
            epoch = first + e
            good = row_of(mask_ref[...].astype(F32), epoch)
            for begin, end, tile in zones:
                factor = good * cover_at(coverage_ref, epoch, tile, column_tile)
                window[i, e, begin:end] = window[i, e, begin:end] * factor.astype(BF16)
            twice = -2.0 * weight_ref[epoch]
            for s, n in spans(sz.rows):
                part = dot(row_table[e, :n, : n + RIM], window[i, e, s : s + n + RIM])
                row_done[i, e, s : s + n] = (part * twice).astype(BF16)
    for i in range(count):
        total = []
        for b in range(0, sz.width, SPAN):
            out = None
            for e in range(sz.local):
                part = dot(row_done[i, e, :, b : b + SPAN], main_table[e])
                out = part if out is None else out + part
            total += [out[:, :LANES], out[:, LANES:]]
        for b in range(LANES, sz.width - LANES, SPAN):
            out = None
            for e in range(sz.local):
                part = dot(row_done[i, e, :, b : b + SPAN], cross_table[e])
                out = part if out is None else out + part
            total[b // LANES] += out[:, :LANES]
            total[b // LANES + 1] += out[:, LANES:]
        if rims:
            total[0] += rim_parts[i][:, :LANES]
            total[-1] += rim_parts[i][:, LANES:]
        for k, piece in enumerate(total):
            outs[i][:, k * LANES : (k + 1) * LANES] = piece.astype(BF16)
    if packs:
        pack_edges(sz, mask_ref, edge, sides, *edge_waits, first_out, second_out)


def image_blocks(
    sz, slots, coverage, offsets, weight, images, mask, psf_rows, psf_cols, *ends, scene=None
):
    packs = scene is not None
    if slots is None:
        count = 1
        grid = dict(
            grid=(sz.blocks,),
            out_shape=jax.ShapeDtypeStruct((sz.blocks * sz.rows, sz.width), BF16),
            out_specs=pl.BlockSpec((sz.rows, sz.width), lambda i: (i, 0)),
        )
    else:
        count = len(slots)
        shapes = [jax.ShapeDtypeStruct((sz.rows, sz.width), BF16)] * count
        if packs:
            shapes += [jax.ShapeDtypeStruct((sz.buffer_rows, LANES), BF16)] * 2
        grid = dict(out_shape=tuple(shapes), out_specs=tuple([VMEM] * len(shapes)))
    pack_scratch = [
        pltpu.VMEM((2 * sz.local, sz.height, LANES), BF16),
        pltpu.VMEM((2, sz.rows, LANES), BF16),
        pltpu.SemaphoreType.DMA((2 * sz.local,)),
        pltpu.SemaphoreType.DMA((2,)),
    ]
    return pl.pallas_call(
        functools.partial(image_kernel, sz, slots, len(ends), packs),
        in_specs=[HBM] * 7 + [VMEM] * len(ends) + [HBM] * packs,
        scratch_shapes=pack_scratch * packs
        + [
            pltpu.SMEM(coverage.shape, jnp.int32),
            pltpu.SMEM(offsets.shape, jnp.int32),
            pltpu.SMEM(weight.shape, F32),
            pltpu.VMEM(mask.shape, jnp.int32),
            pltpu.VMEM(psf_rows.shape, BF16),
            pltpu.VMEM(psf_cols.shape, BF16),
            pltpu.SemaphoreType.DMA((6,)),
            pltpu.VMEM((count, sz.local, sz.rows + RIM, sz.width), BF16),
            pltpu.VMEM((count, sz.local, sz.rows, sz.width), BF16),
            pltpu.VMEM((2, sz.tap_rows, LANES), F32),
            pltpu.VMEM((2, sz.tap_rows, LANES), F32),
            pltpu.VMEM((sz.local, STEP, SPAN), BF16),
            pltpu.VMEM((sz.local, SPAN, SPAN), BF16),
            pltpu.VMEM((sz.local, SPAN, SPAN), BF16),
            pltpu.VMEM((sz.local, SPAN, 2 * LANES), BF16),
            pltpu.SemaphoreType.DMA((count, sz.local, 3)),
        ],
        compiler_params=WHOLE if slots is not None and 0 in slots else PARAMS,
        cost_estimate=SHORT,
        name="image_blocks",
        **grid,
    )(images, coverage, offsets, weight, mask, psf_rows, psf_cols, *ends, *([scene] * packs))


def column_tables(taps, start):
    pair = toeplitz(taps, start, LANES, SPAN)
    here, past = pair[:, :LANES], pair[:, LANES:]
    none = jnp.zeros_like(here)
    main = jnp.concatenate(
        [jnp.concatenate([here, none], axis=1), jnp.concatenate([past, here], axis=1)], axis=0
    )
    rest = jnp.concatenate(
        [jnp.concatenate([past, none], axis=1), jnp.concatenate([none, past], axis=1)], axis=0
    )
    return main, rest, here, past


def column_pass(sz, source, tables, tail):
    main, rest, here, past = tables
    tiles = []
    for b in range(0, sz.width, SPAN):
        out = dot(source[:, b : b + SPAN], main)
        tiles += [out[:, :LANES], out[:, LANES:]]
    ends = list(range(SPAN, sz.wide, SPAN))
    if len(ends) == 2:
        joined = jnp.concatenate([source[:, at : at + LANES] for at in ends], axis=1)
        out = dot(joined, rest)
        parts = [out[:, :LANES], out[:, LANES:]]
    else:
        parts = [dot(source[:, at : at + LANES], past) for at in ends]
    for at, part in zip(ends, parts):
        tiles[at // LANES - 1] += part
    if tail:
        tiles.append(dot(source[:, sz.width : sz.wide], here))
    return tiles


def model_kernel(
    sz, batch, coverage_ref, offsets_ref, weight_ref,
    wide_ref, good_ref, psf_rows_ref, psf_cols_ref, *more,
):
    *extra, out_ref, scene, lifted, residual, pulled, row_lines, col_lines = more
    step = pl.program_id(0)
    place = lax.axis_index("epoch")
    start = place * sz.rows
    column = lax.axis_index("sky") * sz.width

    @pl.when(step == 0)
    def _():
        load_taps(psf_rows_ref, row_lines, sz.epochs, sz.taps)
        load_taps(psf_cols_ref, col_lines, sz.epochs, sz.taps)
        scene[RIM : RIM + sz.rows] = wide_ref[...]
        if sz.blocks != 4:
            head_ref, foot_ref, base_ref = extra
            scene[0:RIM] = head_ref[...]
            scene[RIM + sz.rows :] = foot_ref[...]
            out_ref[...] = base_ref[...]
        else:
            own_ref, one_ref, two_ref, three_ref, back_ref, far_ref = extra
            outer = (place == 0) | (place == 3)
            near = jnp.where(
                outer, unpack_rim(sz, back_ref, 0), unpack_rim(sz, three_ref, sz.rows)
            )
            far = unpack_rim(sz, far_ref, 0)
            none = jnp.zeros_like(near)
            odd = place % 2 == 1
            scene[0:RIM] = jnp.where(odd, near, jnp.where(outer, none, far))
            scene[RIM + sz.rows :] = jnp.where(odd, jnp.where(outer, none, far), near)
            rows = slice(RIM + HALO, 2 * RIM + HALO)
            fix = unpack_part(sz, back_ref[rows], 0) + unpack_part(sz, far_ref[rows], 0)
            for b in range(0, sz.width, LANES):
                cols = slice(b, b + LANES)
                inner = two_ref[:, cols].astype(F32) + three_ref[: sz.rows, cols].astype(F32)
                base = jnp.where(outer, one_ref[:, cols].astype(F32), inner)
                base += own_ref[:, cols].astype(F32)
                for at, side in ((0, 0), (LANES, sz.width - LANES)):
                    if b == side:
                        base += fix[:, at : at + LANES]
                out_ref[:, cols] = base

    epochs = [step * batch + n for n in range(batch)]
    edge = sz.rows + HALO
    for n, epoch in enumerate(epochs):
        row_in = toeplitz(row_of(row_lines[0], epoch), -4 - offsets_ref[0, epoch], STEP, SPAN)
        for s, count in spans(sz.rows + RIM):
            lifted[n, s : s + count] = dot(
                row_in[:count, : count + RIM], scene[s : s + count + RIM]
            ).astype(BF16)
    for n, epoch in enumerate(epochs):
        good = row_of(good_ref[...], epoch) * (2.0 * weight_ref[epoch])
        lane = iota((1, sz.wide), 1)
        factors = []
        for row_tile in (tile_of(start - HALO), tile_of(start), tile_of(start + sz.rows)):
            left, here, right = (
                cover_at(coverage_ref, epoch, row_tile, tile_of(c))
                for c in (column - HALO, column, column + sz.width)
            )
            factors.append(
                good * jnp.where(lane < HALO, left, jnp.where(lane < HALO + sz.width, here, right))
            )
        tables = column_tables(row_of(col_lines[1], epoch), 28 + offsets_ref[1, epoch])
        for k, modeled in enumerate(column_pass(sz, lifted[n], tables, True)):
            b = k * LANES
            head, mid, foot = (f[:, b : b + LANES] for f in factors)
            residual[n, 0:HALO, b : b + LANES] = (modeled[0:HALO] * head).astype(BF16)
            residual[n, HALO:edge, b : b + LANES] = (modeled[HALO:edge] * mid).astype(BF16)
            residual[n, edge:, b : b + LANES] = (modeled[edge:] * foot).astype(BF16)
    for n, epoch in enumerate(epochs):
        tables = column_tables(row_of(col_lines[0], epoch), 28 - offsets_ref[1, epoch])
        for k, tile in enumerate(column_pass(sz, residual[n], tables, False)):
            pulled[n, :, k * LANES : (k + 1) * LANES] = tile.astype(BF16)
    row_outs = [
        toeplitz(row_of(row_lines[1], epoch), offsets_ref[0, epoch] - 4, STEP, SPAN)
        for epoch in epochs
    ]
    for s, count in spans(sz.rows):
        total = out_ref[s : s + count]
        for n in range(batch):
            total += dot(row_outs[n][:count, : count + RIM], pulled[n, s : s + count + RIM])
        out_ref[s : s + count] = total


def model_term(sz, coverage, offsets, weight, wide, good, psf_rows, psf_cols, *extra):
    high = sz.rows + RIM
    batch = 8 if sz.epochs % 8 == 0 else 1
    return pl.pallas_call(
        functools.partial(model_kernel, sz, batch),
        grid=(sz.epochs // batch,),
        out_shape=jax.ShapeDtypeStruct((sz.rows, sz.width), F32),
        in_specs=[SMEM] * 3 + [VMEM] * (4 + len(extra)),
        out_specs=VMEM,
        scratch_shapes=[
            pltpu.VMEM((sz.rows + 2 * RIM, sz.wide), BF16),
            pltpu.VMEM((batch, high, sz.wide), BF16),
            pltpu.VMEM((batch, high, sz.wide), BF16),
            pltpu.VMEM((batch, high, sz.width), BF16),
            pltpu.VMEM((2, sz.tap_rows, LANES), F32),
            pltpu.VMEM((2, sz.tap_rows, LANES), F32),
        ],
        compiler_params=PARAMS,
        cost_estimate=SHORT,
        name="model_term",
    )(coverage, offsets, weight, wide, good, psf_rows, psf_cols, *extra)


def on_device(sky_scene, images, psf_rows, psf_cols, offsets, epoch_weight, column_mask, coverage):
    sz = Sizes(images, sky_scene, psf_rows)
    peers = lax.axis_size("sky")
    depth = lax.axis_size("epoch")
    scalars = (jnp.transpose(coverage, (1, 2, 0)), offsets.T, epoch_weight)
    profiles = (psf_rows, psf_cols)

    def pairs(start, count):
        return [p for i in range(start, count - 1, 2) for p in ((i, i + 1), (i + 1, i))]

    def blocks(slots, shifts, *ends, scene=None):
        return image_blocks(
            sz, slots, scalars[0], shifts, epoch_weight, images, column_mask, *profiles, *ends,
            scene=scene,
        )

    if depth == 4:
        one, two, first, second = blocks((0, 1), scalars[1], scene=sky_scene)
        got_one = lax.ppermute(one, "epoch", pairs(0, depth))
        got_two = lax.ppermute(two, "epoch", pairs(1, depth))
        shifts, one = lax.optimization_barrier((scalars[1], one))
        three, own = blocks((2, 3), shifts)
        first = lax.ppermute(first, "sky", pairs(0, peers))
        second = lax.ppermute(second, "sky", pairs(1, peers))
        second, three = lax.optimization_barrier((second, three))
        far, rim, part = notes(sz, *scalars, sky_scene, first, second, *profiles)
        near = early(sz, scalars[1], sky_scene, first, second, psf_cols, rim, three)
        got_three = lax.ppermute(near, "epoch", [(0, 1), (3, 2)])
        got_far = lax.ppermute(far, "epoch", [(0, 3), (3, 0), (1, 2), (2, 1)])
        passed = merge(sz, two, near, got_one, part)
        passed, got_far, got_two, rim = lax.optimization_barrier((passed, got_far, got_two, rim))
        got_passed = lax.ppermute(passed, "epoch", [(0, 2), (3, 1), (1, 3), (2, 0)])
        wide, good, back, own = finish(
            sz, scalars[1], sky_scene, column_mask, first, second, psf_cols, rim, own
        )
        got_back = lax.ppermute(back, "epoch", [(1, 0), (2, 3)])
        model = model_term(
            sz, *scalars, wide, good, *profiles,
            own, got_one, got_two, got_three, got_back, got_far,
        )
        return model + got_passed.astype(F32)

    first, second = edges(sz, images, sky_scene, column_mask)
    first = lax.ppermute(first, "sky", pairs(0, peers))
    second = lax.ppermute(second, "sky", pairs(1, peers))
    downward = [(i, i + 1) for i in range(depth - 1)]
    upward = [(i + 1, i) for i in range(depth - 1)]
    wide, good = finish(sz, scalars[1], sky_scene, column_mask, first, second)
    head = lax.ppermute(wide[-RIM:], "epoch", downward)
    foot = lax.ppermute(wide[:RIM], "epoch", upward)
    terms = blocks(None, scalars[1], first, second).astype(F32)
    base = lax.psum_scatter(terms, "epoch", scatter_dimension=0, tiled=True)
    return model_term(sz, *scalars, wide, good, *profiles, head, foot, base)


def solution(mesh):
    return jax.shard_map(
        on_device,
        mesh=mesh,
        in_specs=(
            P(("field", "epoch"), "sky"),
            P(("field", "epoch"), None, "sky"),
            P("field", None),
            P("field", None),
            P("field", None),
            P("field"),
            P("field", "sky"),
            P("field", None, None),
        ),
        out_specs=P(("field", "epoch"), "sky"),
        check_vma=False,
    )
```

```python
import functools

import jax
import jax.numpy as jnp
from jax import lax
from jax.experimental import pallas as pl
from jax.experimental.pallas import tpu as pltpu
from jax.sharding import PartitionSpec as P

TILE = 512
HALO = 16
RIM = 2 * HALO
LANES = 128
SPAN = 256
STEP = SPAN - RIM
F32 = jnp.float32
BF16 = jnp.bfloat16
VMEM = pl.BlockSpec(memory_space=pltpu.VMEM)
SMEM = pl.BlockSpec(memory_space=pltpu.SMEM)
HBM = pl.BlockSpec(memory_space=pltpu.HBM)
PARAMS = pltpu.CompilerParams(vmem_limit_bytes=40 * 1024 * 1024)
SHORT = pl.CostEstimate(flops=1000, bytes_accessed=1000, transcendentals=0)
WHOLE = pltpu.CompilerParams(vmem_limit_bytes=59 * 1024 * 1024)


def up_to(value, unit):
    return -(-value // unit) * unit


def dot(a, b, dims=((1,), (0,))):
    return lax.dot_general(a, b, (dims, ((), ())), preferred_element_type=F32)


def iota(shape, dim):
    return lax.broadcasted_iota(jnp.int32, shape, dim)


def selection(rows, cols, shift):
    return (iota((rows, cols), 1) == iota((rows, cols), 0) + shift).astype(BF16)


def toeplitz(taps, start, rows, width):
    line = jnp.concatenate([taps, jnp.zeros((1, width - LANES), F32)], axis=1)
    line = jnp.broadcast_to(line, (8, width))
    line = pltpu.roll(line, lax.rem(2 * width - start, width), 1)[0:1]
    line = jnp.broadcast_to(line, (rows, width))
    return pltpu.roll(line, 0, 1, stride=1, stride_axis=0).astype(BF16)


def row_of(values, index):
    return jnp.sum(jnp.where(iota(values.shape, 0) == index, values, 0), axis=0, keepdims=True)


def load_taps(psf_ref, lines, epochs, taps):
    lines[0] = jnp.zeros(lines.shape[1:], F32)
    lines[0, :epochs, :taps] = psf_ref[...].astype(F32)
    mirror = iota((LANES, LANES), 0) + iota((LANES, LANES), 1) == taps - 1
    lines[1] = dot(lines[0].astype(BF16), mirror.astype(F32).astype(BF16))


def spans(length):
    return [(s, min(STEP, length - s)) for s in range(0, length, STEP)]


class Sizes:
    def __init__(self, images, sky_scene, psf_rows):
        self.local, self.height, self.width = images.shape
        self.rows = sky_scene.shape[0]
        self.epochs = psf_rows.shape[0]
        self.taps = psf_rows.shape[1]
        self.tile_rows = self.height // TILE
        self.wide = self.width + LANES
        self.groups = self.height // SPAN
        self.part = min(self.rows, SPAN)
        self.mask_rows = up_to(self.epochs, HALO)
        self.scene_at = SPAN * self.local
        self.mask_at = self.scene_at + self.part
        self.buffer_rows = self.mask_at + self.mask_rows
        self.blocks = self.height // self.rows
        self.tap_rows = self.mask_rows


def cover_at(coverage_ref, epoch, row_tile, col_tile):
    last_row = coverage_ref.shape[0] - 1
    last_col = coverage_ref.shape[1] - 1
    inside = (row_tile >= 0) & (row_tile <= last_row) & (col_tile >= 0) & (col_tile <= last_col)
    value = coverage_ref[jnp.clip(row_tile, 0, last_row), jnp.clip(col_tile, 0, last_col), epoch]
    return jnp.where(inside, value, 0).astype(F32)


def tile_of(position):
    return (position + TILE) // TILE - 1


def low(index, size):
    return index & (size - 1)


def high(index, size):
    return lax.shift_right_logical(index, size.bit_length() - 1)


def packing(count, width, shift):
    row, lane = iota((LANES * count, LANES), 0), iota((LANES * count, LANES), 1)
    here = high(lane, width) == high(row, LANES)
    here &= low(row, LANES) == low(lane, width) + shift
    return here.astype(F32).astype(BF16)


def side_by_side(ref, count, rows):
    return jnp.concatenate([ref[g * rows : (g + 1) * rows] for g in range(count)], axis=1)


def edge_copies(sz, images_ref, scene_ref, edge, sides, sem, side_sem):
    places = (0, sz.width - LANES)
    copies = []
    for e in range(sz.local):
        for side in range(2):
            slot = 2 * e + side
            copies.append(
                pltpu.make_async_copy(
                    images_ref.at[e, :, pl.ds(places[side], LANES)], edge.at[slot], sem.at[slot]
                )
            )
    side_copies = [
        pltpu.make_async_copy(
            scene_ref.at[:, pl.ds(places[side], LANES)], sides.at[side], side_sem.at[side]
        )
        for side in range(2)
    ]
    return copies, side_copies


def pack_edges(sz, flags, edge, sides, copies, side_copies, first_ref, second_ref):
    epoch = lax.axis_index("epoch") * sz.local
    even = lax.axis_index("sky") % 2 == 0
    places = (0, sz.width - LANES)

    def put(left, right, rows):
        first_ref[rows] = jnp.where(even, right, left).astype(BF16)
        second_ref[rows] = jnp.where(even, left, right).astype(BF16)

    packs = [packing(sz.groups, HALO, shift) for shift in (0, LANES - HALO)]
    row, lane = iota((LANES, LANES), 0), iota((LANES, LANES), 1)
    repeats = [
        (row == low(lane, HALO) + shift).astype(F32).astype(BF16) for shift in (0, LANES - HALO)
    ]
    for copy in copies + side_copies:
        copy.wait()
    goods, rows_good = [], []
    for side in range(2):
        good = flags[:, places[side] : places[side] + LANES].astype(F32)
        rows_good.append(good)
        if side == 1:
            good = pltpu.roll(good, HALO, 1)
        if sz.mask_rows > sz.epochs:
            good = jnp.concatenate(
                [good, jnp.zeros((sz.mask_rows - sz.epochs, LANES), F32)], axis=0
            )
        goods.append(good)
    put(goods[0], goods[1], slice(sz.mask_at, sz.buffer_rows))
    for e in range(sz.local):
        lines = []
        for side in range(2):
            slot = 2 * e + side
            good = jnp.broadcast_to(row_of(rows_good[side], epoch + e), (HALO, LANES))
            good = dot(good.astype(BF16), repeats[side])[0:1]
            lines.append(dot(side_by_side(edge.at[slot], sz.groups, SPAN), packs[side]) * good)
        put(lines[0], lines[1], slice(SPAN * e, SPAN * (e + 1)))
    cells = []
    count = sz.rows // sz.part
    for side, shift in enumerate((0, LANES - RIM)):
        cells.append(
            dot(side_by_side(sides.at[side], count, sz.part), packing(count, RIM, shift))
        )
    put(cells[0], cells[1], slice(sz.scene_at, sz.mask_at))


def edges_kernel(sz, images_ref, scene_ref, mask_ref, first_ref, second_ref, *scratch):
    edge, sides, flags, sem, side_sem, flag_sem = scratch
    copies, side_copies = edge_copies(sz, images_ref, scene_ref, edge, sides, sem, side_sem)
    flag_copy = pltpu.make_async_copy(mask_ref, flags, flag_sem)
    for copy in [flag_copy] + copies + side_copies:
        copy.start()
    flag_copy.wait()
    pack_edges(sz, flags, edge, sides, copies, side_copies, first_ref, second_ref)


def edges(sz, images, scene, mask):
    shape = jax.ShapeDtypeStruct((sz.buffer_rows, LANES), BF16)
    return pl.pallas_call(
        functools.partial(edges_kernel, sz),
        out_shape=(shape, shape),
        in_specs=[HBM, HBM, HBM],
        out_specs=(VMEM, VMEM),
        scratch_shapes=[
            pltpu.VMEM((2 * sz.local, sz.height, LANES), BF16),
            pltpu.VMEM((2, sz.rows, LANES), BF16),
            pltpu.VMEM((sz.epochs, sz.width), jnp.int32),
            pltpu.SemaphoreType.DMA((2 * sz.local,)),
            pltpu.SemaphoreType.DMA((2,)),
            pltpu.SemaphoreType.DMA,
        ],
        compiler_params=WHOLE,
        cost_estimate=SHORT,
        name="edges",
    )(images, scene, mask)


def sides_of(first, second):
    even = lax.axis_index("sky") % 2 == 0
    return jnp.where(even, second, first), jnp.where(even, first, second)


def widen_rows(sz, scene_ref, first_ref, second_ref, start, count):
    group, inside = start // sz.part, start % sz.part
    cells = slice(sz.scene_at + inside, sz.scene_at + inside + count)
    row, lane = iota((LANES, sz.wide), 0), iota((LANES, sz.wide), 1)
    wide = dot(scene_ref[start : start + count], selection(sz.width, sz.wide, RIM))
    ends = sides_of(first_ref[cells], second_ref[cells])
    for end, at in zip(ends, (0, sz.width + RIM)):
        place = (high(row, RIM) == group) & (lane == low(row, RIM) + at)
        wide += dot(end, place.astype(F32).astype(BF16))
    return wide.astype(BF16)


def widen_kernel(sz, scene_ref, mask_ref, first_ref, second_ref, wide_ref, good_ref):
    for start in range(0, sz.rows, sz.part):
        wide_ref[start : start + sz.part] = widen_rows(
            sz, scene_ref, first_ref, second_ref, start, sz.part
        )
    flags = slice(sz.mask_at, sz.buffer_rows)
    before, after = sides_of(first_ref[flags], second_ref[flags])
    own = mask_ref[...].astype(F32)
    if sz.mask_rows > sz.epochs:
        own = jnp.concatenate(
            [own, jnp.zeros((sz.mask_rows - sz.epochs, sz.width), F32)], axis=0
        )
    good = dot(own.astype(BF16), selection(sz.width, sz.wide, HALO))
    inner = iota((LANES, sz.wide), 0) < HALO
    zero = jnp.zeros((LANES, sz.wide), BF16)
    good += dot(before, jnp.where(inner, selection(LANES, sz.wide, 0), zero))
    good += dot(after, jnp.where(inner, selection(LANES, sz.wide, sz.width + HALO), zero))
    good_ref[...] = good


def destination(slot, place):
    return (
        3 * (1 - place % 2),
        2 - place // 2,
        (2 * place + 1) % 5,
        place,
    )[slot]


def rim_rows(sz, epoch, e, coverage_ref, row_line, row_shift, twice, first_ref, second_ref):
    rows = slice(SPAN * e, SPAN * (e + 1))
    column = lax.axis_index("sky") * sz.width
    both = jnp.concatenate(sides_of(first_ref[rows], second_ref[rows]), axis=1)
    lane = iota((1, 2 * LANES), 1)
    factor = jnp.zeros((1, 2 * LANES), F32)
    for side, at in enumerate((column - HALO, column + sz.width)):
        for tile in range(sz.tile_rows):
            cover = cover_at(coverage_ref, epoch, tile, tile_of(at))
            here = high(lane, LANES) == side
            here &= high(low(lane, LANES), HALO * TILE // SPAN) == tile
            factor = jnp.where(here, cover, factor)
    both = both.astype(F32) * factor
    above = pltpu.roll(both[SPAN - HALO :], HALO, 1)
    below = pltpu.roll(both[:HALO], 2 * LANES - HALO, 1)
    above = jnp.where(low(lane, LANES) < HALO, 0.0, above)
    below = jnp.where(low(lane, LANES) >= HALO * (sz.groups - 1), 0.0, below)
    window = jnp.concatenate([above, both, below], axis=0).astype(BF16)
    table = toeplitz(row_line, row_shift - 4, SPAN, SPAN + LANES)[:, : SPAN + RIM]
    return (dot(table, window) * twice).astype(BF16)


def rim_columns(col_line, col_shift):
    enter = toeplitz(col_line, 28 - col_shift, HALO, SPAN)[:, :LANES]
    leave = toeplitz(col_line, SPAN + LANES - 116 - col_shift, HALO, SPAN + LANES)[:, :LANES]
    none = jnp.zeros((HALO, LANES), BF16)
    upper = [jnp.concatenate([enter, none], axis=1)] * (LANES // HALO)
    lower = [jnp.concatenate([none, leave], axis=1)] * (LANES // HALO)
    return jnp.concatenate(upper + lower, axis=0)


def rim_part(sz, start, rim_ref, table):
    group = start // SPAN
    row = iota((2 * LANES, SPAN), 0)
    parts = []
    for k in range(max(sz.rows // SPAN, 1)):
        picked = jnp.where(high(low(row, LANES), HALO) == group + k, table, jnp.zeros_like(table))
        if sz.rows >= SPAN:
            rows = rim_ref[...]
        else:
            rows = rim_ref[pl.ds(pl.multiple_of(start - group * SPAN, sz.rows), sz.rows)]
        parts.append(dot(rows, picked))
    return jnp.concatenate(parts, axis=0) if len(parts) > 1 else parts[0]


def rim_places(sz, h):
    row, lane = iota((SPAN, LANES), 0), iota((SPAN, LANES), 1)
    here = (lane == row + RIM * h) & (row < HALO)
    here |= (lane == row - SPAN + RIM * (h + 1)) & (row >= SPAN - HALO)
    return here.astype(F32).astype(BF16)


def rim_spread(sz, h):
    row, lane = iota((LANES, SPAN), 0), iota((LANES, SPAN), 1)
    here = (row == lane + RIM * h) & (lane < HALO)
    here |= (row == lane - SPAN + RIM * (h + 1)) & (lane >= SPAN - HALO)
    return here.astype(F32).astype(BF16)


def pack_rows(sz, ref, at, rim):
    ref[at : at + RIM] = rim[:, : sz.width]
    left = slice(at + RIM, at + RIM + HALO)
    ref[left, :LANES] = rim[:HALO, sz.width :]
    ref[left, LANES:SPAN] = rim[HALO:, sz.width :]
    ref[left, SPAN:] = jnp.zeros((HALO, sz.width - SPAN), BF16)


def pack_part(sz, ref, at, part):
    total = None
    for h in range(sz.rows // LANES):
        rows = part[h * LANES : (h + 1) * LANES].astype(BF16)
        moved = dot(rows, rim_places(sz, h))
        total = moved if total is None else total + moved
    total = total.astype(BF16)
    for k in range(LANES // RIM):
        ref[at : at + RIM, k * LANES : (k + 1) * LANES] = total[k * RIM : (k + 1) * RIM]


def unpack_rim(sz, ref, at):
    left = slice(at + RIM, at + RIM + HALO)
    rest = jnp.concatenate([ref[left, :LANES], ref[left, LANES:SPAN]], axis=0)
    return jnp.concatenate([ref[at : at + RIM], rest], axis=1)


def unpack_part(sz, ref, at):
    pieces = [ref[at : at + RIM, k * LANES : (k + 1) * LANES] for k in range(LANES // RIM)]
    packed = jnp.concatenate(pieces, axis=0)
    parts = [dot(packed, rim_spread(sz, h)) for h in range(sz.rows // LANES)]
    return jnp.concatenate(parts, axis=0)


def complete(sz, out, part):
    rows = slice(0, sz.rows)
    for at, cols in ((0, slice(0, LANES)), (LANES, slice(sz.width - LANES, sz.width))):
        value = out[rows, cols].astype(F32) + part[:, at : at + LANES]
        out[rows, cols] = value.astype(BF16)


def rim_parts_of(sz, slots, place, offsets_ref, col_lines, rim_ref):
    tables = []
    for e in range(sz.local):
        epoch = place * sz.local + e
        tables.append(rim_columns(row_of(col_lines[0], epoch), offsets_ref[1, epoch]))
    parts = []
    for slot in slots:
        part = None
        for e in range(sz.local):
            term = rim_part(sz, destination(slot, place) * sz.rows, rim_ref.at[e], tables[e])
            part = term if part is None else part + term
        parts.append(part)
    return parts


def notes_kernel(
    sz, coverage_ref, offsets_ref, weight_ref, scene_ref, first_ref, second_ref,
    psf_rows_ref, psf_cols_ref, far_out, rim_ref, part_out, row_lines, col_lines,
):
    place = lax.axis_index("epoch")
    outer = (place == 0) | (place == 3)
    load_taps(psf_rows_ref, row_lines, sz.epochs, sz.taps)
    load_taps(psf_cols_ref, col_lines, sz.epochs, sz.taps)
    for e in range(sz.local):
        epoch = place * sz.local + e
        rim_ref[e] = rim_rows(
            sz, epoch, e, coverage_ref, row_of(row_lines[1], epoch), offsets_ref[0, epoch],
            -2.0 * weight_ref[epoch], first_ref, second_ref,
        )
    parts = rim_parts_of(sz, (0, 1), place, offsets_ref, col_lines, rim_ref)
    top = widen_rows(sz, scene_ref, first_ref, second_ref, 0, RIM)
    bottom = widen_rows(sz, scene_ref, first_ref, second_ref, sz.rows - RIM, RIM)
    pack_rows(sz, far_out, 0, jnp.where(place < 2, bottom, top))
    pack_part(sz, far_out, RIM + HALO, jnp.where(outer, parts[0], parts[1]))
    part_out[...] = parts[1].astype(BF16)


def notes(sz, coverage, offsets, weight, scene, first, second, psf_rows, psf_cols):
    return pl.pallas_call(
        functools.partial(notes_kernel, sz),
        out_shape=(
            jax.ShapeDtypeStruct((2 * RIM + HALO, sz.width), BF16),
            jax.ShapeDtypeStruct((sz.local, SPAN, 2 * LANES), BF16),
            jax.ShapeDtypeStruct((sz.rows, SPAN), BF16),
        ),
        in_specs=[SMEM] * 3 + [VMEM] * 5,
        out_specs=(VMEM, VMEM, VMEM),
        scratch_shapes=[pltpu.VMEM((2, sz.tap_rows, LANES), F32)] * 2,
        compiler_params=PARAMS,
        cost_estimate=SHORT,
        name="notes",
    )(coverage, offsets, weight, scene, first, second, psf_rows, psf_cols)


def early_kernel(
    sz, offsets_ref, scene_ref, first_ref, second_ref, psf_cols_ref, rim_ref, three_ref,
    near_out, col_lines,
):
    place = lax.axis_index("epoch")
    load_taps(psf_cols_ref, col_lines, sz.epochs, sz.taps)
    (part,) = rim_parts_of(sz, (2,), place, offsets_ref, col_lines, rim_ref)
    top = widen_rows(sz, scene_ref, first_ref, second_ref, 0, RIM)
    bottom = widen_rows(sz, scene_ref, first_ref, second_ref, sz.rows - RIM, RIM)
    pack_rows(sz, near_out, sz.rows, jnp.where(place % 2 == 0, bottom, top))
    near_out[: sz.rows] = three_ref[...]
    complete(sz, near_out, part)


def early(sz, offsets, scene, first, second, psf_cols, rim, three):
    return pl.pallas_call(
        functools.partial(early_kernel, sz),
        out_shape=jax.ShapeDtypeStruct((sz.rows + RIM + HALO, sz.width), BF16),
        in_specs=[SMEM] + [VMEM] * 6,
        out_specs=VMEM,
        scratch_shapes=[pltpu.VMEM((2, sz.tap_rows, LANES), F32)],
        compiler_params=PARAMS,
        cost_estimate=SHORT,
        name="early",
    )(offsets, scene, first, second, psf_cols, rim, three)


def merge_kernel(sz, two_ref, near_ref, one_ref, part_ref, out_ref):
    place = lax.axis_index("epoch")
    outer = (place == 0) | (place == 3)

    @pl.when(outer)
    def _():
        out_ref[...] = two_ref[...]
        complete(sz, out_ref, part_ref[...].astype(F32))

    @pl.when(jnp.logical_not(outer))
    def _():
        total = near_ref[: sz.rows].astype(F32) + one_ref[...].astype(F32)
        out_ref[...] = total.astype(BF16)


def merge(sz, two, near, one, part):
    return pl.pallas_call(
        functools.partial(merge_kernel, sz),
        out_shape=jax.ShapeDtypeStruct((sz.rows, sz.width), BF16),
        in_specs=[VMEM] * 4,
        out_specs=VMEM,
        compiler_params=PARAMS,
        cost_estimate=SHORT,
        name="merge",
    )(two, near, one, part)


def finish_kernel(sz, offsets_ref, scene_ref, mask_ref, first_ref, second_ref, *more):
    if sz.blocks != 4:
        widen_kernel(sz, scene_ref, mask_ref, first_ref, second_ref, *more)
        return
    psf_cols_ref, rim_ref, own_ref, wide_ref, good_ref, back_out, own_out, col_lines, sem = more
    place = lax.axis_index("epoch")
    copy = pltpu.make_async_copy(own_ref, own_out, sem)
    copy.start()
    load_taps(psf_cols_ref, col_lines, sz.epochs, sz.taps)
    parts = rim_parts_of(sz, (0, 3), place, offsets_ref, col_lines, rim_ref)
    widen_kernel(sz, scene_ref, mask_ref, first_ref, second_ref, wide_ref, good_ref)
    top, bottom = wide_ref[:RIM], wide_ref[sz.rows - RIM :]
    pack_rows(sz, back_out, 0, jnp.where(place % 2 == 0, bottom, top))
    pack_part(sz, back_out, RIM + HALO, parts[0])
    copy.wait()
    complete(sz, own_out, parts[1])


def finish(sz, offsets, scene, mask, first, second, *more):
    full = jax.ShapeDtypeStruct((sz.rows, sz.width), BF16)
    shapes = [
        jax.ShapeDtypeStruct((sz.rows, sz.wide), BF16),
        jax.ShapeDtypeStruct((sz.mask_rows, sz.wide), F32),
    ]
    scratch = []
    if more:
        shapes += [jax.ShapeDtypeStruct((2 * RIM + HALO, sz.width), BF16), full]
        scratch = [pltpu.VMEM((2, sz.tap_rows, LANES), F32), pltpu.SemaphoreType.DMA]
    return pl.pallas_call(
        functools.partial(finish_kernel, sz),
        out_shape=tuple(shapes),
        in_specs=[SMEM] + [VMEM] * 4 + [VMEM, VMEM, HBM][: len(more)],
        out_specs=tuple([VMEM] * len(shapes)),
        scratch_shapes=scratch,
        compiler_params=PARAMS,
        cost_estimate=SHORT,
        name="finish",
    )(offsets, scene, mask, first, second, *more)


def image_kernel(sz, slots, rims, packs, images_ref, *more):
    count = 1 if slots is None else len(slots)
    small, ends, more = more[:6], more[6 : 6 + rims], more[6 + rims :]
    if packs:
        scene_ref, *more = more
    outs, more = more[:count], more[count:]
    if packs:
        first_out, second_out, edge, sides, edge_sem, side_sem, *more = more
    held, small_sem, more = more[:6], more[6], more[7:]
    coverage_ref, offsets_ref, weight_ref, mask_ref, psf_rows_ref, psf_cols_ref = held
    window, row_done, row_lines, col_lines, row_table, main_table, cross_table, rim_ref, sem = more
    place = lax.axis_index("epoch")
    first = place * sz.local
    column = lax.axis_index("sky") * sz.width
    if slots is None:
        targets = [pl.program_id(0)]
    else:
        targets = [destination(slot, place) for slot in slots]

    copies = []
    for i, target in enumerate(targets):
        start = target * sz.rows
        head = jnp.maximum(start - HALO, 0)
        foot = jnp.minimum(start + sz.rows, sz.height - HALO)
        for e in range(sz.local):
            for n, (source, at, length) in enumerate(
                ((start, HALO, sz.rows), (head, 0, HALO), (foot, HALO + sz.rows, HALO))
            ):
                copies.append(
                    pltpu.make_async_copy(
                        images_ref.at[e, pl.ds(pl.multiple_of(source, HALO), length), :],
                        window.at[i, e, pl.ds(at, length), :],
                        sem.at[i, e, n],
                    )
                )
    held_copies = [
        pltpu.make_async_copy(source, target, small_sem.at[n])
        for n, (source, target) in enumerate(zip(small, held))
    ]
    for copy in held_copies + copies:
        copy.start()
    if packs:
        edge_waits = edge_copies(sz, images_ref, scene_ref, edge, sides, edge_sem, side_sem)
    for copy in held_copies:
        copy.wait()
    load_taps(psf_rows_ref, row_lines, sz.epochs, sz.taps)
    load_taps(psf_cols_ref, col_lines, sz.epochs, sz.taps)
    for e in range(sz.local):
        epoch = first + e
        row_shift, col_shift = offsets_ref[0, epoch], offsets_ref[1, epoch]
        row_table[e] = toeplitz(row_of(row_lines[1], epoch), row_shift - 4, STEP, SPAN)
        line = row_of(col_lines[0], epoch)
        main = toeplitz(line, 12 - col_shift, SPAN, SPAN + LANES)[:, :SPAN]
        main_table[e] = main
        apart = (iota((SPAN, SPAN), 0) < LANES) != (iota((SPAN, SPAN), 1) < LANES)
        cross_table[e] = jnp.where(apart, main, jnp.zeros_like(main))
    rim_parts = []
    for e in range(sz.local if rims else 0):
        epoch = first + e
        rim_ref[e] = rim_rows(
            sz, epoch, e, coverage_ref, row_of(row_lines[1], epoch), offsets_ref[0, epoch],
            -2.0 * weight_ref[epoch], *ends,
        )
        table = rim_columns(row_of(col_lines[0], epoch), offsets_ref[1, epoch])
        for i, target in enumerate(targets):
            part = rim_part(sz, target * sz.rows, rim_ref.at[e], table)
            if e == 0:
                rim_parts.append(part)
            else:
                rim_parts[i] += part
    column_tile = column // TILE
    for i, target in enumerate(targets):
        for copy in copies[3 * sz.local * i : 3 * sz.local * (i + 1)]:
            copy.wait()
        for copy in edge_waits[0] + edge_waits[1] if packs and i == 0 else ():
            copy.start()
        start = target * sz.rows
        zones = (
            (0, HALO, tile_of(start - HALO)),
            (HALO, HALO + sz.rows, tile_of(start)),
            (HALO + sz.rows, RIM + sz.rows, tile_of(start + sz.rows)),
        )
        for e in range(sz.local):
            epoch = first + e
            good = row_of(mask_ref[...].astype(F32), epoch)
            for begin, end, tile in zones:
                factor = good * cover_at(coverage_ref, epoch, tile, column_tile)
                window[i, e, begin:end] = window[i, e, begin:end] * factor.astype(BF16)
            twice = -2.0 * weight_ref[epoch]
            for s, n in spans(sz.rows):
                part = dot(row_table[e, :n, : n + RIM], window[i, e, s : s + n + RIM])
                row_done[i, e, s : s + n] = (part * twice).astype(BF16)
    for i in range(count):
        total = []
        for b in range(0, sz.width, SPAN):
            out = None
            for e in range(sz.local):
                part = dot(row_done[i, e, :, b : b + SPAN], main_table[e])
                out = part if out is None else out + part
            total += [out[:, :LANES], out[:, LANES:]]
        for b in range(LANES, sz.width - LANES, SPAN):
            out = None
            for e in range(sz.local):
                part = dot(row_done[i, e, :, b : b + SPAN], cross_table[e])
                out = part if out is None else out + part
            total[b // LANES] += out[:, :LANES]
            total[b // LANES + 1] += out[:, LANES:]
        if rims:
            total[0] += rim_parts[i][:, :LANES]
            total[-1] += rim_parts[i][:, LANES:]
        for k, piece in enumerate(total):
            outs[i][:, k * LANES : (k + 1) * LANES] = piece.astype(BF16)
    if packs:
        pack_edges(sz, mask_ref, edge, sides, *edge_waits, first_out, second_out)


def image_blocks(
    sz, slots, coverage, offsets, weight, images, mask, psf_rows, psf_cols, *ends, scene=None
):
    packs = scene is not None
    if slots is None:
        count = 1
        grid = dict(
            grid=(sz.blocks,),
            out_shape=jax.ShapeDtypeStruct((sz.blocks * sz.rows, sz.width), BF16),
            out_specs=pl.BlockSpec((sz.rows, sz.width), lambda i: (i, 0)),
        )
    else:
        count = len(slots)
        shapes = [jax.ShapeDtypeStruct((sz.rows, sz.width), BF16)] * count
        if packs:
            shapes += [jax.ShapeDtypeStruct((sz.buffer_rows, LANES), BF16)] * 2
        grid = dict(out_shape=tuple(shapes), out_specs=tuple([VMEM] * len(shapes)))
    pack_scratch = [
        pltpu.VMEM((2 * sz.local, sz.height, LANES), BF16),
        pltpu.VMEM((2, sz.rows, LANES), BF16),
        pltpu.SemaphoreType.DMA((2 * sz.local,)),
        pltpu.SemaphoreType.DMA((2,)),
    ]
    return pl.pallas_call(
        functools.partial(image_kernel, sz, slots, len(ends), packs),
        in_specs=[HBM] * 7 + [VMEM] * len(ends) + [HBM] * packs,
        scratch_shapes=pack_scratch * packs
        + [
            pltpu.SMEM(coverage.shape, jnp.int32),
            pltpu.SMEM(offsets.shape, jnp.int32),
            pltpu.SMEM(weight.shape, F32),
            pltpu.VMEM(mask.shape, jnp.int32),
            pltpu.VMEM(psf_rows.shape, BF16),
            pltpu.VMEM(psf_cols.shape, BF16),
            pltpu.SemaphoreType.DMA((6,)),
            pltpu.VMEM((count, sz.local, sz.rows + RIM, sz.width), BF16),
            pltpu.VMEM((count, sz.local, sz.rows, sz.width), BF16),
            pltpu.VMEM((2, sz.tap_rows, LANES), F32),
            pltpu.VMEM((2, sz.tap_rows, LANES), F32),
            pltpu.VMEM((sz.local, STEP, SPAN), BF16),
            pltpu.VMEM((sz.local, SPAN, SPAN), BF16),
            pltpu.VMEM((sz.local, SPAN, SPAN), BF16),
            pltpu.VMEM((sz.local, SPAN, 2 * LANES), BF16),
            pltpu.SemaphoreType.DMA((count, sz.local, 3)),
        ],
        compiler_params=WHOLE if slots is not None and 0 in slots else PARAMS,
        cost_estimate=SHORT,
        name="image_blocks",
        **grid,
    )(images, coverage, offsets, weight, mask, psf_rows, psf_cols, *ends, *([scene] * packs))


def column_tables(taps, start):
    pair = toeplitz(taps, start, LANES, SPAN)
    here, past = pair[:, :LANES], pair[:, LANES:]
    none = jnp.zeros_like(here)
    main = jnp.concatenate(
        [jnp.concatenate([here, none], axis=1), jnp.concatenate([past, here], axis=1)], axis=0
    )
    rest = jnp.concatenate(
        [jnp.concatenate([past, none], axis=1), jnp.concatenate([none, past], axis=1)], axis=0
    )
    return main, rest, here, past


def column_pass(sz, source, tables, tail):
    main, rest, here, past = tables
    tiles = []
    for b in range(0, sz.width, SPAN):
        out = dot(source[:, b : b + SPAN], main)
        tiles += [out[:, :LANES], out[:, LANES:]]
    ends = list(range(SPAN, sz.wide, SPAN))
    if len(ends) == 2:
        joined = jnp.concatenate([source[:, at : at + LANES] for at in ends], axis=1)
        out = dot(joined, rest)
        parts = [out[:, :LANES], out[:, LANES:]]
    else:
        parts = [dot(source[:, at : at + LANES], past) for at in ends]
    for at, part in zip(ends, parts):
        tiles[at // LANES - 1] += part
    if tail:
        tiles.append(dot(source[:, sz.width : sz.wide], here))
    return tiles


def model_kernel(
    sz, batch, coverage_ref, offsets_ref, weight_ref,
    wide_ref, good_ref, psf_rows_ref, psf_cols_ref, *more,
):
    *extra, out_ref, scene, lifted, residual, pulled, row_lines, col_lines = more
    step = pl.program_id(0)
    place = lax.axis_index("epoch")
    start = place * sz.rows
    column = lax.axis_index("sky") * sz.width

    @pl.when(step == 0)
    def _():
        load_taps(psf_rows_ref, row_lines, sz.epochs, sz.taps)
        load_taps(psf_cols_ref, col_lines, sz.epochs, sz.taps)
        scene[RIM : RIM + sz.rows] = wide_ref[...]
        if sz.blocks != 4:
            head_ref, foot_ref, base_ref = extra
            scene[0:RIM] = head_ref[...]
            scene[RIM + sz.rows :] = foot_ref[...]
            out_ref[...] = base_ref[...]
        else:
            own_ref, one_ref, two_ref, three_ref, back_ref, far_ref = extra
            outer = (place == 0) | (place == 3)
            near = jnp.where(
                outer, unpack_rim(sz, back_ref, 0), unpack_rim(sz, three_ref, sz.rows)
            )
            far = unpack_rim(sz, far_ref, 0)
            none = jnp.zeros_like(near)
            odd = place % 2 == 1
            scene[0:RIM] = jnp.where(odd, near, jnp.where(outer, none, far))
            scene[RIM + sz.rows :] = jnp.where(odd, jnp.where(outer, none, far), near)
            rows = slice(RIM + HALO, 2 * RIM + HALO)
            fix = unpack_part(sz, back_ref[rows], 0) + unpack_part(sz, far_ref[rows], 0)
            for b in range(0, sz.width, LANES):
                cols = slice(b, b + LANES)
                inner = two_ref[:, cols].astype(F32) + three_ref[: sz.rows, cols].astype(F32)
                base = jnp.where(outer, one_ref[:, cols].astype(F32), inner)
                base += own_ref[:, cols].astype(F32)
                for at, side in ((0, 0), (LANES, sz.width - LANES)):
                    if b == side:
                        base += fix[:, at : at + LANES]
                out_ref[:, cols] = base

    epochs = [step * batch + n for n in range(batch)]
    edge = sz.rows + HALO
    for n, epoch in enumerate(epochs):
        row_in = toeplitz(row_of(row_lines[0], epoch), -4 - offsets_ref[0, epoch], STEP, SPAN)
        for s, count in spans(sz.rows + RIM):
            lifted[n, s : s + count] = dot(
                row_in[:count, : count + RIM], scene[s : s + count + RIM]
            ).astype(BF16)
    for n, epoch in enumerate(epochs):
        good = row_of(good_ref[...], epoch) * (2.0 * weight_ref[epoch])
        lane = iota((1, sz.wide), 1)
        factors = []
        for row_tile in (tile_of(start - HALO), tile_of(start), tile_of(start + sz.rows)):
            left, here, right = (
                cover_at(coverage_ref, epoch, row_tile, tile_of(c))
                for c in (column - HALO, column, column + sz.width)
            )
            factors.append(
                good * jnp.where(lane < HALO, left, jnp.where(lane < HALO + sz.width, here, right))
            )
        tables = column_tables(row_of(col_lines[1], epoch), 28 + offsets_ref[1, epoch])
        for k, modeled in enumerate(column_pass(sz, lifted[n], tables, True)):
            b = k * LANES
            head, mid, foot = (f[:, b : b + LANES] for f in factors)
            residual[n, 0:HALO, b : b + LANES] = (modeled[0:HALO] * head).astype(BF16)
            residual[n, HALO:edge, b : b + LANES] = (modeled[HALO:edge] * mid).astype(BF16)
            residual[n, edge:, b : b + LANES] = (modeled[edge:] * foot).astype(BF16)
    for n, epoch in enumerate(epochs):
        tables = column_tables(row_of(col_lines[0], epoch), 28 - offsets_ref[1, epoch])
        for k, tile in enumerate(column_pass(sz, residual[n], tables, False)):
            pulled[n, :, k * LANES : (k + 1) * LANES] = tile.astype(BF16)
    row_outs = [
        toeplitz(row_of(row_lines[1], epoch), offsets_ref[0, epoch] - 4, STEP, SPAN)
        for epoch in epochs
    ]
    for s, count in spans(sz.rows):
        total = out_ref[s : s + count]
        for n in range(batch):
            total += dot(row_outs[n][:count, : count + RIM], pulled[n, s : s + count + RIM])
        out_ref[s : s + count] = total


def model_term(sz, coverage, offsets, weight, wide, good, psf_rows, psf_cols, *extra):
    high = sz.rows + RIM
    batch = 8 if sz.epochs % 8 == 0 else 1
    return pl.pallas_call(
        functools.partial(model_kernel, sz, batch),
        grid=(sz.epochs // batch,),
        out_shape=jax.ShapeDtypeStruct((sz.rows, sz.width), F32),
        in_specs=[SMEM] * 3 + [VMEM] * (4 + len(extra)),
        out_specs=VMEM,
        scratch_shapes=[
            pltpu.VMEM((sz.rows + 2 * RIM, sz.wide), BF16),
            pltpu.VMEM((batch, high, sz.wide), BF16),
            pltpu.VMEM((batch, high, sz.wide), BF16),
            pltpu.VMEM((batch, high, sz.width), BF16),
            pltpu.VMEM((2, sz.tap_rows, LANES), F32),
            pltpu.VMEM((2, sz.tap_rows, LANES), F32),
        ],
        compiler_params=PARAMS,
        cost_estimate=SHORT,
        name="model_term",
    )(coverage, offsets, weight, wide, good, psf_rows, psf_cols, *extra)


def on_device(sky_scene, images, psf_rows, psf_cols, offsets, epoch_weight, column_mask, coverage):
    sz = Sizes(images, sky_scene, psf_rows)
    peers = lax.axis_size("sky")
    depth = lax.axis_size("epoch")
    scalars = (jnp.transpose(coverage, (1, 2, 0)), offsets.T, epoch_weight)
    profiles = (psf_rows, psf_cols)

    def pairs(start, count):
        return [p for i in range(start, count - 1, 2) for p in ((i, i + 1), (i + 1, i))]

    def blocks(slots, shifts, *ends, scene=None):
        return image_blocks(
            sz, slots, scalars[0], shifts, epoch_weight, images, column_mask, *profiles, *ends,
            scene=scene,
        )

    if depth == 4:
        one, two, first, second = blocks((0, 1), scalars[1], scene=sky_scene)
        got_one = lax.ppermute(one, "epoch", pairs(0, depth))
        got_two = lax.ppermute(two, "epoch", pairs(1, depth))
        shifts, one = lax.optimization_barrier((scalars[1], one))
        three, own = blocks((2, 3), shifts)
        first = lax.ppermute(first, "sky", pairs(0, peers))
        second = lax.ppermute(second, "sky", pairs(1, peers))
        second, three = lax.optimization_barrier((second, three))
        far, rim, part = notes(sz, *scalars, sky_scene, first, second, *profiles)
        near = early(sz, scalars[1], sky_scene, first, second, psf_cols, rim, three)
        got_three = lax.ppermute(near, "epoch", [(0, 1), (3, 2)])
        got_far = lax.ppermute(far, "epoch", [(0, 3), (3, 0), (1, 2), (2, 1)])
        passed = merge(sz, two, near, got_one, part)
        passed, got_far, got_two, rim = lax.optimization_barrier((passed, got_far, got_two, rim))
        got_passed = lax.ppermute(passed, "epoch", [(0, 2), (3, 1), (1, 3), (2, 0)])
        wide, good, back, own = finish(
            sz, scalars[1], sky_scene, column_mask, first, second, psf_cols, rim, own
        )
        got_back = lax.ppermute(back, "epoch", [(1, 0), (2, 3)])
        model = model_term(
            sz, *scalars, wide, good, *profiles,
            own, got_one, got_two, got_three, got_back, got_far,
        )
        return model + got_passed.astype(F32)

    first, second = edges(sz, images, sky_scene, column_mask)
    first = lax.ppermute(first, "sky", pairs(0, peers))
    second = lax.ppermute(second, "sky", pairs(1, peers))
    downward = [(i, i + 1) for i in range(depth - 1)]
    upward = [(i + 1, i) for i in range(depth - 1)]
    wide, good = finish(sz, scalars[1], sky_scene, column_mask, first, second)
    head = lax.ppermute(wide[-RIM:], "epoch", downward)
    foot = lax.ppermute(wide[:RIM], "epoch", upward)
    terms = blocks(None, scalars[1], first, second).astype(F32)
    base = lax.psum_scatter(terms, "epoch", scatter_dimension=0, tiled=True)
    return model_term(sz, *scalars, wide, good, *profiles, head, foot, base)


def solution(mesh):
    return jax.shard_map(
        on_device,
        mesh=mesh,
        in_specs=(
            P(("field", "epoch"), "sky"),
            P(("field", "epoch"), None, "sky"),
            P("field", None),
            P("field", None),
            P("field", None),
            P("field"),
            P("field", "sky"),
            P("field", None, None),
        ),
        out_specs=P(("field", "epoch"), "sky"),
        check_vma=False,
    )
```

```python
import functools

import jax
import jax.numpy as jnp
from jax import lax
from jax.experimental import pallas as pl
from jax.experimental.pallas import tpu as pltpu
from jax.sharding import PartitionSpec as P

TILE = 512
HALO = 16
RIM = 2 * HALO
LANES = 128
SPAN = 256
STEP = SPAN - RIM
F32 = jnp.float32
BF16 = jnp.bfloat16
VMEM = pl.BlockSpec(memory_space=pltpu.VMEM)
SMEM = pl.BlockSpec(memory_space=pltpu.SMEM)
HBM = pl.BlockSpec(memory_space=pltpu.HBM)
PARAMS = pltpu.CompilerParams(vmem_limit_bytes=40 * 1024 * 1024)
SHORT = pl.CostEstimate(flops=1000, bytes_accessed=1000, transcendentals=0)
WHOLE = pltpu.CompilerParams(vmem_limit_bytes=59 * 1024 * 1024)


def up_to(value, unit):
    return -(-value // unit) * unit


def dot(a, b, dims=((1,), (0,))):
    return lax.dot_general(a, b, (dims, ((), ())), preferred_element_type=F32)


def iota(shape, dim):
    return lax.broadcasted_iota(jnp.int32, shape, dim)


def selection(rows, cols, shift):
    return (iota((rows, cols), 1) == iota((rows, cols), 0) + shift).astype(BF16)


def toeplitz(taps, start, rows, width):
    line = jnp.concatenate([taps, jnp.zeros((1, width - LANES), F32)], axis=1)
    line = jnp.broadcast_to(line, (8, width))
    line = pltpu.roll(line, lax.rem(2 * width - start, width), 1)[0:1]
    line = jnp.broadcast_to(line, (rows, width))
    return pltpu.roll(line, 0, 1, stride=1, stride_axis=0).astype(BF16)


def row_of(values, index):
    return jnp.sum(jnp.where(iota(values.shape, 0) == index, values, 0), axis=0, keepdims=True)


def load_taps(psf_ref, lines, epochs, taps):
    lines[0] = jnp.zeros(lines.shape[1:], F32)
    lines[0, :epochs, :taps] = psf_ref[...].astype(F32)
    mirror = iota((LANES, LANES), 0) + iota((LANES, LANES), 1) == taps - 1
    lines[1] = dot(lines[0].astype(BF16), mirror.astype(F32).astype(BF16))


def spans(length):
    return [(s, min(STEP, length - s)) for s in range(0, length, STEP)]


class Sizes:
    def __init__(self, images, sky_scene, psf_rows):
        self.local, self.height, self.width = images.shape
        self.rows = sky_scene.shape[0]
        self.epochs = psf_rows.shape[0]
        self.taps = psf_rows.shape[1]
        self.tile_rows = self.height // TILE
        self.wide = self.width + LANES
        self.groups = self.height // SPAN
        self.part = min(self.rows, SPAN)
        self.mask_rows = up_to(self.epochs, HALO)
        self.scene_at = SPAN * self.local
        self.mask_at = self.scene_at + self.part
        self.buffer_rows = self.mask_at + self.mask_rows
        self.blocks = self.height // self.rows
        self.tap_rows = self.mask_rows


def cover_at(coverage_ref, epoch, row_tile, col_tile):
    last_row = coverage_ref.shape[0] - 1
    last_col = coverage_ref.shape[1] - 1
    inside = (row_tile >= 0) & (row_tile <= last_row) & (col_tile >= 0) & (col_tile <= last_col)
    value = coverage_ref[jnp.clip(row_tile, 0, last_row), jnp.clip(col_tile, 0, last_col), epoch]
    return jnp.where(inside, value, 0).astype(F32)


def tile_of(position):
    return (position + TILE) // TILE - 1


def low(index, size):
    return index & (size - 1)


def high(index, size):
    return lax.shift_right_logical(index, size.bit_length() - 1)


def packing(count, width, shift):
    row, lane = iota((LANES * count, LANES), 0), iota((LANES * count, LANES), 1)
    here = high(lane, width) == high(row, LANES)
    here &= low(row, LANES) == low(lane, width) + shift
    return here.astype(F32).astype(BF16)


def side_by_side(ref, count, rows):
    return jnp.concatenate([ref[g * rows : (g + 1) * rows] for g in range(count)], axis=1)


def edge_copies(sz, images_ref, scene_ref, edge, sides, sem, side_sem):
    places = (0, sz.width - LANES)
    copies = []
    for e in range(sz.local):
        for side in range(2):
            slot = 2 * e + side
            copies.append(
                pltpu.make_async_copy(
                    images_ref.at[e, :, pl.ds(places[side], LANES)], edge.at[slot], sem.at[slot]
                )
            )
    side_copies = [
        pltpu.make_async_copy(
            scene_ref.at[:, pl.ds(places[side], LANES)], sides.at[side], side_sem.at[side]
        )
        for side in range(2)
    ]
    return copies, side_copies


def pack_edges(sz, flags, edge, sides, copies, side_copies, first_ref, second_ref):
    epoch = lax.axis_index("epoch") * sz.local
    even = lax.axis_index("sky") % 2 == 0
    places = (0, sz.width - LANES)

    def put(left, right, rows):
        first_ref[rows] = jnp.where(even, right, left).astype(BF16)
        second_ref[rows] = jnp.where(even, left, right).astype(BF16)

    packs = [packing(sz.groups, HALO, shift) for shift in (0, LANES - HALO)]
    row, lane = iota((LANES, LANES), 0), iota((LANES, LANES), 1)
    repeats = [
        (row == low(lane, HALO) + shift).astype(F32).astype(BF16) for shift in (0, LANES - HALO)
    ]
    for copy in copies + side_copies:
        copy.wait()
    goods, rows_good = [], []
    for side in range(2):
        good = flags[:, places[side] : places[side] + LANES].astype(F32)
        rows_good.append(good)
        if side == 1:
            good = pltpu.roll(good, HALO, 1)
        if sz.mask_rows > sz.epochs:
            good = jnp.concatenate(
                [good, jnp.zeros((sz.mask_rows - sz.epochs, LANES), F32)], axis=0
            )
        goods.append(good)
    put(goods[0], goods[1], slice(sz.mask_at, sz.buffer_rows))
    for e in range(sz.local):
        lines = []
        for side in range(2):
            slot = 2 * e + side
            good = jnp.broadcast_to(row_of(rows_good[side], epoch + e), (HALO, LANES))
            good = dot(good.astype(BF16), repeats[side])[0:1]
            lines.append(dot(side_by_side(edge.at[slot], sz.groups, SPAN), packs[side]) * good)
        put(lines[0], lines[1], slice(SPAN * e, SPAN * (e + 1)))
    cells = []
    count = sz.rows // sz.part
    for side, shift in enumerate((0, LANES - RIM)):
        cells.append(
            dot(side_by_side(sides.at[side], count, sz.part), packing(count, RIM, shift))
        )
    put(cells[0], cells[1], slice(sz.scene_at, sz.mask_at))


def edges_kernel(sz, images_ref, scene_ref, mask_ref, first_ref, second_ref, *scratch):
    edge, sides, flags, sem, side_sem, flag_sem = scratch
    copies, side_copies = edge_copies(sz, images_ref, scene_ref, edge, sides, sem, side_sem)
    flag_copy = pltpu.make_async_copy(mask_ref, flags, flag_sem)
    for copy in [flag_copy] + copies + side_copies:
        copy.start()
    flag_copy.wait()
    pack_edges(sz, flags, edge, sides, copies, side_copies, first_ref, second_ref)


def edges(sz, images, scene, mask):
    shape = jax.ShapeDtypeStruct((sz.buffer_rows, LANES), BF16)
    return pl.pallas_call(
        functools.partial(edges_kernel, sz),
        out_shape=(shape, shape),
        in_specs=[HBM, HBM, HBM],
        out_specs=(VMEM, VMEM),
        scratch_shapes=[
            pltpu.VMEM((2 * sz.local, sz.height, LANES), BF16),
            pltpu.VMEM((2, sz.rows, LANES), BF16),
            pltpu.VMEM((sz.epochs, sz.width), jnp.int32),
            pltpu.SemaphoreType.DMA((2 * sz.local,)),
            pltpu.SemaphoreType.DMA((2,)),
            pltpu.SemaphoreType.DMA,
        ],
        compiler_params=WHOLE,
        cost_estimate=SHORT,
        name="edges",
    )(images, scene, mask)


def sides_of(first, second):
    even = lax.axis_index("sky") % 2 == 0
    return jnp.where(even, second, first), jnp.where(even, first, second)


def widen_rows(sz, scene_ref, first_ref, second_ref, start, count):
    group, inside = start // sz.part, start % sz.part
    cells = slice(sz.scene_at + inside, sz.scene_at + inside + count)
    row, lane = iota((LANES, sz.wide), 0), iota((LANES, sz.wide), 1)
    wide = dot(scene_ref[start : start + count], selection(sz.width, sz.wide, RIM))
    ends = sides_of(first_ref[cells], second_ref[cells])
    for end, at in zip(ends, (0, sz.width + RIM)):
        place = (high(row, RIM) == group) & (lane == low(row, RIM) + at)
        wide += dot(end, place.astype(F32).astype(BF16))
    return wide.astype(BF16)


def widen_kernel(sz, scene_ref, mask_ref, first_ref, second_ref, wide_ref, good_ref):
    for start in range(0, sz.rows, sz.part):
        wide_ref[start : start + sz.part] = widen_rows(
            sz, scene_ref, first_ref, second_ref, start, sz.part
        )
    flags = slice(sz.mask_at, sz.buffer_rows)
    before, after = sides_of(first_ref[flags], second_ref[flags])
    own = mask_ref[...].astype(F32)
    if sz.mask_rows > sz.epochs:
        own = jnp.concatenate(
            [own, jnp.zeros((sz.mask_rows - sz.epochs, sz.width), F32)], axis=0
        )
    good = dot(own.astype(BF16), selection(sz.width, sz.wide, HALO))
    inner = iota((LANES, sz.wide), 0) < HALO
    zero = jnp.zeros((LANES, sz.wide), BF16)
    good += dot(before, jnp.where(inner, selection(LANES, sz.wide, 0), zero))
    good += dot(after, jnp.where(inner, selection(LANES, sz.wide, sz.width + HALO), zero))
    good_ref[...] = good


def destination(slot, place):
    return (
        3 * (1 - place % 2),
        2 - place // 2,
        (2 * place + 1) % 5,
        place,
    )[slot]


def rim_rows(sz, epoch, e, coverage_ref, row_line, row_shift, twice, first_ref, second_ref):
    rows = slice(SPAN * e, SPAN * (e + 1))
    column = lax.axis_index("sky") * sz.width
    both = jnp.concatenate(sides_of(first_ref[rows], second_ref[rows]), axis=1)
    lane = iota((1, 2 * LANES), 1)
    factor = jnp.zeros((1, 2 * LANES), F32)
    for side, at in enumerate((column - HALO, column + sz.width)):
        for tile in range(sz.tile_rows):
            cover = cover_at(coverage_ref, epoch, tile, tile_of(at))
            here = high(lane, LANES) == side
            here &= high(low(lane, LANES), HALO * TILE // SPAN) == tile
            factor = jnp.where(here, cover, factor)
    both = both.astype(F32) * factor
    above = pltpu.roll(both[SPAN - HALO :], HALO, 1)
    below = pltpu.roll(both[:HALO], 2 * LANES - HALO, 1)
    above = jnp.where(low(lane, LANES) < HALO, 0.0, above)
    below = jnp.where(low(lane, LANES) >= HALO * (sz.groups - 1), 0.0, below)
    window = jnp.concatenate([above, both, below], axis=0).astype(BF16)
    table = toeplitz(row_line, row_shift - 4, SPAN, SPAN + LANES)[:, : SPAN + RIM]
    return (dot(table, window) * twice).astype(BF16)


def rim_columns(col_line, col_shift):
    enter = toeplitz(col_line, 28 - col_shift, HALO, SPAN)[:, :LANES]
    leave = toeplitz(col_line, SPAN + LANES - 116 - col_shift, HALO, SPAN + LANES)[:, :LANES]
    none = jnp.zeros((HALO, LANES), BF16)
    upper = [jnp.concatenate([enter, none], axis=1)] * (LANES // HALO)
    lower = [jnp.concatenate([none, leave], axis=1)] * (LANES // HALO)
    return jnp.concatenate(upper + lower, axis=0)


def rim_part(sz, start, rim_ref, table):
    group = start // SPAN
    row = iota((2 * LANES, SPAN), 0)
    parts = []
    for k in range(max(sz.rows // SPAN, 1)):
        picked = jnp.where(high(low(row, LANES), HALO) == group + k, table, jnp.zeros_like(table))
        if sz.rows >= SPAN:
            rows = rim_ref[...]
        else:
            rows = rim_ref[pl.ds(pl.multiple_of(start - group * SPAN, sz.rows), sz.rows)]
        parts.append(dot(rows, picked))
    return jnp.concatenate(parts, axis=0) if len(parts) > 1 else parts[0]


def rim_places(sz, h):
    row, lane = iota((SPAN, LANES), 0), iota((SPAN, LANES), 1)
    here = (lane == row + RIM * h) & (row < HALO)
    here |= (lane == row - SPAN + RIM * (h + 1)) & (row >= SPAN - HALO)
    return here.astype(F32).astype(BF16)


def rim_spread(sz, h):
    row, lane = iota((LANES, SPAN), 0), iota((LANES, SPAN), 1)
    here = (row == lane + RIM * h) & (lane < HALO)
    here |= (row == lane - SPAN + RIM * (h + 1)) & (lane >= SPAN - HALO)
    return here.astype(F32).astype(BF16)


def pack_rows(sz, ref, at, rim):
    ref[at : at + RIM] = rim[:, : sz.width]
    left = slice(at + RIM, at + RIM + HALO)
    ref[left, :LANES] = rim[:HALO, sz.width :]
    ref[left, LANES:SPAN] = rim[HALO:, sz.width :]
    ref[left, SPAN:] = jnp.zeros((HALO, sz.width - SPAN), BF16)


def pack_part(sz, ref, at, part):
    total = None
    for h in range(sz.rows // LANES):
        rows = part[h * LANES : (h + 1) * LANES].astype(BF16)
        moved = dot(rows, rim_places(sz, h))
        total = moved if total is None else total + moved
    total = total.astype(BF16)
    for k in range(LANES // RIM):
        ref[at : at + RIM, k * LANES : (k + 1) * LANES] = total[k * RIM : (k + 1) * RIM]


def unpack_rim(sz, ref, at):
    left = slice(at + RIM, at + RIM + HALO)
    rest = jnp.concatenate([ref[left, :LANES], ref[left, LANES:SPAN]], axis=0)
    return jnp.concatenate([ref[at : at + RIM], rest], axis=1)


def unpack_part(sz, ref, at):
    pieces = [ref[at : at + RIM, k * LANES : (k + 1) * LANES] for k in range(LANES // RIM)]
    packed = jnp.concatenate(pieces, axis=0)
    parts = [dot(packed, rim_spread(sz, h)) for h in range(sz.rows // LANES)]
    return jnp.concatenate(parts, axis=0)


def complete(sz, out, part):
    rows = slice(0, sz.rows)
    for at, cols in ((0, slice(0, LANES)), (LANES, slice(sz.width - LANES, sz.width))):
        value = out[rows, cols].astype(F32) + part[:, at : at + LANES]
        out[rows, cols] = value.astype(BF16)


def rim_parts_of(sz, slots, place, offsets_ref, col_lines, rim_ref):
    tables = []
    for e in range(sz.local):
        epoch = place * sz.local + e
        tables.append(rim_columns(row_of(col_lines[0], epoch), offsets_ref[1, epoch]))
    parts = []
    for slot in slots:
        part = None
        for e in range(sz.local):
            term = rim_part(sz, destination(slot, place) * sz.rows, rim_ref.at[e], tables[e])
            part = term if part is None else part + term
        parts.append(part)
    return parts


def notes_kernel(
    sz, coverage_ref, offsets_ref, weight_ref, scene_ref, first_ref, second_ref,
    psf_rows_ref, psf_cols_ref, far_out, rim_ref, part_out, row_lines, col_lines,
):
    place = lax.axis_index("epoch")
    outer = (place == 0) | (place == 3)
    load_taps(psf_rows_ref, row_lines, sz.epochs, sz.taps)
    load_taps(psf_cols_ref, col_lines, sz.epochs, sz.taps)
    for e in range(sz.local):
        epoch = place * sz.local + e
        rim_ref[e] = rim_rows(
            sz, epoch, e, coverage_ref, row_of(row_lines[1], epoch), offsets_ref[0, epoch],
            -2.0 * weight_ref[epoch], first_ref, second_ref,
        )
    parts = rim_parts_of(sz, (0, 1), place, offsets_ref, col_lines, rim_ref)
    top = widen_rows(sz, scene_ref, first_ref, second_ref, 0, RIM)
    bottom = widen_rows(sz, scene_ref, first_ref, second_ref, sz.rows - RIM, RIM)
    pack_rows(sz, far_out, 0, jnp.where(place < 2, bottom, top))
    pack_part(sz, far_out, RIM + HALO, jnp.where(outer, parts[0], parts[1]))
    part_out[...] = parts[1].astype(BF16)


def notes(sz, coverage, offsets, weight, scene, first, second, psf_rows, psf_cols):
    return pl.pallas_call(
        functools.partial(notes_kernel, sz),
        out_shape=(
            jax.ShapeDtypeStruct((2 * RIM + HALO, sz.width), BF16),
            jax.ShapeDtypeStruct((sz.local, SPAN, 2 * LANES), BF16),
            jax.ShapeDtypeStruct((sz.rows, SPAN), BF16),
        ),
        in_specs=[SMEM] * 3 + [VMEM] * 5,
        out_specs=(VMEM, VMEM, VMEM),
        scratch_shapes=[pltpu.VMEM((2, sz.tap_rows, LANES), F32)] * 2,
        compiler_params=PARAMS,
        cost_estimate=SHORT,
        name="notes",
    )(coverage, offsets, weight, scene, first, second, psf_rows, psf_cols)


def early_kernel(
    sz, offsets_ref, scene_ref, first_ref, second_ref, psf_cols_ref, rim_ref, three_ref,
    near_out, col_lines,
):
    place = lax.axis_index("epoch")
    load_taps(psf_cols_ref, col_lines, sz.epochs, sz.taps)
    (part,) = rim_parts_of(sz, (2,), place, offsets_ref, col_lines, rim_ref)
    top = widen_rows(sz, scene_ref, first_ref, second_ref, 0, RIM)
    bottom = widen_rows(sz, scene_ref, first_ref, second_ref, sz.rows - RIM, RIM)
    pack_rows(sz, near_out, sz.rows, jnp.where(place % 2 == 0, bottom, top))
    near_out[: sz.rows] = three_ref[...]
    complete(sz, near_out, part)


def early(sz, offsets, scene, first, second, psf_cols, rim, three):
    return pl.pallas_call(
        functools.partial(early_kernel, sz),
        out_shape=jax.ShapeDtypeStruct((sz.rows + RIM + HALO, sz.width), BF16),
        in_specs=[SMEM] + [VMEM] * 6,
        out_specs=VMEM,
        scratch_shapes=[pltpu.VMEM((2, sz.tap_rows, LANES), F32)],
        compiler_params=PARAMS,
        cost_estimate=SHORT,
        name="early",
    )(offsets, scene, first, second, psf_cols, rim, three)


def merge_kernel(sz, two_ref, near_ref, one_ref, part_ref, out_ref):
    place = lax.axis_index("epoch")
    outer = (place == 0) | (place == 3)

    @pl.when(outer)
    def _():
        out_ref[...] = two_ref[...]
        complete(sz, out_ref, part_ref[...].astype(F32))

    @pl.when(jnp.logical_not(outer))
    def _():
        total = near_ref[: sz.rows].astype(F32) + one_ref[...].astype(F32)
        out_ref[...] = total.astype(BF16)


def merge(sz, two, near, one, part):
    return pl.pallas_call(
        functools.partial(merge_kernel, sz),
        out_shape=jax.ShapeDtypeStruct((sz.rows, sz.width), BF16),
        in_specs=[VMEM] * 4,
        out_specs=VMEM,
        compiler_params=PARAMS,
        cost_estimate=SHORT,
        name="merge",
    )(two, near, one, part)


def finish_kernel(sz, offsets_ref, scene_ref, mask_ref, first_ref, second_ref, *more):
    if sz.blocks != 4:
        widen_kernel(sz, scene_ref, mask_ref, first_ref, second_ref, *more)
        return
    psf_cols_ref, rim_ref, own_ref, wide_ref, good_ref, back_out, own_out, col_lines, sem = more
    place = lax.axis_index("epoch")
    copy = pltpu.make_async_copy(own_ref, own_out, sem)
    copy.start()
    load_taps(psf_cols_ref, col_lines, sz.epochs, sz.taps)
    parts = rim_parts_of(sz, (0, 3), place, offsets_ref, col_lines, rim_ref)
    widen_kernel(sz, scene_ref, mask_ref, first_ref, second_ref, wide_ref, good_ref)
    top, bottom = wide_ref[:RIM], wide_ref[sz.rows - RIM :]
    pack_rows(sz, back_out, 0, jnp.where(place % 2 == 0, bottom, top))
    pack_part(sz, back_out, RIM + HALO, parts[0])
    copy.wait()
    complete(sz, own_out, parts[1])


def finish(sz, offsets, scene, mask, first, second, *more):
    full = jax.ShapeDtypeStruct((sz.rows, sz.width), BF16)
    shapes = [
        jax.ShapeDtypeStruct((sz.rows, sz.wide), BF16),
        jax.ShapeDtypeStruct((sz.mask_rows, sz.wide), F32),
    ]
    scratch = []
    if more:
        shapes += [jax.ShapeDtypeStruct((2 * RIM + HALO, sz.width), BF16), full]
        scratch = [pltpu.VMEM((2, sz.tap_rows, LANES), F32), pltpu.SemaphoreType.DMA]
    return pl.pallas_call(
        functools.partial(finish_kernel, sz),
        out_shape=tuple(shapes),
        in_specs=[SMEM] + [VMEM] * 4 + [VMEM, VMEM, HBM][: len(more)],
        out_specs=tuple([VMEM] * len(shapes)),
        scratch_shapes=scratch,
        compiler_params=PARAMS,
        cost_estimate=SHORT,
        name="finish",
    )(offsets, scene, mask, first, second, *more)


def image_kernel(sz, slots, rims, packs, images_ref, *more):
    count = 1 if slots is None else len(slots)
    small, ends, more = more[:6], more[6 : 6 + rims], more[6 + rims :]
    if packs:
        scene_ref, *more = more
    outs, more = more[:count], more[count:]
    if packs:
        first_out, second_out, edge, sides, edge_sem, side_sem, *more = more
    held, small_sem, more = more[:6], more[6], more[7:]
    coverage_ref, offsets_ref, weight_ref, mask_ref, psf_rows_ref, psf_cols_ref = held
    window, row_done, row_lines, col_lines, row_table, main_table, cross_table, rim_ref, sem = more
    place = lax.axis_index("epoch")
    first = place * sz.local
    column = lax.axis_index("sky") * sz.width
    if slots is None:
        targets = [pl.program_id(0)]
    else:
        targets = [destination(slot, place) for slot in slots]

    copies = []
    for i, target in enumerate(targets):
        start = target * sz.rows
        head = jnp.maximum(start - HALO, 0)
        foot = jnp.minimum(start + sz.rows, sz.height - HALO)
        for e in range(sz.local):
            for n, (source, at, length) in enumerate(
                ((start, HALO, sz.rows), (head, 0, HALO), (foot, HALO + sz.rows, HALO))
            ):
                copies.append(
                    pltpu.make_async_copy(
                        images_ref.at[e, pl.ds(pl.multiple_of(source, HALO), length), :],
                        window.at[i, e, pl.ds(at, length), :],
                        sem.at[i, e, n],
                    )
                )
    held_copies = [
        pltpu.make_async_copy(source, target, small_sem.at[n])
        for n, (source, target) in enumerate(zip(small, held))
    ]
    for copy in held_copies + copies:
        copy.start()
    if packs:
        edge_waits = edge_copies(sz, images_ref, scene_ref, edge, sides, edge_sem, side_sem)
    for copy in held_copies:
        copy.wait()
    load_taps(psf_rows_ref, row_lines, sz.epochs, sz.taps)
    load_taps(psf_cols_ref, col_lines, sz.epochs, sz.taps)
    for e in range(sz.local):
        epoch = first + e
        row_shift, col_shift = offsets_ref[0, epoch], offsets_ref[1, epoch]
        row_table[e] = toeplitz(row_of(row_lines[1], epoch), row_shift - 4, STEP, SPAN)
        line = row_of(col_lines[0], epoch)
        main = toeplitz(line, 12 - col_shift, SPAN, SPAN + LANES)[:, :SPAN]
        main_table[e] = main
        apart = (iota((SPAN, SPAN), 0) < LANES) != (iota((SPAN, SPAN), 1) < LANES)
        cross_table[e] = jnp.where(apart, main, jnp.zeros_like(main))
    rim_parts = []
    for e in range(sz.local if rims else 0):
        epoch = first + e
        rim_ref[e] = rim_rows(
            sz, epoch, e, coverage_ref, row_of(row_lines[1], epoch), offsets_ref[0, epoch],
            -2.0 * weight_ref[epoch], *ends,
        )
        table = rim_columns(row_of(col_lines[0], epoch), offsets_ref[1, epoch])
        for i, target in enumerate(targets):
            part = rim_part(sz, target * sz.rows, rim_ref.at[e], table)
            if e == 0:
                rim_parts.append(part)
            else:
                rim_parts[i] += part
    column_tile = column // TILE
    for i, target in enumerate(targets):
        wait = copies[3 * sz.local * i : 3 * sz.local * (i + 1)]
        if not packs:
            wait = copies if i == 0 else []
        for copy in wait:
            copy.wait()
        for copy in edge_waits[0] + edge_waits[1] if packs and i == 0 else ():
            copy.start()
        start = target * sz.rows
        zones = (
            (0, HALO, tile_of(start - HALO)),
            (HALO, HALO + sz.rows, tile_of(start)),
            (HALO + sz.rows, RIM + sz.rows, tile_of(start + sz.rows)),
        )
        for e in range(sz.local):
            epoch = first + e
            good = row_of(mask_ref[...].astype(F32), epoch)
            for begin, end, tile in zones:
                factor = good * cover_at(coverage_ref, epoch, tile, column_tile)
                window[i, e, begin:end] = window[i, e, begin:end] * factor.astype(BF16)
            twice = -2.0 * weight_ref[epoch]
            for s, n in spans(sz.rows):
                part = dot(row_table[e, :n, : n + RIM], window[i, e, s : s + n + RIM])
                row_done[i, e, s : s + n] = (part * twice).astype(BF16)
    for i in range(count):
        total = []
        for b in range(0, sz.width, SPAN):
            out = None
            for e in range(sz.local):
                part = dot(row_done[i, e, :, b : b + SPAN], main_table[e])
                out = part if out is None else out + part
            total += [out[:, :LANES], out[:, LANES:]]
        for b in range(LANES, sz.width - LANES, SPAN):
            out = None
            for e in range(sz.local):
                part = dot(row_done[i, e, :, b : b + SPAN], cross_table[e])
                out = part if out is None else out + part
            total[b // LANES] += out[:, :LANES]
            total[b // LANES + 1] += out[:, LANES:]
        if rims:
            total[0] += rim_parts[i][:, :LANES]
            total[-1] += rim_parts[i][:, LANES:]
        for k, piece in enumerate(total):
            outs[i][:, k * LANES : (k + 1) * LANES] = piece.astype(BF16)
    if packs:
        pack_edges(sz, mask_ref, edge, sides, *edge_waits, first_out, second_out)


def image_blocks(
    sz, slots, coverage, offsets, weight, images, mask, psf_rows, psf_cols, *ends, scene=None
):
    packs = scene is not None
    if slots is None:
        count = 1
        grid = dict(
            grid=(sz.blocks,),
            out_shape=jax.ShapeDtypeStruct((sz.blocks * sz.rows, sz.width), BF16),
            out_specs=pl.BlockSpec((sz.rows, sz.width), lambda i: (i, 0)),
        )
    else:
        count = len(slots)
        shapes = [jax.ShapeDtypeStruct((sz.rows, sz.width), BF16)] * count
        if packs:
            shapes += [jax.ShapeDtypeStruct((sz.buffer_rows, LANES), BF16)] * 2
        grid = dict(out_shape=tuple(shapes), out_specs=tuple([VMEM] * len(shapes)))
    pack_scratch = [
        pltpu.VMEM((2 * sz.local, sz.height, LANES), BF16),
        pltpu.VMEM((2, sz.rows, LANES), BF16),
        pltpu.SemaphoreType.DMA((2 * sz.local,)),
        pltpu.SemaphoreType.DMA((2,)),
    ]
    return pl.pallas_call(
        functools.partial(image_kernel, sz, slots, len(ends), packs),
        in_specs=[HBM] * 7 + [VMEM] * len(ends) + [HBM] * packs,
        scratch_shapes=pack_scratch * packs
        + [
            pltpu.SMEM(coverage.shape, jnp.int32),
            pltpu.SMEM(offsets.shape, jnp.int32),
            pltpu.SMEM(weight.shape, F32),
            pltpu.VMEM(mask.shape, jnp.int32),
            pltpu.VMEM(psf_rows.shape, BF16),
            pltpu.VMEM(psf_cols.shape, BF16),
            pltpu.SemaphoreType.DMA((6,)),
            pltpu.VMEM((count, sz.local, sz.rows + RIM, sz.width), BF16),
            pltpu.VMEM((count, sz.local, sz.rows, sz.width), BF16),
            pltpu.VMEM((2, sz.tap_rows, LANES), F32),
            pltpu.VMEM((2, sz.tap_rows, LANES), F32),
            pltpu.VMEM((sz.local, STEP, SPAN), BF16),
            pltpu.VMEM((sz.local, SPAN, SPAN), BF16),
            pltpu.VMEM((sz.local, SPAN, SPAN), BF16),
            pltpu.VMEM((sz.local, SPAN, 2 * LANES), BF16),
            pltpu.SemaphoreType.DMA((count, sz.local, 3)),
        ],
        compiler_params=WHOLE if slots is not None and 0 in slots else PARAMS,
        cost_estimate=SHORT,
        name="image_blocks",
        **grid,
    )(images, coverage, offsets, weight, mask, psf_rows, psf_cols, *ends, *([scene] * packs))


def column_tables(taps, start):
    pair = toeplitz(taps, start, LANES, SPAN)
    here, past = pair[:, :LANES], pair[:, LANES:]
    none = jnp.zeros_like(here)
    main = jnp.concatenate(
        [jnp.concatenate([here, none], axis=1), jnp.concatenate([past, here], axis=1)], axis=0
    )
    rest = jnp.concatenate(
        [jnp.concatenate([past, none], axis=1), jnp.concatenate([none, past], axis=1)], axis=0
    )
    return main, rest, here, past


def column_pass(sz, source, tables, tail):
    main, rest, here, past = tables
    tiles = []
    for b in range(0, sz.width, SPAN):
        out = dot(source[:, b : b + SPAN], main)
        tiles += [out[:, :LANES], out[:, LANES:]]
    ends = list(range(SPAN, sz.wide, SPAN))
    if len(ends) == 2:
        joined = jnp.concatenate([source[:, at : at + LANES] for at in ends], axis=1)
        out = dot(joined, rest)
        parts = [out[:, :LANES], out[:, LANES:]]
    else:
        parts = [dot(source[:, at : at + LANES], past) for at in ends]
    for at, part in zip(ends, parts):
        tiles[at // LANES - 1] += part
    if tail:
        tiles.append(dot(source[:, sz.width : sz.wide], here))
    return tiles


def model_kernel(
    sz, batch, coverage_ref, offsets_ref, weight_ref,
    wide_ref, good_ref, psf_rows_ref, psf_cols_ref, *more,
):
    *extra, out_ref, scene, lifted, residual, pulled, row_lines, col_lines = more
    step = pl.program_id(0)
    place = lax.axis_index("epoch")
    start = place * sz.rows
    column = lax.axis_index("sky") * sz.width

    @pl.when(step == 0)
    def _():
        load_taps(psf_rows_ref, row_lines, sz.epochs, sz.taps)
        load_taps(psf_cols_ref, col_lines, sz.epochs, sz.taps)
        scene[RIM : RIM + sz.rows] = wide_ref[...]
        if sz.blocks != 4:
            head_ref, foot_ref, base_ref = extra
            scene[0:RIM] = head_ref[...]
            scene[RIM + sz.rows :] = foot_ref[...]
            out_ref[...] = base_ref[...]
        else:
            own_ref, one_ref, two_ref, three_ref, back_ref, far_ref = extra
            outer = (place == 0) | (place == 3)
            near = jnp.where(
                outer, unpack_rim(sz, back_ref, 0), unpack_rim(sz, three_ref, sz.rows)
            )
            far = unpack_rim(sz, far_ref, 0)
            none = jnp.zeros_like(near)
            odd = place % 2 == 1
            scene[0:RIM] = jnp.where(odd, near, jnp.where(outer, none, far))
            scene[RIM + sz.rows :] = jnp.where(odd, jnp.where(outer, none, far), near)
            rows = slice(RIM + HALO, 2 * RIM + HALO)
            fix = unpack_part(sz, back_ref[rows], 0) + unpack_part(sz, far_ref[rows], 0)
            for b in range(0, sz.width, LANES):
                cols = slice(b, b + LANES)
                inner = two_ref[:, cols].astype(F32) + three_ref[: sz.rows, cols].astype(F32)
                base = jnp.where(outer, one_ref[:, cols].astype(F32), inner)
                base += own_ref[:, cols].astype(F32)
                for at, side in ((0, 0), (LANES, sz.width - LANES)):
                    if b == side:
                        base += fix[:, at : at + LANES]
                out_ref[:, cols] = base

    epochs = [step * batch + n for n in range(batch)]
    edge = sz.rows + HALO
    for n, epoch in enumerate(epochs):
        row_in = toeplitz(row_of(row_lines[0], epoch), -4 - offsets_ref[0, epoch], STEP, SPAN)
        for s, count in spans(sz.rows + RIM):
            lifted[n, s : s + count] = dot(
                row_in[:count, : count + RIM], scene[s : s + count + RIM]
            ).astype(BF16)
    for n, epoch in enumerate(epochs):
        good = row_of(good_ref[...], epoch) * (2.0 * weight_ref[epoch])
        lane = iota((1, sz.wide), 1)
        factors = []
        for row_tile in (tile_of(start - HALO), tile_of(start), tile_of(start + sz.rows)):
            left, here, right = (
                cover_at(coverage_ref, epoch, row_tile, tile_of(c))
                for c in (column - HALO, column, column + sz.width)
            )
            factors.append(
                good * jnp.where(lane < HALO, left, jnp.where(lane < HALO + sz.width, here, right))
            )
        tables = column_tables(row_of(col_lines[1], epoch), 28 + offsets_ref[1, epoch])
        for k, modeled in enumerate(column_pass(sz, lifted[n], tables, True)):
            b = k * LANES
            head, mid, foot = (f[:, b : b + LANES] for f in factors)
            residual[n, 0:HALO, b : b + LANES] = (modeled[0:HALO] * head).astype(BF16)
            residual[n, HALO:edge, b : b + LANES] = (modeled[HALO:edge] * mid).astype(BF16)
            residual[n, edge:, b : b + LANES] = (modeled[edge:] * foot).astype(BF16)
    for n, epoch in enumerate(epochs):
        tables = column_tables(row_of(col_lines[0], epoch), 28 - offsets_ref[1, epoch])
        for k, tile in enumerate(column_pass(sz, residual[n], tables, False)):
            pulled[n, :, k * LANES : (k + 1) * LANES] = tile.astype(BF16)
    row_outs = [
        toeplitz(row_of(row_lines[1], epoch), offsets_ref[0, epoch] - 4, STEP, SPAN)
        for epoch in epochs
    ]
    for s, count in spans(sz.rows):
        total = out_ref[s : s + count]
        for n in range(batch):
            total += dot(row_outs[n][:count, : count + RIM], pulled[n, s : s + count + RIM])
        out_ref[s : s + count] = total


def model_term(sz, coverage, offsets, weight, wide, good, psf_rows, psf_cols, *extra):
    high = sz.rows + RIM
    batch = 8 if sz.epochs % 8 == 0 else 1
    return pl.pallas_call(
        functools.partial(model_kernel, sz, batch),
        grid=(sz.epochs // batch,),
        out_shape=jax.ShapeDtypeStruct((sz.rows, sz.width), F32),
        in_specs=[SMEM] * 3 + [VMEM] * (4 + len(extra)),
        out_specs=VMEM,
        scratch_shapes=[
            pltpu.VMEM((sz.rows + 2 * RIM, sz.wide), BF16),
            pltpu.VMEM((batch, high, sz.wide), BF16),
            pltpu.VMEM((batch, high, sz.wide), BF16),
            pltpu.VMEM((batch, high, sz.width), BF16),
            pltpu.VMEM((2, sz.tap_rows, LANES), F32),
            pltpu.VMEM((2, sz.tap_rows, LANES), F32),
        ],
        compiler_params=PARAMS,
        cost_estimate=SHORT,
        name="model_term",
    )(coverage, offsets, weight, wide, good, psf_rows, psf_cols, *extra)


def on_device(sky_scene, images, psf_rows, psf_cols, offsets, epoch_weight, column_mask, coverage):
    sz = Sizes(images, sky_scene, psf_rows)
    peers = lax.axis_size("sky")
    depth = lax.axis_size("epoch")
    scalars = (jnp.transpose(coverage, (1, 2, 0)), offsets.T, epoch_weight)
    profiles = (psf_rows, psf_cols)

    def pairs(start, count):
        return [p for i in range(start, count - 1, 2) for p in ((i, i + 1), (i + 1, i))]

    def blocks(slots, shifts, *ends, scene=None):
        return image_blocks(
            sz, slots, scalars[0], shifts, epoch_weight, images, column_mask, *profiles, *ends,
            scene=scene,
        )

    if depth == 4:
        one, two, first, second = blocks((0, 1), scalars[1], scene=sky_scene)
        got_one = lax.ppermute(one, "epoch", pairs(0, depth))
        got_two = lax.ppermute(two, "epoch", pairs(1, depth))
        shifts, one = lax.optimization_barrier((scalars[1], one))
        three, own = blocks((2, 3), shifts)
        first = lax.ppermute(first, "sky", pairs(0, peers))
        second = lax.ppermute(second, "sky", pairs(1, peers))
        second, three = lax.optimization_barrier((second, three))
        far, rim, part = notes(sz, *scalars, sky_scene, first, second, *profiles)
        near = early(sz, scalars[1], sky_scene, first, second, psf_cols, rim, three)
        got_three = lax.ppermute(near, "epoch", [(0, 1), (3, 2)])
        got_far = lax.ppermute(far, "epoch", [(0, 3), (3, 0), (1, 2), (2, 1)])
        passed = merge(sz, two, near, got_one, part)
        passed, got_far, got_two, rim = lax.optimization_barrier((passed, got_far, got_two, rim))
        got_passed = lax.ppermute(passed, "epoch", [(0, 2), (3, 1), (1, 3), (2, 0)])
        wide, good, back, own = finish(
            sz, scalars[1], sky_scene, column_mask, first, second, psf_cols, rim, own
        )
        got_back = lax.ppermute(back, "epoch", [(1, 0), (2, 3)])
        model = model_term(
            sz, *scalars, wide, good, *profiles,
            own, got_one, got_two, got_three, got_back, got_far,
        )
        return model + got_passed.astype(F32)

    first, second = edges(sz, images, sky_scene, column_mask)
    first = lax.ppermute(first, "sky", pairs(0, peers))
    second = lax.ppermute(second, "sky", pairs(1, peers))
    downward = [(i, i + 1) for i in range(depth - 1)]
    upward = [(i + 1, i) for i in range(depth - 1)]
    wide, good = finish(sz, scalars[1], sky_scene, column_mask, first, second)
    head = lax.ppermute(wide[-RIM:], "epoch", downward)
    foot = lax.ppermute(wide[:RIM], "epoch", upward)
    terms = blocks(None, scalars[1], first, second).astype(F32)
    base = lax.psum_scatter(terms, "epoch", scatter_dimension=0, tiled=True)
    return model_term(sz, *scalars, wide, good, *profiles, head, foot, base)


def solution(mesh):
    return jax.shard_map(
        on_device,
        mesh=mesh,
        in_specs=(
            P(("field", "epoch"), "sky"),
            P(("field", "epoch"), None, "sky"),
            P("field", None),
            P("field", None),
            P("field", None),
            P("field"),
            P("field", "sky"),
            P("field", None, None),
        ),
        out_specs=P(("field", "epoch"), "sky"),
        check_vma=False,
    )
```
